32 devices in a mesh: dp: 2 (over x), row: 8 (over z, core), col: 2 (over y).
Axes of the slice: x: 2, y: 2, z: 4, core: 2. Of those that a mesh axis runs over, the one named last changes fastest.
Arguments:
- streams: float32 [2, 4, 3072, 2048], P(None, None, ('dp', 'row'), 'col'), may hold values from -6 to 6
- cotangent: float32 [2, 4, 3072, 2048], P(None, None, ('dp', 'row'), 'col'), may hold values from -6 to 6
- destination: int32 [2, 3072], P(None, ('dp', 'row')), may hold values from 0 to 3071, as said below
- segments: int32 [2, 2, 1536], P(None, 'dp'), may hold values from 0 to 3, never falling along the last dimension, each value on 1 to 1152 neighbouring positions
- attention_in: float32 [3, 2048, 2048], P(None, ('col', 'dp'), 'row'), may hold values from -0.125 to 0.125
- feedforward_in: float32 [2, 2048, 8192], P(None, ('col', 'dp'), 'row'), may hold values from -0.125 to 0.125
- attention_out: float32 [2048, 2048], P(('row', 'dp'), 'col'), may hold values from -1.5 to 1.5
- feedforward_out: float32 [8192, 2048], P(('row', 'dp'), 'col'), may hold values from -0.0625 to 0.0625
- attention_in_moment: float32 [3, 2048, 2048], P(None, ('col', 'dp'), 'row')
- feedforward_in_moment: float32 [2, 2048, 8192], P(None, ('col', 'dp'), 'row')
- attention_out_moment: float32 [2048, 2048], P(('row', 'dp'), 'col')
- feedforward_out_moment: float32 [8192, 2048], P(('row', 'dp'), 'col')
- attention_in_second: float32 [3, 2048, 2048], P(None, ('col', 'dp'), 'row'), as said below
- feedforward_in_second: float32 [2, 2048, 8192], P(None, ('col', 'dp'), 'row'), as said below
- attention_out_second: float32 [2048, 2048], P(('row', 'dp'), 'col'), as said below
- feedforward_out_second: float32 [8192, 2048], P(('row', 'dp'), 'col'), as said below
- hyper_weights: float32 [2, 4, 6], replicated, may hold values from 0.2 to 0.8
- hyper_moment: float32 [2, 4, 6], replicated, may hold values from -0.15625 to 0.15625
- hyper_second: float32 [2, 4, 6], replicated, may hold values from 6e-06 to 0.0001
- step_count: int32 [1], replicated, may hold values from 1 to 20
Outputs:
- streams_out: float32 [2, 4, 3072, 2048], P(None, None, ('dp', 'row'), 'col')
- stream_grad: float32 [2, 4, 3072, 2048], P(None, None, ('dp', 'row'), 'col')
- grad_norm: float32 [1], replicated
- attention_in_grad: float32 [3, 2048, 2048], P(None, ('col', 'dp'), 'row')
- feedforward_in_grad: float32 [2, 2048, 8192], P(None, ('col', 'dp'), 'row')
- attention_out_grad: float32 [2048, 2048], P(('row', 'dp'), 'col')
- feedforward_out_grad: float32 [8192, 2048], P(('row', 'dp'), 'col')
- hyper_grad: float32 [2, 4, 6], replicated
- attention_in_master: float32 [3, 2048, 2048], P(None, ('col', 'dp'), 'row')
- feedforward_in_master: float32 [2, 2048, 8192], P(None, ('col', 'dp'), 'row')
- attention_out_master: float32 [2048, 2048], P(('row', 'dp'), 'col')
- feedforward_out_master: float32 [8192, 2048], P(('row', 'dp'), 'col')
- hyper_master: float32 [2, 4, 6], replicated
- attention_in_moment_new: float32 [3, 2048, 2048], P(None, ('col', 'dp'), 'row')
- feedforward_in_moment_new: float32 [2, 2048, 8192], P(None, ('col', 'dp'), 'row')
- attention_out_moment_new: float32 [2048, 2048], P(('row', 'dp'), 'col')
- feedforward_out_moment_new: float32 [8192, 2048], P(('row', 'dp'), 'col')
- hyper_moment_new: float32 [2, 4, 6], replicated
- attention_in_second_new: float32 [3, 2048, 2048], P(None, ('col', 'dp'), 'row')
- feedforward_in_second_new: float32 [2, 2048, 8192], P(None, ('col', 'dp'), 'row')
- attention_out_second_new: float32 [2048, 2048], P(('row', 'dp'), 'col')
- feedforward_out_second_new: float32 [8192, 2048], P(('row', 'dp'), 'col')
- hyper_second_new: float32 [2, 4, 6], replicated
The draws below stay inside these ranges and needn't reach their ends.
Inputs may be any that keep to these rules, and one draw needn't show every extreme that they name: `destination`: each row is a permutation of 0 to 3071. The token at given position t = a * 1536 + r * 192 + i goes to a working position b * 1536 + r * 192 + a * 96 + j with j < 96; each (a, r) sends exactly 96 tokens to each b. `attention_in_second`: entries are positive. `feedforward_in_second`: entries are positive. `attention_out_second`: entries are positive. `feedforward_out_second`: entries are positive.
All inputs are finite; a program needn't handle non-finite values.
Results may differ from the reference program's by a relative error of at most 0.012.
The reference program's roundings to bfloat16 on the way count: a program that leaves them out, or rounds other values in their place, can miss the bound.
Values may be sent and summed in bfloat16 or wider, within the bound.
A program may use at most 320 MiB of HBM per device.

```python
import math
import jax
import jax.numpy as jnp
import numpy as np
from jax import lax

D = 2048
HEADS = 16
HEAD = 128
FF = 8192
STREAMS = 4
MICRO = 2
SEGS = 4
GROUP_TOK = 1536
ROWS = 192
GROUPS = 2
TOKENS = 3072
SEQ_MAX = 1152
N_DP = 2


def draw_destination(key, part):
    groups = TOKENS // GROUP_TOK
    grid_rows = GROUP_TOK // ROWS
    slot_count = ROWS // groups
    keys_all = jax.random.split(key, MICRO * groups * grid_rows)
    orders = jax.vmap(lambda single: jax.random.permutation(single, ROWS))(keys_all)
    orders = orders.reshape(MICRO, groups, grid_rows, ROWS).astype(jnp.int32)
    source = jnp.arange(groups, dtype=jnp.int32)[None, :, None, None]
    row_ids = jnp.arange(grid_rows, dtype=jnp.int32)[None, None, :, None]
    target_group = orders // slot_count
    target_slot = orders % slot_count
    placed = (target_group * grid_rows + row_ids) * ROWS + source * slot_count + target_slot
    return placed.reshape(MICRO, TOKENS).astype(jnp.int32)


def entry_share():
    return 1.0 / float(4 * D * D + 3 * D * FF)


def first_state(key, shape):
    base = jax.random.truncated_normal(key, -6.0, 6.0, shape, jnp.float32)
    return base * (entry_share() ** 0.5 / 9.0)


def second_state(key, shape, spread):
    level = jax.random.uniform(key, shape, jnp.float32)
    return entry_share() * spread / 19.0 * jnp.exp(jnp.log(0.25) + level * jnp.log(16.0))


def draw_attention_in_moment(key, part):
    return first_state(key, (3, D, D))


def draw_feedforward_in_moment(key, part):
    return first_state(key, (2, D, FF))


def draw_attention_out_moment(key, part):
    return first_state(key, (D, D))


def draw_feedforward_out_moment(key, part):
    return first_state(key, (FF, D))


def draw_attention_in_second(key, part):
    return second_state(key, (3, D, D), 1.0)


def draw_feedforward_in_second(key, part):
    return second_state(key, (2, D, FF), 0.05)


def draw_attention_out_second(key, part):
    return second_state(key, (D, D), 1.0)


def draw_feedforward_out_second(key, part):
    return second_state(key, (FF, D), 1.0)


def block_scale(rng, shape, cuts, low, largest):
    def one(axis_at, parts):
        draws = jax.random.uniform(jax.random.fold_in(jax.random.fold_in(rng, 6), axis_at), (parts,), jnp.float32, low / len(cuts), largest / len(cuts))
        return jnp.repeat(jnp.exp(draws), shape[axis_at] // parts).reshape((-1,) + (1,) * (len(shape) - axis_at - 1))

    factor_of = one(*cuts[0])
    for cut in cuts[1:]:
        factor_of = factor_of * one(*cut)
    return factor_of


def split_up(count, total, most, skew):
    loads = [(1 << 20) // math.isqrt(rank ** skew) + 1 for rank in range(2, count + 1)]
    surplus, holding = total - most - (count - 1), [1] * (count - 1)
    while surplus > 0:
        candidates = [i for i in range(count - 1) if holding[i] < most]
        mass, budget = sum([loads[i] for i in candidates]), surplus
        for i in candidates:
            addition = min(most - holding[i], max(1, budget * loads[i] // mass), surplus)
            holding[i] = holding[i] + addition
            surplus = surplus - addition
    return np.array([most] + holding)


def uneven(own_key, count, total, reach, slope):
    if count == 2:
        one = jax.random.randint(own_key, (), max(1, total - reach), min(reach, total - 1) + 1)
        return jnp.stack([one, total - one])
    tallies = jnp.asarray(split_up(count, total, reach, slope), jnp.int32)
    twos = (count - 1) // 2
    giver, taker = tallies[1:1 + 2 * twos:2], tallies[2:2 + 2 * twos:2]
    slack = jnp.minimum(giver - 1, reach - taker)
    shifted = jax.random.randint(jax.random.fold_in(own_key, 1), (twos,), 0, 1 << 20) % (slack + 1)
    tallies = tallies.at[1:1 + 2 * twos:2].set(giver - shifted).at[2:2 + 2 * twos:2].set(taker + shifted)
    return tallies[jax.random.permutation(jax.random.fold_in(own_key, 2), count)]


def normal_values(own_key, extent, width, most, cuts=(), held_as=jnp.bfloat16):
    result = jax.random.normal(own_key, extent, jnp.float32) * width
    if len(cuts) > 0:
        result = block_scale(own_key, extent, cuts, -0.22, 0.18) * result
    return jnp.clip(result, min=-most, max=most).astype(held_as)


def setup_inputs(seed: int = 0) -> dict:
    arg_keys = jax.random.split(jax.random.key(seed), 21)
    return {
        "streams": normal_values(arg_keys[0], (MICRO, STREAMS, TOKENS, D), 1.0, 6.0, ((2, 16), (3, 2)), jnp.float32),
        "cotangent": normal_values(arg_keys[1], (MICRO, STREAMS, TOKENS, D), 1.0, 6.0, ((2, 16), (3, 2)), jnp.float32),
        "destination": draw_destination(jax.random.fold_in(arg_keys[20], 71), 0),
        "segments": jax.vmap(lambda own: jnp.searchsorted(jnp.cumsum(uneven(own, SEGS, GROUP_TOK, SEQ_MAX, 2)), jnp.arange(GROUP_TOK), side="right"))(jax.random.split(arg_keys[3], MICRO * GROUPS)).reshape((MICRO, GROUPS, GROUP_TOK)).astype(jnp.int32),
        "attention_in": normal_values(arg_keys[4], (3, D, D), D ** -0.5, 0.125, ((1, 4), (2, 8)), jnp.float32),
        "feedforward_in": normal_values(arg_keys[5], (2, D, FF), D ** -0.5, 0.125, ((1, 4), (2, 8)), jnp.float32),
        "attention_out": normal_values(arg_keys[6], (D, D), (D // 128) ** -0.5, 1.5, ((0, 16), (1, 2)), jnp.float32),
        "feedforward_out": normal_values(arg_keys[7], (FF, D), FF ** -0.5, 0.0625, ((0, 16), (1, 2)), jnp.float32),
        "attention_in_moment": draw_attention_in_moment(jax.random.fold_in(arg_keys[20], 71), 0),
        "feedforward_in_moment": draw_feedforward_in_moment(jax.random.fold_in(arg_keys[20], 71), 0),
        "attention_out_moment": draw_attention_out_moment(jax.random.fold_in(arg_keys[20], 71), 0),
        "feedforward_out_moment": draw_feedforward_out_moment(jax.random.fold_in(arg_keys[20], 71), 0),
        "attention_in_second": draw_attention_in_second(jax.random.fold_in(arg_keys[20], 71), 0),
        "feedforward_in_second": draw_feedforward_in_second(jax.random.fold_in(arg_keys[20], 71), 0),
        "attention_out_second": draw_attention_out_second(jax.random.fold_in(arg_keys[20], 71), 0),
        "feedforward_out_second": draw_feedforward_out_second(jax.random.fold_in(arg_keys[20], 71), 0),
        "hyper_weights": jnp.clip(jax.random.uniform(arg_keys[16], (2, STREAMS, STREAMS + 2), jnp.float32, 0.2, 0.8), 0.2, 0.8),
        "hyper_moment": normal_values(arg_keys[17], (2, STREAMS, STREAMS + 2), 0.01, 0.15625, (), jnp.float32),
        "hyper_second": jnp.clip(jnp.exp(jax.random.uniform(arg_keys[18], (2, STREAMS, STREAMS + 2), jnp.float32, math.log(6.000000212225132e-06), math.log(0.0001))), 6.000000212225132e-06, 0.0001),
        "step_count": jax.random.randint(arg_keys[19], (1,), 1, 21).astype(jnp.int32),
    }


HIGHEST = lax.Precision.HIGHEST
norm_eps = 1e-05
beta_first = 0.9
beta_second = 0.95
adam_eps = 1e-08
learning_rate = 0.05
weight_decay = 0.1

@jax.custom_vjp
def low(v):
    return lax.optimization_barrier(v.astype(jnp.bfloat16)).astype(jnp.float32)

@jax.custom_vjp
def low_back(v):
    return v

def low_keep(v):
    return (low(v), None)

def low_pass(kept, grad):
    return (grad,)

def back_keep(v):
    return (v, None)

def back_low(kept, grad):
    return (low(grad),)
low.defvjp(low_keep, low_pass)
low_back.defvjp(back_keep, back_low)

def rotary_tables(segment):
    length = segment.shape[0]
    places = jnp.arange(length, dtype=jnp.int32)
    starts = jnp.searchsorted(segment, segment, side='left').astype(jnp.int32)
    offsets = (places - starts).astype(jnp.float32)
    halves = jnp.arange(HEAD // 2, dtype=jnp.float32)
    inverse = jnp.exp(halves * (-2.0 * math.log(10000.0) / HEAD))
    angles = offsets[:, None] * inverse[None, :]
    return (jnp.cos(angles), jnp.sin(angles))

def rotate(values_in, cosine, sine):
    half_width = values_in.shape[-1] // 2
    leading = values_in[..., :half_width]
    trailing = values_in[..., half_width:]
    return jnp.concatenate([leading * cosine - trailing * sine, leading * sine + trailing * cosine], axis=-1)

def attend(inputs):
    queries, keys_in, values_in, segment = inputs
    cosine, sine = rotary_tables(segment)
    query_low = low(rotate(queries, cosine[:, None, :], sine[:, None, :]))
    key_low = low(rotate(keys_in, cosine[:, None, :], sine[:, None, :]))
    value_low = low(values_in)
    raw_scores = low_back(jnp.einsum('qhe,khe->hqk', query_low, key_low, precision=HIGHEST))
    places = jnp.arange(segment.shape[0], dtype=jnp.int32)
    allowed = (segment[:, None] == segment[None, :]) & (places[None, :] <= places[:, None])
    scores = jnp.where(allowed[None], raw_scores * HEAD ** (-0.5), -1e+30)
    probs = low(jax.nn.softmax(scores, axis=-1))
    return jnp.einsum('hqk,khe->qhe', probs, value_low, precision=HIGHEST)

def layer_norm(hidden):
    means = lax.optimization_barrier(jnp.mean(hidden, axis=-1, keepdims=True))
    squares = lax.optimization_barrier(jnp.mean(hidden * hidden, axis=-1, keepdims=True))
    return (hidden - means) * lax.rsqrt(squares - means * means + norm_eps)

def mix_in(layer_weights, stream_set):
    return jnp.einsum('i,itd->td', layer_weights[:, 0], stream_set, precision=HIGHEST)

def mix_out(layer_weights, stream_set, branch):
    mixed = jnp.einsum('ij,itd->jtd', layer_weights[:, 1:STREAMS + 1], stream_set, precision=HIGHEST)
    return mixed + layer_weights[:, STREAMS + 1][:, None, None] * branch[None]

def forward(params, streams_in, segment_ids):
    attention_in, feedforward_in, attention_out, feedforward_out, hyper_weights = params
    token_count = streams_in.shape[1]
    normed_att = low(layer_norm(mix_in(hyper_weights[0], streams_in)))
    queries = low_back(jnp.dot(normed_att, attention_in[0], precision=HIGHEST))
    keys_in = low_back(jnp.dot(normed_att, attention_in[1], precision=HIGHEST))
    values_in = low_back(jnp.dot(normed_att, attention_in[2], precision=HIGHEST))
    grouped = (N_DP, GROUP_TOK, HEADS, HEAD)
    attended = lax.map(jax.checkpoint(attend), (queries.reshape(grouped), keys_in.reshape(grouped), values_in.reshape(grouped), segment_ids))
    heads_out = low(low_back(attended.reshape(token_count, D)))
    branch_att = low_back(jnp.dot(heads_out, attention_out, precision=HIGHEST))
    middle = mix_out(hyper_weights[0], streams_in, branch_att)
    normed_ffn = low(layer_norm(mix_in(hyper_weights[1], middle)))
    gate_pre = low_back(jnp.dot(normed_ffn, feedforward_in[0], precision=HIGHEST))
    up_pre = low_back(jnp.dot(normed_ffn, feedforward_in[1], precision=HIGHEST))
    hidden = low(jax.nn.silu(gate_pre) * up_pre)
    branch_ffn = low_back(jnp.dot(hidden, feedforward_out, precision=HIGHEST))
    return mix_out(hyper_weights[1], middle, branch_ffn)

def adam_update(weight, grad_sum, moment_one, moment_two, clip_factor, step_value):
    clipped = grad_sum * clip_factor
    new_one = beta_first * moment_one + (1.0 - beta_first) * clipped
    new_two = beta_second * moment_two + (1.0 - beta_second) * clipped * clipped
    fix_one = 1.0 - jnp.power(beta_first, step_value)
    fix_two = 1.0 - jnp.power(beta_second, step_value)
    new_weight = weight - learning_rate * (new_one / fix_one / (jnp.sqrt(new_two / fix_two) + adam_eps) + weight_decay * weight)
    return (new_weight, new_one, new_two)

def reference(streams, cotangent, destination, segments, attention_in, feedforward_in, attention_out, feedforward_out, attention_in_moment, feedforward_in_moment, attention_out_moment, feedforward_out_moment, attention_in_second, feedforward_in_second, attention_out_second, feedforward_out_second, hyper_weights, hyper_moment, hyper_second, step_count):
    params = (attention_in.astype(jnp.bfloat16).astype(jnp.float32), feedforward_in.astype(jnp.bfloat16).astype(jnp.float32), attention_out.astype(jnp.bfloat16).astype(jnp.float32), feedforward_out.astype(jnp.bfloat16).astype(jnp.float32), hyper_weights)
    totals = tuple((jnp.zeros_like(param) for param in params))
    results = []
    backs = []
    for micro_index in range(MICRO):
        placement = destination[micro_index]
        work_streams = jnp.zeros_like(streams[micro_index]).at[:, placement].set(streams[micro_index])
        work_cot = jnp.zeros_like(cotangent[micro_index]).at[:, placement].set(cotangent[micro_index])
        segment_ids = segments[micro_index]
        output, pullback = jax.vjp(lambda param_set, stream_set: forward(param_set, stream_set, segment_ids), params, work_streams)
        grads, grad_streams = pullback(work_cot)
        totals = tuple((running + grad_part for running, grad_part in zip(totals, grads)))
        results.append(output[:, placement])
        backs.append(grad_streams[:, placement])
    square = jnp.sum(totals[0] * totals[0]) + jnp.sum(totals[1] * totals[1]) + jnp.sum(totals[2] * totals[2]) + jnp.sum(totals[3] * totals[3]) + jnp.sum(totals[4] * totals[4])
    grad_norm = jnp.sqrt(square)
    clip_factor = 1.0 / jnp.maximum(grad_norm, 1.0)
    step_value = step_count[0].astype(jnp.float32)
    attention_in_new = adam_update(attention_in, totals[0], attention_in_moment, attention_in_second, clip_factor, step_value)
    feedforward_in_new = adam_update(feedforward_in, totals[1], feedforward_in_moment, feedforward_in_second, clip_factor, step_value)
    attention_out_new = adam_update(attention_out, totals[2], attention_out_moment, attention_out_second, clip_factor, step_value)
    feedforward_out_new = adam_update(feedforward_out, totals[3], feedforward_out_moment, feedforward_out_second, clip_factor, step_value)
    hyper_new = adam_update(hyper_weights, totals[4], hyper_moment, hyper_second, clip_factor, step_value)
    return (jnp.stack(results), jnp.stack(backs), grad_norm.reshape(1), totals[0], totals[1], totals[2], totals[3], totals[4], attention_in_new[0], feedforward_in_new[0], attention_out_new[0], feedforward_out_new[0], hyper_new[0], attention_in_new[1], feedforward_in_new[1], attention_out_new[1], feedforward_out_new[1], hyper_new[1], attention_in_new[2], feedforward_in_new[2], attention_out_new[2], feedforward_out_new[2], hyper_new[2])
```

```python
import math

import jax
import jax.numpy as jnp
from jax import lax
from jax.sharding import PartitionSpec as P

D = 2048
HEAD = 128
STREAMS = 4
MICRO = 2


HIGHEST = lax.Precision.HIGHEST
norm_eps = 1e-05
beta_first = 0.9
beta_second = 0.95
adam_eps = 1e-08
learning_rate = 0.05
weight_decay = 0.1


def rotary_tables(segment):
    length = segment.shape[0]
    places = jnp.arange(length, dtype=jnp.int32)
    starts = jnp.sum((segment[None, :] < segment[:, None]).astype(jnp.int32), axis=1)
    offsets = (places - starts).astype(jnp.float32)
    halves = jnp.arange(HEAD // 2, dtype=jnp.float32)
    inverse = jnp.exp(halves * (-2.0 * math.log(10000.0) / HEAD))
    angles = offsets[:, None] * inverse[None, :]
    return (jnp.cos(angles), jnp.sin(angles))


def rotate(values_in, cosine, sine):
    half_width = values_in.shape[-1] // 2
    leading = values_in[..., :half_width]
    trailing = values_in[..., half_width:]
    return jnp.concatenate(
        [leading * cosine - trailing * sine, leading * sine + trailing * cosine], axis=-1
    )


def norm_forward(hidden):
    means = jnp.sum(hidden, axis=-1, keepdims=True) / D
    squares = jnp.sum(hidden * hidden, axis=-1, keepdims=True) / D
    inverse = lax.rsqrt(squares - means * means + norm_eps)
    return ((hidden - means) * inverse, inverse)


def norm_backward(upstream, normed, inverse):
    mean_one = jnp.sum(upstream, axis=-1, keepdims=True) / D
    mean_two = jnp.sum(upstream * normed, axis=-1, keepdims=True) / D
    return inverse * (upstream - mean_one - normed * mean_two)


def gather_tokens(rows_low):
    return lax.all_gather(rows_low, "row", axis=0, tiled=True)


def sum_tokens(partial_sums):
    return lax.psum_scatter(
        partial_sums.astype(jnp.bfloat16), "row", scatter_dimension=0, tiled=True
    ).astype(jnp.float32)


def to_work(home_rows):
    n_dp, n_col = lax.axis_size("dp"), lax.axis_size("col")
    rows, width = home_rows.shape[1:]
    slot = rows // n_dp
    parts = home_rows.reshape(n_col, n_dp, slot, width).transpose(1, 0, 2, 3)
    parts = lax.all_to_all(
        parts.reshape(n_dp * n_col, slot, width),
        ("dp", "col"),
        split_axis=0,
        concat_axis=0,
        tiled=True,
    )
    parts = parts.reshape(n_dp, n_col, slot, width).transpose(0, 2, 1, 3)
    return parts.reshape(rows, n_col * width)


def to_home(work_rows):
    n_dp, n_col = lax.axis_size("dp"), lax.axis_size("col")
    rows, width = work_rows.shape[0], work_rows.shape[1] // n_col
    slot = rows // n_dp
    parts = work_rows.reshape(n_dp, slot, n_col, width).transpose(0, 2, 1, 3)
    parts = lax.all_to_all(
        parts.reshape(n_dp * n_col, slot, width),
        ("dp", "col"),
        split_axis=0,
        concat_axis=0,
        tiled=True,
    )
    parts = parts.reshape(n_dp, n_col, slot, width).transpose(1, 0, 2, 3)
    return parts.reshape(n_col, rows, width)


def gather_in(weight_low):
    return lax.all_gather(weight_low, ("col", "dp"), axis=1, tiled=True)


def gather_out(weight_low):
    return lax.all_gather(
        lax.all_gather(weight_low, "dp", axis=0, tiled=True), "col", axis=1, tiled=True
    )


def scatter_in(grad):
    return lax.psum_scatter(
        grad.astype(jnp.bfloat16), ("col", "dp"), scatter_dimension=1, tiled=True
    ).astype(jnp.float32)


def scatter_out(grad):
    half = lax.psum_scatter(grad.astype(jnp.bfloat16), "col", scatter_dimension=1, tiled=True)
    return lax.psum_scatter(half, "dp", scatter_dimension=0, tiled=True).astype(jnp.float32)


def combine(weights, stream_set):
    total = weights[0] * stream_set[:, 0]
    for index in range(1, STREAMS):
        total = total + weights[index] * stream_set[:, index]
    return total


def mat(left, right):
    return jnp.sum(left[:, :, None] * right[None, :, :], axis=1)


def block_masks(segment):
    length = segment.shape[0]
    block_rows = min(512, length)
    blocks = length // block_rows
    places = jnp.arange(length, dtype=jnp.int32)
    return (length, block_rows, blocks, places)


def masked_scores(query_part, key_low, segment_part, place_part, segment, places):
    scores = jnp.einsum(
        "qe,ke->qk", query_part, key_low, preferred_element_type=jnp.float32
    ) * HEAD ** (-0.5)
    allowed = (segment_part[:, None] == segment[None, :]) & (places[None, :] <= place_part[:, None])
    return jnp.where(allowed, scores, -1e30)


def attend_forward(query_low, key_low, value_low, segment):
    length, block_rows, blocks, places = block_masks(segment)

    def one_block(inputs):
        query_part, segment_part, place_part = inputs
        scores = masked_scores(query_part, key_low, segment_part, place_part, segment, places)
        largest = jnp.max(scores, axis=-1, keepdims=True)
        weights = jnp.exp(scores - largest)
        totals = jnp.sum(weights, axis=-1, keepdims=True)
        probs = (weights / totals).astype(jnp.bfloat16)
        outputs = jnp.dot(probs, value_low, preferred_element_type=jnp.float32)
        return (outputs, (largest + jnp.log(totals))[:, 0])

    outputs, log_totals = lax.map(
        one_block,
        (
            query_low.reshape(blocks, block_rows, HEAD),
            segment.reshape(blocks, block_rows),
            places.reshape(blocks, block_rows),
        ),
    )
    return (outputs.reshape(length, HEAD), log_totals.reshape(length))


def attend_backward(grad_low, query_low, key_low, value_low, log_totals, segment):
    length, block_rows, blocks, places = block_masks(segment)

    def one_block(carry, inputs):
        grad_keys, grad_values = carry
        query_part, grad_part, log_part, segment_part, place_part = inputs
        scores = masked_scores(query_part, key_low, segment_part, place_part, segment, places)
        probs = jnp.exp(scores - log_part[:, None])
        grad_probs = jnp.einsum(
            "qe,ke->qk", grad_part, value_low, preferred_element_type=jnp.float32
        )
        inner = jnp.sum(probs * grad_probs, axis=-1, keepdims=True)
        grad_scores = (probs * (grad_probs - inner) * HEAD ** (-0.5)).astype(jnp.bfloat16)
        grad_queries = jnp.dot(grad_scores, key_low, preferred_element_type=jnp.float32)
        grad_keys = grad_keys + jnp.einsum(
            "qk,qe->ke", grad_scores, query_part, preferred_element_type=jnp.float32
        )
        grad_values = grad_values + jnp.einsum(
            "qk,qe->ke", probs.astype(jnp.bfloat16), grad_part, preferred_element_type=jnp.float32
        )
        return ((grad_keys, grad_values), grad_queries)

    zeros_rows = jnp.zeros((length, HEAD), jnp.float32)
    carried, grad_queries = lax.scan(
        one_block,
        (zeros_rows, zeros_rows),
        (
            query_low.reshape(blocks, block_rows, HEAD),
            grad_low.reshape(blocks, block_rows, HEAD),
            log_totals.reshape(blocks, block_rows),
            segment.reshape(blocks, block_rows),
            places.reshape(blocks, block_rows),
        ),
    )
    return (grad_queries.reshape(length, HEAD), carried[0], carried[1])


def adam_update(weight, grad_sum, moment_one, moment_two, clip_factor, step_value):
    clipped = grad_sum * clip_factor
    new_one = beta_first * moment_one + (1.0 - beta_first) * clipped
    new_two = beta_second * moment_two + (1.0 - beta_second) * clipped * clipped
    fix_one = 1.0 - jnp.power(beta_first, step_value)
    fix_two = 1.0 - jnp.power(beta_second, step_value)
    new_weight = weight - learning_rate * (
        new_one / fix_one / (jnp.sqrt(new_two / fix_two) + adam_eps) + weight_decay * weight
    )
    return (new_weight, new_one, new_two)


def body(
    streams,
    cotangent,
    destination,
    segments,
    attention_in,
    feedforward_in,
    attention_out,
    feedforward_out,
    attention_in_moment,
    feedforward_in_moment,
    attention_out_moment,
    feedforward_out_moment,
    attention_in_second,
    feedforward_in_second,
    attention_out_second,
    feedforward_out_second,
    hyper_weights,
    hyper_moment,
    hyper_second,
    step_count,
):
    low = jnp.bfloat16
    n_dp = lax.axis_size("dp")
    rows = destination.shape[1]
    group_tokens = segments.shape[2]
    slot = rows // n_dp
    home_dp, home_row, col_index = (
        lax.axis_index("dp"),
        lax.axis_index("row"),
        lax.axis_index("col"),
    )
    attention_in_low = gather_in(attention_in.astype(low))
    attention_out_low = gather_out(attention_out.astype(low))
    feedforward_in_low = gather_in(feedforward_in.astype(low))
    feedforward_out_low = gather_out(feedforward_out.astype(low))

    a0, m0, c0 = hyper_weights[0, :, 0], hyper_weights[0, :, 1:5], hyper_weights[0, :, 5]
    a1, m1, c1 = hyper_weights[1, :, 0], hyper_weights[1, :, 1:5], hyper_weights[1, :, 5]
    m01 = mat(m0, m1)
    forward_mix = jnp.sum(m0 * a1[None, :], axis=1)
    forward_branch = jnp.sum(a1 * c0)
    backward_mix = jnp.sum(m1 * c0[:, None], axis=0)
    backward_branch = jnp.sum(c0 * a1)

    group = destination // group_tokens
    sent = (
        group * slot + destination - group * group_tokens - home_row * rows - home_dp * slot
    )
    orders = jnp.argsort(sent, axis=1)

    def sort_rows(values_in):
        return jnp.stack([values_in[index][orders[index]] for index in range(MICRO)])

    def unsort_rows(values_in):
        return jnp.stack([values_in[index][sent[index]] for index in range(MICRO)])

    hidden_att = to_work(sort_rows(combine(a0, streams)))
    hidden_mix = to_work(sort_rows(combine(forward_mix, streams)))
    branch_rows_ffn = to_work(sort_rows(combine(c1, cotangent)).astype(low))
    grad_mix_rows = to_work(sort_rows(combine(backward_mix, cotangent)))
    gram = jnp.stack(
        [
            jnp.stack([jnp.sum(streams[:, i] * cotangent[:, j]) for j in range(STREAMS)])
            for i in range(STREAMS)
        ]
    )

    segment = lax.dynamic_index_in_dim(segments[:, 0], col_index, 0, keepdims=False)
    cosine, sine = rotary_tables(segment)

    normed_att, inverse_att = norm_forward(hidden_att)
    rows_att = gather_tokens(normed_att.astype(low))
    qkv = jnp.einsum("td,kdu->ktu", rows_att, attention_in_low, preferred_element_type=jnp.float32)
    heads = qkv.shape[2] // HEAD
    qkv = qkv.reshape(3, group_tokens, heads, HEAD).transpose(0, 2, 1, 3)
    query_low = rotate(qkv[0], cosine, sine).astype(low)
    key_low = rotate(qkv[1], cosine, sine).astype(low)
    value_low = qkv[2].astype(low)
    heads_out, log_totals = jax.vmap(attend_forward, in_axes=(0, 0, 0, None))(
        query_low, key_low, value_low, segment
    )
    heads_low = heads_out.astype(low).transpose(1, 0, 2).reshape(group_tokens, heads * HEAD)
    branch_att = sum_tokens(
        jnp.dot(heads_low, attention_out_low, preferred_element_type=jnp.float32)
    )

    hidden_ffn = hidden_mix + forward_branch * branch_att
    normed_ffn, inverse_ffn = norm_forward(hidden_ffn)
    rows_ffn = gather_tokens(normed_ffn.astype(low))
    grad_rows_ffn = gather_tokens(branch_rows_ffn)
    gate_pre = jnp.dot(rows_ffn, feedforward_in_low[0], preferred_element_type=jnp.float32)
    up_pre = jnp.dot(rows_ffn, feedforward_in_low[1], preferred_element_type=jnp.float32)
    sigma = jax.nn.sigmoid(gate_pre)
    silu = gate_pre * sigma
    hidden_low = (silu * up_pre).astype(low)
    branch_ffn = sum_tokens(
        jnp.dot(hidden_low, feedforward_out_low, preferred_element_type=jnp.float32)
    )
    grad_hidden = jnp.einsum(
        "td,ud->tu", grad_rows_ffn, feedforward_out_low, preferred_element_type=jnp.float32
    )
    grad_gate = (grad_hidden * up_pre * sigma * (1.0 + gate_pre * (1.0 - sigma))).astype(low)
    grad_up = (grad_hidden * silu).astype(low)
    grad_normed = sum_tokens(
        jnp.einsum(
            "tu,du->td", grad_gate, feedforward_in_low[0], preferred_element_type=jnp.float32
        )
        + jnp.einsum(
            "tu,du->td", grad_up, feedforward_in_low[1], preferred_element_type=jnp.float32
        )
    )
    shard_feedforward_out = scatter_out(
        jnp.einsum("tu,td->ud", hidden_low, grad_rows_ffn, preferred_element_type=jnp.float32)
    )
    shard_feedforward_in = scatter_in(
        jnp.stack(
            [
                jnp.einsum("td,tu->du", rows_ffn, grad, preferred_element_type=jnp.float32)
                for grad in (grad_gate, grad_up)
            ]
        )
    )
    grad_hidden_ffn = norm_backward(grad_normed, normed_ffn, inverse_ffn)
    grad_rows_att = gather_tokens(
        (grad_mix_rows + backward_branch * grad_hidden_ffn).astype(low)
    )
    shard_attention_out = scatter_out(
        jnp.einsum("tu,td->ud", heads_low, grad_rows_att, preferred_element_type=jnp.float32)
    )
    grad_heads = jnp.einsum(
        "td,ud->tu", grad_rows_att, attention_out_low, preferred_element_type=jnp.float32
    ).astype(low)
    grad_heads = grad_heads.reshape(group_tokens, heads, HEAD).transpose(1, 0, 2)
    grad_q, grad_k, grad_v = jax.vmap(attend_backward, in_axes=(0, 0, 0, 0, 0, None))(
        grad_heads, query_low, key_low, value_low, log_totals, segment
    )
    grad_units = (
        jnp.stack([rotate(grad_q, cosine, -sine), rotate(grad_k, cosine, -sine), grad_v])
        .astype(low)
        .transpose(0, 2, 1, 3)
        .reshape(3, group_tokens, heads * HEAD)
    )
    shard_attention_in = scatter_in(
        jnp.einsum("td,ktu->kdu", rows_att, grad_units, preferred_element_type=jnp.float32)
    )
    grad_normed = sum_tokens(
        jnp.einsum("ktu,kdu->td", grad_units, attention_in_low, preferred_element_type=jnp.float32)
    )
    grad_hidden_att = norm_backward(grad_normed, normed_att, inverse_att)

    home_att = unsort_rows(to_home(branch_att.astype(low)))
    home_ffn = unsort_rows(to_home(branch_ffn.astype(low)))
    home_grad_ffn = unsort_rows(to_home(grad_hidden_ffn.astype(low)))
    home_grad_att = unsort_rows(to_home(grad_hidden_att.astype(low)))
    home_att, home_ffn, home_grad_ffn, home_grad_att = (
        value.astype(jnp.float32) for value in (home_att, home_ffn, home_grad_ffn, home_grad_att)
    )
    mix_branch = jnp.sum(m1 * c0[:, None], axis=0)
    streams_out = jnp.stack(
        [
            combine(m01[:, j], streams) + mix_branch[j] * home_att + c1[j] * home_ffn
            for j in range(STREAMS)
        ],
        axis=1,
    )
    mix_grad = jnp.sum(m0 * a1[None, :], axis=1)
    stream_grad = jnp.stack(
        [
            combine(m01[i], cotangent) + mix_grad[i] * home_grad_ffn + a0[i] * home_grad_att
            for i in range(STREAMS)
        ],
        axis=1,
    )
    dots = jnp.concatenate(
        [
            gram.reshape(-1),
            jnp.stack([jnp.sum(cotangent[:, j] * home_att) for j in range(STREAMS)]),
            jnp.stack([jnp.sum(cotangent[:, j] * home_ffn) for j in range(STREAMS)]),
            jnp.stack([jnp.sum(streams[:, i] * home_grad_ffn) for i in range(STREAMS)]),
            jnp.stack([jnp.sum(streams[:, i] * home_grad_att) for i in range(STREAMS)]),
            jnp.sum(home_att * home_grad_ffn)[None],
        ]
    )
    square = (
        jnp.sum(shard_attention_in * shard_attention_in)
        + jnp.sum(shard_feedforward_in * shard_feedforward_in)
        + jnp.sum(shard_attention_out * shard_attention_out)
        + jnp.sum(shard_feedforward_out * shard_feedforward_out)
    )
    totals = lax.psum(jnp.concatenate([dots, square[None]]), ("dp", "row", "col"))
    gram = totals[:16].reshape(STREAMS, STREAMS)
    att_cot, ffn_cot = totals[16:20], totals[20:24]
    streams_ffn, streams_att = totals[24:28], totals[28:32]
    att_ffn, square_total = totals[32], totals[33]
    grad_m1 = mat(m0.T, gram) + c0[:, None] * att_cot[None, :]
    grad_a1 = jnp.sum(m0 * streams_ffn[:, None], axis=0) + c0 * att_ffn
    grad_m0 = mat(gram, m1.T) + streams_ffn[:, None] * a1[None, :]
    grad_c0 = jnp.sum(m1 * att_cot[None, :], axis=1) + a1 * att_ffn
    hyper_grad = jnp.stack(
        [
            jnp.concatenate([streams_att[:, None], grad_m0, grad_c0[:, None]], axis=1),
            jnp.concatenate([grad_a1[:, None], grad_m1, ffn_cot[:, None]], axis=1),
        ]
    )
    grad_norm = jnp.sqrt(square_total + jnp.sum(hyper_grad * hyper_grad))
    clip_factor = 1.0 / jnp.maximum(grad_norm, 1.0)
    step_value = step_count[0].astype(jnp.float32)
    attention_in_new = adam_update(
        attention_in,
        shard_attention_in,
        attention_in_moment,
        attention_in_second,
        clip_factor,
        step_value,
    )
    feedforward_in_new = adam_update(
        feedforward_in,
        shard_feedforward_in,
        feedforward_in_moment,
        feedforward_in_second,
        clip_factor,
        step_value,
    )
    attention_out_new = adam_update(
        attention_out,
        shard_attention_out,
        attention_out_moment,
        attention_out_second,
        clip_factor,
        step_value,
    )
    feedforward_out_new = adam_update(
        feedforward_out,
        shard_feedforward_out,
        feedforward_out_moment,
        feedforward_out_second,
        clip_factor,
        step_value,
    )
    hyper_new = adam_update(
        hyper_weights, hyper_grad, hyper_moment, hyper_second, clip_factor, step_value
    )
    return (
        streams_out,
        stream_grad,
        grad_norm.reshape(1),
        shard_attention_in,
        shard_feedforward_in,
        shard_attention_out,
        shard_feedforward_out,
        hyper_grad,
        attention_in_new[0],
        feedforward_in_new[0],
        attention_out_new[0],
        feedforward_out_new[0],
        hyper_new[0],
        attention_in_new[1],
        feedforward_in_new[1],
        attention_out_new[1],
        feedforward_out_new[1],
        hyper_new[1],
        attention_in_new[2],
        feedforward_in_new[2],
        attention_out_new[2],
        feedforward_out_new[2],
        hyper_new[2],
    )


def solution(mesh):
    placed = (
        P(None, None, ("dp", "row"), "col"),
        P(None, None, ("dp", "row"), "col"),
        P(None, ("dp", "row")),
        P(None, "dp", None),
        P(None, ("col", "dp"), "row"),
        P(None, ("col", "dp"), "row"),
        P(("row", "dp"), "col"),
        P(("row", "dp"), "col"),
        P(None, ("col", "dp"), "row"),
        P(None, ("col", "dp"), "row"),
        P(("row", "dp"), "col"),
        P(("row", "dp"), "col"),
        P(None, ("col", "dp"), "row"),
        P(None, ("col", "dp"), "row"),
        P(("row", "dp"), "col"),
        P(("row", "dp"), "col"),
        P(),
        P(),
        P(),
        P(),
    )
    return jax.shard_map(
        body,
        mesh=mesh,
        in_specs=placed,
        out_specs=(
            P(None, None, ("dp", "row"), "col"),
            P(None, None, ("dp", "row"), "col"),
            P(),
            P(None, ("col", "dp"), "row"),
            P(None, ("col", "dp"), "row"),
            P(("row", "dp"), "col"),
            P(("row", "dp"), "col"),
            P(),
            P(None, ("col", "dp"), "row"),
            P(None, ("col", "dp"), "row"),
            P(("row", "dp"), "col"),
            P(("row", "dp"), "col"),
            P(),
            P(None, ("col", "dp"), "row"),
            P(None, ("col", "dp"), "row"),
            P(("row", "dp"), "col"),
            P(("row", "dp"), "col"),
            P(),
            P(None, ("col", "dp"), "row"),
            P(None, ("col", "dp"), "row"),
            P(("row", "dp"), "col"),
            P(("row", "dp"), "col"),
            P(),
        ),
        check_vma=False,
    )
```

```python
import functools
import math

import jax
import jax.numpy as jnp
from jax import lax
from jax.experimental import pallas as pl
from jax.experimental.pallas import tpu as pltpu
from jax.sharding import PartitionSpec as P

D = 2048
HEAD = 128
STREAMS = 4
MICRO = 2


norm_eps = 1e-05
beta_first = 0.9
beta_second = 0.95
adam_eps = 1e-08
learning_rate = 0.05
weight_decay = 0.1

LOW = jnp.bfloat16
FULL = jnp.float32
DMA = pltpu.SemaphoreType.DMA
ANY = pl.BlockSpec(memory_space=pl.ANY)
VMEM = pl.BlockSpec(memory_space=pltpu.VMEM)
SMEM = pl.BlockSpec(memory_space=pltpu.SMEM)
ROOM = 48 * 2**20


def rotary_tables(segment):
    length = segment.shape[0]
    places = jnp.arange(length, dtype=jnp.int32)
    starts = jnp.sum((segment[None, :] < segment[:, None]).astype(jnp.int32), axis=1)
    offsets = (places - starts).astype(jnp.float32)
    halves = jnp.arange(HEAD // 2, dtype=jnp.float32)
    inverse = jnp.exp(halves * (-2.0 * math.log(10000.0) / HEAD))
    angles = offsets[:, None] * inverse[None, :]
    cosine, sine = jnp.cos(angles), jnp.sin(angles)
    return (
        jnp.concatenate([cosine, cosine], axis=1),
        jnp.concatenate([-sine, sine], axis=1),
        starts[:, None],
    )


def norm_forward(hidden):
    means = jnp.sum(hidden, axis=-1, keepdims=True) / D
    squares = jnp.sum(hidden * hidden, axis=-1, keepdims=True) / D
    inverse = lax.rsqrt(squares - means * means + norm_eps)
    return ((hidden - means) * inverse, inverse)


def norm_backward(upstream, hidden):
    normed, inverse = norm_forward(hidden)
    mean_one = jnp.sum(upstream, axis=-1, keepdims=True) / D
    mean_two = jnp.sum(upstream * normed, axis=-1, keepdims=True) / D
    return inverse * (upstream - mean_one - normed * mean_two)


def hyper_parts(hyper):
    width = STREAMS + 2
    parts = []
    for layer in range(2):
        at = [[hyper[(layer * STREAMS + i) * width + k] for k in range(width)] for i in range(STREAMS)]
        parts.append(
            ([row[0] for row in at], [row[1 : STREAMS + 1] for row in at], [row[-1] for row in at])
        )
    return parts


def dot_of(left, right):
    total = left[0] * right[0]
    for a, b in zip(left[1:], right[1:]):
        total = total + a * b
    return total


def column(matrix, index):
    return [row[index] for row in matrix]


def branch_weight(hyper):
    (_, _, c0), (a1, _, _) = hyper_parts(hyper)
    return dot_of(a1, c0)


def combine(weights, stream_set):
    return dot_of(weights, stream_set)


def fold(product):
    rows, width = product.shape
    return jnp.sum(product.reshape(rows // 8, 8, width), axis=0)


def place_rows(match, values_in):
    if values_in.dtype == LOW:
        return jnp.dot(match.astype(LOW), values_in, preferred_element_type=FULL)
    return jnp.dot(
        match.astype(FULL), values_in, precision=lax.Precision.HIGHEST, preferred_element_type=FULL
    )


def prepare_kernel(hyper, streams, cotangent, sent, h_out, mix_out, back_out, gy_out, gram_out):
    rows, width = streams.shape[2:]
    parts, slot = h_out.shape[0], h_out.shape[2]
    (a0, m0, c0), (a1, m1, c1) = hyper_parts(hyper)
    first = [streams[0, i] for i in range(STREAMS)]
    second = [cotangent[0, j] for j in range(STREAMS)]
    match = lax.broadcasted_iota(jnp.int32, (rows, rows), 0) == sent[0]

    def put(out, values_in):
        moved = place_rows(match, values_in)
        for part in range(parts):
            out[part, 0] = moved[part * slot : (part + 1) * slot].astype(out.dtype)

    put(h_out, combine(a0, first))
    put(mix_out, combine([dot_of(row, a1) for row in m0], first))
    put(gy_out, combine(c1, second).astype(LOW))
    put(back_out, combine([dot_of(c0, column(m1, k)) for k in range(STREAMS)], second))

    @pl.when((pl.program_id(0) == 0) & (pl.program_id(1) == 0))
    def _():
        gram_out[...] = jnp.zeros_like(gram_out)

    for i in range(STREAMS):
        for j in range(STREAMS):
            gram_out[i * STREAMS + j] += fold(first[i] * second[j])


def prepare(hyper, streams, cotangent, sent, n_dp, travel):
    micro, _, rows, width = streams.shape
    slot, wide = rows // n_dp, 256
    block = pl.BlockSpec((1, STREAMS, rows, wide), lambda m, f: (m, 0, 0, f))
    home = pl.BlockSpec((n_dp, 1, slot, wide), lambda m, f: (0, m, 0, f))
    shape = (n_dp, micro, slot, width)
    return pl.pallas_call(
        prepare_kernel,
        grid=(micro, width // wide),
        in_specs=[SMEM, block, block, pl.BlockSpec((1, 1, rows), lambda m, f: (m, 0, 0))],
        out_specs=[home] * 4 + [pl.BlockSpec((STREAMS * STREAMS, 8, wide), lambda m, f: (0, 0, 0))],
        out_shape=[jax.ShapeDtypeStruct(shape, FULL)] * 3
        + [
            jax.ShapeDtypeStruct(shape, travel),
            jax.ShapeDtypeStruct((STREAMS * STREAMS, 8, wide), FULL),
        ],
        compiler_params=pltpu.CompilerParams(vmem_limit_bytes=ROOM),
    )(hyper, streams, cotangent, sent[:, None, :])


def finish_kernel(
    hyper, streams, cotangent, sent, y_att, y_ffn, gh_ffn, gh_att, streams_out, grad_out, dots_out
):
    rows, width = streams.shape[2:]
    (a0, m0, c0), (a1, m1, c1) = hyper_parts(hyper)
    first = [streams[0, i] for i in range(STREAMS)]
    second = [cotangent[0, j] for j in range(STREAMS)]
    match = lax.broadcasted_iota(jnp.int32, (rows, rows), 1) == sent[0]
    home_att, home_ffn, back_ffn, back_att = (
        place_rows(match, value[:, 0].reshape(rows, width)) for value in (y_att, y_ffn, gh_ffn, gh_att)
    )
    for j in range(STREAMS):
        mixed = combine([dot_of(m0[k], column(m1, j)) for k in range(STREAMS)], first)
        streams_out[0, j] = mixed + dot_of(c0, column(m1, j)) * home_att + c1[j] * home_ffn
    for i in range(STREAMS):
        mixed = combine([dot_of(m0[i], column(m1, k)) for k in range(STREAMS)], second)
        grad_out[0, i] = mixed + dot_of(m0[i], a1) * back_ffn + a0[i] * back_att

    @pl.when((pl.program_id(0) == 0) & (pl.program_id(1) == 0))
    def _():
        dots_out[...] = jnp.zeros_like(dots_out)

    pairs = (
        [(value, home_att) for value in second]
        + [(value, home_ffn) for value in second]
        + [(value, back_ffn) for value in first]
        + [(value, back_att) for value in first]
        + [(home_att, back_ffn)]
    )
    for index, (left, right) in enumerate(pairs):
        dots_out[index] += fold(left * right)


def finish(hyper, streams, cotangent, sent, homes):
    micro, _, rows, width = streams.shape
    n_dp, _, slot, _ = homes[0].shape
    wide = 256
    block = pl.BlockSpec((1, STREAMS, rows, wide), lambda m, f: (m, 0, 0, f))
    home = pl.BlockSpec((n_dp, 1, slot, wide), lambda m, f: (0, m, 0, f))
    count = 4 * STREAMS + 1
    return pl.pallas_call(
        finish_kernel,
        grid=(micro, width // wide),
        in_specs=[SMEM, block, block, pl.BlockSpec((1, rows, 1), lambda m, f: (m, 0, 0))] + [home] * 4,
        out_specs=[block, block, pl.BlockSpec((count, 8, wide), lambda m, f: (0, 0, 0))],
        out_shape=[
            jax.ShapeDtypeStruct(streams.shape, FULL),
            jax.ShapeDtypeStruct(streams.shape, FULL),
            jax.ShapeDtypeStruct((count, 8, wide), FULL),
        ],
        compiler_params=pltpu.CompilerParams(vmem_limit_bytes=ROOM),
    )(hyper, streams, cotangent, sent[:, :, None], *homes)


def turn(values_in, cosine, sine):
    half = HEAD // 2
    swapped = jnp.concatenate([values_in[:, half:], values_in[:, :half]], axis=1)
    return values_in * cosine + swapped * sine


def dot_last(left, right):
    return lax.dot_general(left, right, (((1,), (1,)), ((), ())), preferred_element_type=jnp.float32)


def dot_first(left, right):
    return lax.dot_general(left, right, (((0,), (0,)), ((), ())), preferred_element_type=jnp.float32)


def allowed_pairs(start_ref, base, block, keys):
    column = lax.broadcasted_iota(jnp.int32, (block, keys), 1)
    row = lax.broadcasted_iota(jnp.int32, (block, keys), 0) + base
    return (column >= start_ref[pl.ds(base, block)]) & (column <= row)


def attend_forward_kernel(
    block, q_in, k_in, v_in, cosine, sine, start, out, log_out, q_out, k_out, v_out
):
    length = q_in.shape[0]
    q_out[...] = turn(q_in[...], cosine[...], sine[...]).astype(jnp.bfloat16)
    k_out[...] = turn(k_in[...], cosine[...], sine[...]).astype(jnp.bfloat16)
    v_out[...] = v_in[...].astype(jnp.bfloat16)
    for base in range(0, length, block):
        keys = base + block
        scores = dot_last(q_out[pl.ds(base, block)], k_out[pl.ds(0, keys)]) * HEAD ** (-0.5)
        scores = jnp.where(allowed_pairs(start, base, block, keys), scores, -1e30)
        largest = jnp.max(scores, axis=1, keepdims=True)
        weights = jnp.exp(scores - largest)
        totals = jnp.sum(weights, axis=1, keepdims=True)
        probs = (weights * (1.0 / totals)).astype(jnp.bfloat16)
        out[pl.ds(base, block)] = jnp.dot(
            probs, v_out[pl.ds(0, keys)], preferred_element_type=jnp.float32
        ).astype(jnp.bfloat16)
        log_out[0, pl.ds(base, block)] = largest + jnp.log(totals)


def attend_backward_kernel(
    block, grad, q, k, v, log_in, cosine, sine, start, q_out, k_out, v_out, k_sum, v_sum
):
    length = q.shape[0]
    k_sum[...] = jnp.zeros_like(k_sum)
    v_sum[...] = jnp.zeros_like(v_sum)
    for base in range(0, length, block):
        keys = base + block
        rows, span = pl.ds(base, block), pl.ds(0, keys)
        scores = dot_last(q[rows], k[span]) * HEAD ** (-0.5)
        probs = jnp.where(
            allowed_pairs(start, base, block, keys), jnp.exp(scores - log_in[0, rows]), 0.0
        )
        grad_probs = dot_last(grad[rows], v[span])
        inner = jnp.sum(probs * grad_probs, axis=1, keepdims=True)
        grad_scores = (probs * (grad_probs - inner) * HEAD ** (-0.5)).astype(jnp.bfloat16)
        grad_query = jnp.dot(grad_scores, k[span], preferred_element_type=jnp.float32)
        q_out[rows] = turn(grad_query, cosine[rows], -sine[rows]).astype(jnp.bfloat16)
        k_sum[span] += dot_first(grad_scores, q[rows])
        v_sum[span] += dot_first(probs.astype(jnp.bfloat16), grad[rows])
    k_out[...] = turn(k_sum[...], cosine[...], -sine[...]).astype(jnp.bfloat16)
    v_out[...] = v_sum[...].astype(jnp.bfloat16)


def attend_forward(qkv, cosine, sine, start):
    length, width = qkv.shape
    heads = width // (3 * HEAD)
    block = min(256, length)

    def part(offset):
        return pl.BlockSpec((length, HEAD), lambda h: (0, offset + h))

    whole = pl.BlockSpec((length, HEAD), lambda h: (0, 0))
    low = jax.ShapeDtypeStruct((length, heads * HEAD), jnp.bfloat16)
    return pl.pallas_call(
        functools.partial(attend_forward_kernel, block),
        grid=(heads,),
        in_specs=[part(0), part(heads), part(2 * heads), whole, whole,
                  pl.BlockSpec((length, 1), lambda h: (0, 0))],
        out_specs=[part(0), pl.BlockSpec((1, length, 1), lambda h: (h, 0, 0)), part(0), part(0), part(0)],
        out_shape=[low, jax.ShapeDtypeStruct((heads, length, 1), jnp.float32), low, low, low],
        compiler_params=pltpu.CompilerParams(vmem_limit_bytes=40 * 2**20),
    )(qkv, qkv, qkv, cosine, sine, start)


def attend_backward(grad, q, k, v, log_totals, cosine, sine, start):
    length, width = q.shape
    heads = width // HEAD
    block = min(256, length)
    part = pl.BlockSpec((length, HEAD), lambda h: (0, h))
    whole = pl.BlockSpec((length, HEAD), lambda h: (0, 0))
    low = jax.ShapeDtypeStruct((length, width), jnp.bfloat16)
    return pl.pallas_call(
        functools.partial(attend_backward_kernel, block),
        grid=(heads,),
        in_specs=[part, part, part, part, pl.BlockSpec((1, length, 1), lambda h: (h, 0, 0)), whole, whole,
                  pl.BlockSpec((length, 1), lambda h: (0, 0))],
        out_specs=[part, part, part],
        out_shape=[low, low, low],
        scratch_shapes=[pltpu.VMEM((length, HEAD), jnp.float32)] * 2,
        compiler_params=pltpu.CompilerParams(vmem_limit_bytes=40 * 2**20),
    )(grad, q, k, v, log_totals, cosine, sine, start)


def remote(source, target, send_sem, recv_sem, device):
    return pltpu.make_async_remote_copy(
        src_ref=source,
        dst_ref=target,
        send_sem=send_sem,
        recv_sem=recv_sem,
        device_id=device,
        device_id_type=pl.DeviceIdType.MESH,
    )


def line_place():
    me = lax.axis_index("row")
    return me, me // 2, me % 2


def greet(pairs, plane=None):
    me, place, side = line_place()
    barrier = pltpu.get_barrier_semaphore()

    def signal(device):
        pl.semaphore_signal(barrier, inc=1, device_id=device, device_id_type=pl.DeviceIdType.MESH)

    signal({"row": me + 1 - 2 * side})

    @pl.when(place < pairs - 1)
    def _():
        signal({"row": me + 2})

    @pl.when(place > 0)
    def _():
        signal({"row": me - 2})

    count = 1
    if plane is not None:
        for offset in offsets(plane):
            signal(peer(plane, offset))
            count += 1
    last = pairs - 1
    neighbours = (place + last) // pairs + (2 * last - place) // pairs
    pl.semaphore_wait(barrier, count + neighbours)


def offsets(plane):
    n_dp, n_col = plane
    return [(d, c) for d in range(n_dp) for c in range(n_col) if (d, c) != (0, 0)]


def peer(plane, offset):
    n_dp, n_col = plane
    return {
        "dp": (lax.axis_index("dp") + offset[0]) % n_dp,
        "col": (lax.axis_index("col") + offset[1]) % n_col,
    }


class Exchange:
    def __init__(self, plane, source_of, target, sends, receives, keep):
        self.plane, self.source_of, self.target = plane, source_of, target
        self.sends, self.receives, self.keep = sends, receives, keep

    def move(self, offset):
        device = peer(self.plane, offset)
        return remote(
            self.source_of(device["dp"], device["col"]),
            self.target,
            self.sends.at[offset[0], offset[1]],
            self.receives.at[offset[0], offset[1]],
            device,
        )

    def stay(self):
        return pltpu.make_async_copy(
            self.source_of(lax.axis_index("dp"), lax.axis_index("col")), self.target, self.keep
        )

    def start(self):
        for offset in offsets(self.plane):
            self.move(offset).start()
        self.stay().start()

    def arrive(self):
        for offset in offsets(self.plane):
            self.move(offset).wait_recv()
        self.stay().wait()

    def leave(self):
        for offset in offsets(self.plane):
            self.move(offset).wait_send()


def exchange_sems(plane, count):
    return [DMA((count,) + plane), DMA((count,) + plane), DMA((count,))]


def work_block(work, slot, width, part, side):
    return work.at[
        pl.ds(pl.multiple_of(part * slot, slot), slot), pl.ds(pl.multiple_of(side * width, width), width)
    ]


def to_work(plane, home, work, sems, index):
    slot, width = home.shape[2:]
    return Exchange(
        plane,
        lambda b, c: home.at[b, c],
        work_block(work, slot, width, lax.axis_index("dp"), lax.axis_index("col")),
        sems[0].at[index],
        sems[1].at[index],
        sems[2].at[index],
    )


def to_home(plane, work, home, sems, index):
    slot, width = home.shape[2:]
    return Exchange(
        plane,
        lambda b, c: work_block(work, slot, width, b, c),
        home.at[lax.axis_index("dp"), lax.axis_index("col")],
        sems[0].at[index],
        sems[1].at[index],
        sems[2].at[index],
    )


class Gather:
    def __init__(self, pairs, cuts, own, out, sems):
        self.pairs, self.cuts, self.own, self.out = pairs, cuts, own, out
        self.right, self.left, self.twin_send, self.line, self.twin_recv, self.keep = sems
        self.height = own.shape[0] // cuts

    def piece(self, ref, cut):
        return ref.at[pl.ds(cut * self.height, self.height)]

    def move(self, row, sends, receives, origin, cut, first):
        _, _, side = line_place()
        block = self.piece(self.out.at[origin * 2 + side], cut)
        return remote(
            self.piece(self.own, cut) if first else block,
            block,
            sends.at[origin, cut],
            receives.at[origin, cut],
            {"row": row},
        )

    def to_twin(self, origin, cut, first=False):
        me, _, side = line_place()
        return self.move(me + 1 - 2 * side, self.twin_send, self.twin_recv, origin, cut, first)

    def to_right(self, origin, cut, first=False):
        return self.move(line_place()[0] + 2, self.right, self.line, origin, cut, first)

    def to_left(self, origin, cut, first=False):
        return self.move(line_place()[0] - 2, self.left, self.line, origin, cut, first)

    def stay(self):
        return pltpu.make_async_copy(self.own, self.out.at[line_place()[0]], self.keep)

    def start(self):
        _, place, _ = line_place()
        for cut in range(self.cuts):
            @pl.when(place < self.pairs - 1)
            def _():
                self.to_right(place, cut, True).start()

            @pl.when(place > 0)
            def _():
                self.to_left(place, cut, True).start()

        for cut in range(self.cuts):
            self.to_twin(place, cut, True).start()
        self.stay().start()

    def step(self, step, cut):
        _, place, _ = line_place()

        @pl.when(place >= step)
        def _():
            origin = place - step
            self.to_right(origin, cut).wait_recv()

            @pl.when(place < self.pairs - 1)
            def _():
                self.to_right(origin, cut).start()

            self.to_twin(origin, cut).start()

        @pl.when(place + step <= self.pairs - 1)
        def _():
            origin = place + step
            self.to_left(origin, cut).wait_recv()

            @pl.when(place > 0)
            def _():
                self.to_left(origin, cut).start()

            self.to_twin(origin, cut).start()

    def finish(self):
        me, place, side = line_place()
        self.stay().wait()
        for origin in range(self.pairs):
            for cut in range(self.cuts):
                self.to_twin(origin, cut).wait_send()
                other = self.piece(self.out.at[origin * 2 + 1 - side], cut)
                remote(
                    other,
                    other,
                    self.twin_send.at[origin, cut],
                    self.twin_recv.at[origin, cut],
                    {"row": me + 1 - 2 * side},
                ).wait_recv()

                @pl.when((place < self.pairs - 1) & (origin <= place))
                def _():
                    self.to_right(origin, cut).wait_send()

                @pl.when((place > 0) & (origin >= place))
                def _():
                    self.to_left(origin, cut).wait_send()


def gather_sems(pairs, cuts):
    return [DMA((pairs, cuts))] * 5 + [DMA]


class Scatter:
    def __init__(self, pairs, cuts, part, buffers, sems):
        self.pairs, self.cuts, self.part = pairs, cuts, part
        self.own, self.twin, self.from_left, self.from_right, self.out_right, self.out_left = buffers
        (
            self.right_send,
            self.left_send,
            self.twin_send,
            self.right_recv,
            self.left_recv,
            self.twin_recv,
            self.loaded,
        ) = sems
        self.height = part.shape[1] // cuts
        self.ready = set()

    def piece(self, ref, dest, cut):
        return ref.at[dest, pl.ds(cut * self.height, self.height)]

    def value(self, ref, dest, cut):
        return ref[dest, pl.ds(cut * self.height, self.height)].astype(FULL)

    def load(self, dest, cut):
        _, _, side = line_place()
        return pltpu.make_async_copy(
            self.piece(self.part, dest * 2 + side, cut),
            self.piece(self.own, dest, cut),
            self.loaded.at[dest, cut],
        )

    def to_twin(self, dest, cut):
        me, _, side = line_place()
        return remote(
            self.piece(self.part, dest * 2 + 1 - side, cut),
            self.piece(self.twin, dest, cut),
            self.twin_send.at[dest, cut],
            self.twin_recv.at[dest, cut],
            {"row": me + 1 - 2 * side},
        )

    def to_right(self, dest, cut):
        return remote(
            self.piece(self.out_right, dest, cut),
            self.piece(self.from_left, dest, cut),
            self.right_send.at[dest, cut],
            self.right_recv.at[dest, cut],
            {"row": line_place()[0] + 2},
        )

    def to_left(self, dest, cut):
        return remote(
            self.piece(self.out_left, dest, cut),
            self.piece(self.from_right, dest, cut),
            self.left_send.at[dest, cut],
            self.left_recv.at[dest, cut],
            {"row": line_place()[0] - 2},
        )

    def start(self):
        order = []
        for step in range(self.pairs):
            for dest in (self.pairs - 1 - step, step):
                if dest not in order:
                    order.append(dest)
        for dest in order:
            for cut in range(self.cuts):
                self.to_twin(dest, cut).start()
                self.load(dest, cut).start()

    def here(self, dest, cut):
        return self.value(self.own, dest, cut) + self.value(self.twin, dest, cut)

    def step(self, step, cut):
        _, place, _ = line_place()
        last = self.pairs - 1
        span = pl.ds(cut * self.height, self.height)
        for dest, sending, first, out, arrived, copy in (
            (last - step, place < last - step, place == 0, self.out_right, self.from_left, self.to_right),
            (step, place > step, place == last, self.out_left, self.from_right, self.to_left),
        ):
            if (dest, cut) not in self.ready:
                self.ready.add((dest, cut))
                self.to_twin(dest, cut).wait_recv()
                self.load(dest, cut).wait()

            @pl.when(sending & first)
            def _():
                out[dest, span] = self.here(dest, cut).astype(out.dtype)
                copy(dest, cut).start()

            @pl.when(sending & jnp.logical_not(first))
            def _():
                copy(dest, cut).wait_recv()
                out[dest, span] = (self.here(dest, cut) + self.value(arrived, dest, cut)).astype(out.dtype)
                copy(dest, cut).start()

    def finish(self, total):
        _, place, _ = line_place()
        last = self.pairs - 1
        for cut in range(self.cuts):
            span = pl.ds(cut * self.height, self.height)
            total[span] = self.here(place, cut)

            @pl.when(place > 0)
            def _():
                self.to_right(place, cut).wait_recv()
                total[span] += self.value(self.from_left, place, cut)

            @pl.when(place < last)
            def _():
                self.to_left(place, cut).wait_recv()
                total[span] += self.value(self.from_right, place, cut)

        for dest in range(self.pairs):
            for cut in range(self.cuts):
                self.to_twin(dest, cut).wait_send()

                @pl.when(place < dest)
                def _():
                    self.to_right(dest, cut).wait_send()

                @pl.when(place > dest)
                def _():
                    self.to_left(dest, cut).wait_send()


def scatter_buffers(pairs, rows, width):
    return [pltpu.VMEM((pairs, rows, width), LOW)] * 6


def scatter_sems(pairs, cuts):
    return [DMA((pairs, cuts))] * 7


CUTS = 2


def call_remote(kernel, collective, **options):
    return pl.pallas_call(
        kernel,
        compiler_params=pltpu.CompilerParams(
            collective_id=collective, has_side_effects=True, vmem_limit_bytes=ROOM
        ),
        **options,
    )


def enter_kernel(plane, pairs, h_home, mix_home, back_home, gy_home, rows_out, h, mix, back, gy, own, *sems):
    plane_sems, line_sems = sems[:3], sems[3:]
    greet(pairs, plane)
    first = to_work(plane, h_home, h, plane_sems, 0)
    others = [
        to_work(plane, home, work, plane_sems, index)
        for index, (home, work) in enumerate(((mix_home, mix), (back_home, back), (gy_home, gy)), 1)
    ]
    first.start()
    first.arrive()
    for other in others:
        other.start()
    own[...] = norm_forward(h[...])[0].astype(LOW)
    gather = Gather(pairs, CUTS, own, rows_out, line_sems)
    gather.start()
    for step in range(1, pairs):
        for cut in range(CUTS):
            gather.step(step, cut)
    gather.finish()
    for other in others:
        other.arrive()
        other.leave()
    first.leave()


def enter(plane, pairs, h_home, mix_home, back_home, gy_home, collective):
    n_dp, n_col, slot, width = h_home.shape
    rows = n_dp * slot
    work = jax.ShapeDtypeStruct((rows, n_col * width), FULL)
    outs = call_remote(
        functools.partial(enter_kernel, plane, pairs),
        collective,
        in_specs=[ANY] * 4,
        out_specs=[ANY, VMEM, ANY, ANY, ANY],
        out_shape=[
            jax.ShapeDtypeStruct((2 * pairs, rows, n_col * width), LOW),
            work,
            work,
            work,
            jax.ShapeDtypeStruct(work.shape, gy_home.dtype),
        ],
        scratch_shapes=[pltpu.VMEM(work.shape, LOW)] + exchange_sems(plane, 4) + gather_sems(pairs, CUTS),
    )(h_home, mix_home, back_home, gy_home)
    return [outs[0].reshape(2 * pairs * rows, n_col * width)] + list(outs[1:])


def duplex_kernel(pairs, part, gathered, rows_out, low_out, total, *scratch):
    scatter = Scatter(pairs, CUTS, part, scratch[:6], scratch[6:13])
    gather = Gather(pairs, CUTS, gathered, rows_out, scratch[13:])
    greet(pairs)
    scatter.start()
    gather.start()
    for step in range(pairs - 1):
        for cut in range(CUTS):
            scatter.step(step, cut)
            gather.step(step + 1, cut)
    scatter.finish(total)
    low_out[...] = total[...].astype(LOW)
    gather.finish()


def duplex(pairs, partial, gathered, collective):
    rows, width = gathered.shape
    whole = jax.ShapeDtypeStruct((2 * pairs, rows, width), LOW)
    outs = call_remote(
        functools.partial(duplex_kernel, pairs),
        collective,
        in_specs=[ANY, ANY],
        out_specs=[ANY, VMEM, VMEM],
        out_shape=[
            whole,
            jax.ShapeDtypeStruct((rows, width), LOW),
            jax.ShapeDtypeStruct((rows, width), FULL),
        ],
        scratch_shapes=scatter_buffers(pairs, rows, width)
        + scatter_sems(pairs, CUTS)
        + gather_sems(pairs, CUTS),
    )(partial.reshape(whole.shape), gathered)
    return [outs[0].reshape(2 * pairs * rows, width)] + list(outs[1:])


def middle_kernel(pairs, hyper, mix, branch, rows_out, h, own, *sems):
    greet(pairs)
    h[...] = mix[...] + branch_weight(hyper) * branch[...]
    own[...] = norm_forward(h[...])[0].astype(LOW)
    gather = Gather(pairs, CUTS, own, rows_out, sems)
    gather.start()
    for step in range(1, pairs):
        for cut in range(CUTS):
            gather.step(step, cut)
    gather.finish()


def middle(pairs, hyper, mix, branch, collective):
    rows, width = mix.shape
    outs = call_remote(
        functools.partial(middle_kernel, pairs),
        collective,
        in_specs=[SMEM, VMEM, VMEM],
        out_specs=[ANY, VMEM],
        out_shape=[
            jax.ShapeDtypeStruct((2 * pairs, rows, width), LOW),
            jax.ShapeDtypeStruct((rows, width), FULL),
        ],
        scratch_shapes=[pltpu.VMEM((rows, width), LOW)] + gather_sems(pairs, CUTS),
    )(hyper, mix, branch)
    return outs[0].reshape(2 * pairs * rows, width), outs[1]


def turn_back_kernel(pairs, hyper, part, h, back, gh_out, gy_out, total, *scratch):
    scatter = Scatter(pairs, CUTS, part, scratch[:6], scratch[6:])
    greet(pairs)
    scatter.start()
    for step in range(pairs - 1):
        for cut in range(CUTS):
            scatter.step(step, cut)
    scatter.finish(total)
    grad = norm_backward(total[...], h[...])
    gh_out[...] = grad.astype(LOW)
    gy_out[...] = (back[...] + branch_weight(hyper) * grad).astype(LOW)


def turn_back(pairs, hyper, partial, h, back, collective):
    rows, width = h.shape
    low = jax.ShapeDtypeStruct((rows, width), LOW)
    return call_remote(
        functools.partial(turn_back_kernel, pairs),
        collective,
        in_specs=[SMEM, ANY, VMEM, VMEM],
        out_specs=[VMEM, VMEM],
        out_shape=[low, low],
        scratch_shapes=[pltpu.VMEM((rows, width), FULL)]
        + scatter_buffers(pairs, rows, width)
        + scatter_sems(pairs, CUTS),
    )(hyper, partial.reshape(2 * pairs, rows, width), h, back)


def leave_kernel(plane, pairs, part, h, y_att, y_ffn, gh_ffn, *rest):
    homes, total, last = rest[:4], rest[4], rest[5]
    plane_sems, scratch = rest[6:9], rest[9:]
    scatter = Scatter(pairs, CUTS, part, scratch[:6], scratch[6:])
    greet(pairs, plane)
    scatter.start()
    ways = [
        to_home(plane, work, home, plane_sems, index)
        for index, (work, home) in enumerate(zip((y_att, y_ffn, gh_ffn, last), homes))
    ]
    for way in ways[:3]:
        way.start()
    for step in range(pairs - 1):
        for cut in range(CUTS):
            scatter.step(step, cut)
    scatter.finish(total)
    last[...] = norm_backward(total[...], h[...]).astype(last.dtype)
    ways[3].start()
    for way in ways:
        way.arrive()
        way.leave()


def leave(plane, pairs, partial, h, works, collective):
    rows, width = h.shape
    n_dp, n_col = plane
    home = jax.ShapeDtypeStruct((n_dp, n_col, rows // n_dp, width // n_col), works[0].dtype)
    return call_remote(
        functools.partial(leave_kernel, plane, pairs),
        collective,
        in_specs=[ANY, VMEM, ANY, ANY, ANY],
        out_specs=[ANY] * 4,
        out_shape=[home] * 4,
        scratch_shapes=[pltpu.VMEM((rows, width), FULL), pltpu.VMEM((rows, width), works[0].dtype)]
        + exchange_sems(plane, 4)
        + scatter_buffers(pairs, rows, width)
        + scatter_sems(pairs, CUTS),
    )(partial.reshape(2 * pairs, rows, width), h, *works)


def total_kernel(plane, count, own, out, line, flat, line_send, line_recv, flat_send, flat_recv):
    n_dp, n_col = plane
    me = lax.axis_index("row")
    here = lax.axis_index("dp") * n_col + lax.axis_index("col")
    barrier = pltpu.get_barrier_semaphore()
    rows = [(me + step) % count for step in range(1, count)]
    for row in rows:
        pl.semaphore_signal(barrier, inc=1, device_id={"row": row}, device_id_type=pl.DeviceIdType.MESH)
    for offset in offsets(plane):
        pl.semaphore_signal(
            barrier, inc=1, device_id=peer(plane, offset), device_id_type=pl.DeviceIdType.MESH
        )
    pl.semaphore_wait(barrier, count - 1 + n_dp * n_col - 1)
    line[me] = own[...]
    copies = [
        remote(line.at[me], line.at[me], line_send.at[step], line_recv.at[step], {"row": row})
        for step, row in enumerate(rows)
    ]
    for copy in copies:
        copy.start()
    for copy in copies:
        copy.wait()
    sums = line[0]
    for row in range(1, count):
        sums = sums + line[row]
    flat[here] = sums
    copies = [
        remote(
            flat.at[here],
            flat.at[here],
            flat_send.at[offset[0], offset[1]],
            flat_recv.at[offset[0], offset[1]],
            peer(plane, offset),
        )
        for offset in offsets(plane)
    ]
    for copy in copies:
        copy.start()
    for copy in copies:
        copy.wait()
    sums = flat[0]
    for index in range(1, n_dp * n_col):
        sums = sums + flat[index]
    out[...] = sums


def sum_everywhere(plane, values_in, collective):
    count = lax.axis_size("row")
    shape = values_in.shape
    return call_remote(
        functools.partial(total_kernel, plane, count),
        collective,
        in_specs=[VMEM],
        out_specs=VMEM,
        out_shape=jax.ShapeDtypeStruct(shape, FULL),
        scratch_shapes=[
            pltpu.VMEM((count,) + shape, FULL),
            pltpu.VMEM((plane[0] * plane[1],) + shape, FULL),
            DMA((count - 1,)),
            DMA((count - 1,)),
            DMA(plane),
            DMA(plane),
        ],
    )(values_in)


def mat(left, right):
    return jnp.sum(left[:, :, None] * right[None, :, :], axis=1)


def gather_blocks(weight_low):
    return lax.all_gather(weight_low, ("col", "dp"), axis=0, tiled=True)


def scatter_blocks(grad_low):
    return lax.psum_scatter(grad_low, ("col", "dp"), scatter_dimension=0, tiled=True).astype(FULL)


def side_by_side(weight):
    return jnp.concatenate([weight[index] for index in range(weight.shape[0])], axis=1)


def apart(weight, count):
    width = weight.shape[1] // count
    return jnp.stack([weight[:, index * width : (index + 1) * width] for index in range(count)])


def whole_out(weight_low, n_dp, n_col):
    rows, width = weight_low.shape
    blocks = gather_blocks(weight_low).reshape(n_col, n_dp, rows, width)
    return blocks.transpose(1, 2, 0, 3).reshape(n_dp * rows, n_col * width)


def own_out(grad, n_dp, n_col):
    rows, width = grad.shape[0] // n_dp, grad.shape[1] // n_col
    blocks = grad.astype(LOW).reshape(n_dp, rows, n_col, width).transpose(2, 0, 1, 3)
    return scatter_blocks(blocks.reshape(n_col * n_dp * rows, width))


def adam_update(weight, grad_sum, moment_one, moment_two, clip_factor, step_value):
    clipped = grad_sum * clip_factor
    new_one = beta_first * moment_one + (1.0 - beta_first) * clipped
    new_two = beta_second * moment_two + (1.0 - beta_second) * clipped * clipped
    fix_one = 1.0 - jnp.power(beta_first, step_value)
    fix_two = 1.0 - jnp.power(beta_second, step_value)
    new_weight = weight - learning_rate * (
        new_one / fix_one / (jnp.sqrt(new_two / fix_two) + adam_eps) + weight_decay * weight
    )
    return (new_weight, new_one, new_two)


def body(
    streams,
    cotangent,
    destination,
    segments,
    attention_in,
    feedforward_in,
    attention_out,
    feedforward_out,
    attention_in_moment,
    feedforward_in_moment,
    attention_out_moment,
    feedforward_out_moment,
    attention_in_second,
    feedforward_in_second,
    attention_out_second,
    feedforward_out_second,
    hyper_weights,
    hyper_moment,
    hyper_second,
    step_count,
):
    n_dp, n_col, count = lax.axis_size("dp"), lax.axis_size("col"), lax.axis_size("row")
    plane, pairs = (n_dp, n_col), count // 2
    rows = destination.shape[1]
    group_tokens = segments.shape[2]
    slot = rows // n_dp
    travel = LOW if slot % 16 == 0 else FULL
    attention_in_low = gather_blocks(side_by_side(attention_in).astype(LOW))
    attention_out_low = whole_out(attention_out.astype(LOW), n_dp, n_col)
    feedforward_in_low = gather_blocks(side_by_side(feedforward_in).astype(LOW))
    feedforward_out_low = whole_out(feedforward_out.astype(LOW), n_dp, n_col)

    group = destination // group_tokens
    sent = (
        group * slot
        + (destination - group * group_tokens)
        - lax.axis_index("row") * rows
        - lax.axis_index("dp") * slot
    )
    hyper = hyper_weights.reshape(-1)
    h_home, mix_home, back_home, gy_home, gram = prepare(
        hyper, streams, cotangent, sent, n_dp, travel
    )
    segment = lax.dynamic_index_in_dim(segments[:, 0], lax.axis_index("col"), 0, keepdims=False)
    cosine, sine, start = rotary_tables(segment)

    rows_att, hidden_att, mix_work, back_work, gy_work = enter(
        plane, pairs, h_home, mix_home, back_home, gy_home, 1
    )
    qkv = jnp.dot(rows_att, attention_in_low, preferred_element_type=FULL)
    heads_low, log_totals, query_low, key_low, value_low = attend_forward(qkv, cosine, sine, start)
    partial_att = jnp.dot(heads_low, attention_out_low, preferred_element_type=FULL).astype(LOW)
    grad_rows_ffn, branch_low, branch_att = duplex(pairs, partial_att, gy_work.astype(LOW), 2)
    rows_ffn, hidden_ffn = middle(pairs, hyper, mix_work, branch_att, 3)

    gate_up = jnp.dot(rows_ffn, feedforward_in_low, preferred_element_type=FULL)
    units = gate_up.shape[1] // 2
    gate_pre, up_pre = gate_up[:, :units], gate_up[:, units:]
    sigma = jax.nn.sigmoid(gate_pre)
    silu = gate_pre * sigma
    hidden_low = (silu * up_pre).astype(LOW)
    grad_hidden = jnp.einsum("td,ud->tu", grad_rows_ffn, feedforward_out_low, preferred_element_type=FULL)
    grad_gate = (grad_hidden * up_pre * sigma * (1.0 + gate_pre * (1.0 - sigma))).astype(LOW)
    grad_up = (grad_hidden * silu).astype(LOW)
    grad_units = jnp.concatenate([grad_gate, grad_up], axis=1)
    partial_grad = jnp.einsum(
        "tu,du->td", grad_units, feedforward_in_low, preferred_element_type=FULL
    ).astype(LOW)
    grad_hidden_ffn, grad_branch = turn_back(pairs, hyper, partial_grad, hidden_ffn, back_work, 4)
    partial_ffn = jnp.dot(hidden_low, feedforward_out_low, preferred_element_type=FULL).astype(LOW)
    shard_feedforward_in = apart(
        scatter_blocks(
            jnp.einsum("td,tu->du", rows_ffn, grad_units, preferred_element_type=FULL).astype(LOW)
        ),
        2,
    )
    shard_feedforward_out = own_out(
        jnp.einsum("tu,td->ud", hidden_low, grad_rows_ffn, preferred_element_type=FULL), n_dp, n_col
    )
    grad_rows_att, branch_ffn, _ = duplex(pairs, partial_ffn, grad_branch, 5)

    shard_attention_out = own_out(
        jnp.einsum("tu,td->ud", heads_low, grad_rows_att, preferred_element_type=FULL), n_dp, n_col
    )
    grad_heads = jnp.einsum(
        "td,ud->tu", grad_rows_att, attention_out_low, preferred_element_type=FULL
    ).astype(LOW)
    grad_units_att = jnp.concatenate(
        attend_backward(grad_heads, query_low, key_low, value_low, log_totals, cosine, sine, start),
        axis=1,
    )
    shard_attention_in = apart(
        scatter_blocks(
            jnp.einsum("td,tu->du", rows_att, grad_units_att, preferred_element_type=FULL).astype(LOW)
        ),
        3,
    )
    partial_grad = jnp.einsum(
        "tu,du->td", grad_units_att, attention_in_low, preferred_element_type=FULL
    ).astype(LOW)
    homes = leave(
        plane,
        pairs,
        partial_grad,
        hidden_att,
        [value.astype(travel) for value in (branch_low, branch_ffn, grad_hidden_ffn)],
        6,
    )
    streams_out, stream_grad, dots = finish(hyper, streams, cotangent, sent, homes)
    square = (
        jnp.sum(shard_attention_in * shard_attention_in)
        + jnp.sum(shard_feedforward_in * shard_feedforward_in)
        + jnp.sum(shard_attention_out * shard_attention_out)
        + jnp.sum(shard_feedforward_out * shard_feedforward_out)
    )
    dots = jnp.concatenate([jnp.sum(gram, axis=(1, 2)), jnp.sum(dots, axis=(1, 2)), square[None]])
    totals = sum_everywhere(plane, jnp.pad(dots, (0, 128 - dots.shape[0])).reshape(1, 128), 7)[0]
    a0, m0, c0 = hyper_weights[0, :, 0], hyper_weights[0, :, 1:5], hyper_weights[0, :, 5]
    a1, m1, c1 = hyper_weights[1, :, 0], hyper_weights[1, :, 1:5], hyper_weights[1, :, 5]
    gram = totals[:16].reshape(STREAMS, STREAMS)
    att_cot, ffn_cot = totals[16:20], totals[20:24]
    streams_ffn, streams_att = totals[24:28], totals[28:32]
    att_ffn, square_total = totals[32], totals[33]
    grad_m1 = mat(m0.T, gram) + c0[:, None] * att_cot[None, :]
    grad_a1 = jnp.sum(m0 * streams_ffn[:, None], axis=0) + c0 * att_ffn
    grad_m0 = mat(gram, m1.T) + streams_ffn[:, None] * a1[None, :]
    grad_c0 = jnp.sum(m1 * att_cot[None, :], axis=1) + a1 * att_ffn
    hyper_grad = jnp.stack(
        [
            jnp.concatenate([streams_att[:, None], grad_m0, grad_c0[:, None]], axis=1),
            jnp.concatenate([grad_a1[:, None], grad_m1, ffn_cot[:, None]], axis=1),
        ]
    )
    grad_norm = jnp.sqrt(square_total + jnp.sum(hyper_grad * hyper_grad))
    clip_factor = 1.0 / jnp.maximum(grad_norm, 1.0)
    step_value = step_count[0].astype(jnp.float32)
    attention_in_new = adam_update(
        attention_in,
        shard_attention_in,
        attention_in_moment,
        attention_in_second,
        clip_factor,
        step_value,
    )
    feedforward_in_new = adam_update(
        feedforward_in,
        shard_feedforward_in,
        feedforward_in_moment,
        feedforward_in_second,
        clip_factor,
        step_value,
    )
    attention_out_new = adam_update(
        attention_out,
        shard_attention_out,
        attention_out_moment,
        attention_out_second,
        clip_factor,
        step_value,
    )
    feedforward_out_new = adam_update(
        feedforward_out,
        shard_feedforward_out,
        feedforward_out_moment,
        feedforward_out_second,
        clip_factor,
        step_value,
    )
    hyper_new = adam_update(
        hyper_weights, hyper_grad, hyper_moment, hyper_second, clip_factor, step_value
    )
    return (
        streams_out,
        stream_grad,
        grad_norm.reshape(1),
        shard_attention_in,
        shard_feedforward_in,
        shard_attention_out,
        shard_feedforward_out,
        hyper_grad,
        attention_in_new[0],
        feedforward_in_new[0],
        attention_out_new[0],
        feedforward_out_new[0],
        hyper_new[0],
        attention_in_new[1],
        feedforward_in_new[1],
        attention_out_new[1],
        feedforward_out_new[1],
        hyper_new[1],
        attention_in_new[2],
        feedforward_in_new[2],
        attention_out_new[2],
        feedforward_out_new[2],
        hyper_new[2],
    )


def solution(mesh):
    placed = (
        P(None, None, ("dp", "row"), "col"),
        P(None, None, ("dp", "row"), "col"),
        P(None, ("dp", "row")),
        P(None, "dp", None),
        P(None, ("col", "dp"), "row"),
        P(None, ("col", "dp"), "row"),
        P(("row", "dp"), "col"),
        P(("row", "dp"), "col"),
        P(None, ("col", "dp"), "row"),
        P(None, ("col", "dp"), "row"),
        P(("row", "dp"), "col"),
        P(("row", "dp"), "col"),
        P(None, ("col", "dp"), "row"),
        P(None, ("col", "dp"), "row"),
        P(("row", "dp"), "col"),
        P(("row", "dp"), "col"),
        P(),
        P(),
        P(),
        P(),
    )
    return jax.shard_map(
        body,
        mesh=mesh,
        in_specs=placed,
        out_specs=(
            P(None, None, ("dp", "row"), "col"),
            P(None, None, ("dp", "row"), "col"),
            P(),
            P(None, ("col", "dp"), "row"),
            P(None, ("col", "dp"), "row"),
            P(("row", "dp"), "col"),
            P(("row", "dp"), "col"),
            P(),
            P(None, ("col", "dp"), "row"),
            P(None, ("col", "dp"), "row"),
            P(("row", "dp"), "col"),
            P(("row", "dp"), "col"),
            P(),
            P(None, ("col", "dp"), "row"),
            P(None, ("col", "dp"), "row"),
            P(("row", "dp"), "col"),
            P(("row", "dp"), "col"),
            P(),
            P(None, ("col", "dp"), "row"),
            P(None, ("col", "dp"), "row"),
            P(("row", "dp"), "col"),
            P(("row", "dp"), "col"),
            P(),
        ),
        check_vma=False,
    )
```

```python
import functools
import math

import jax
import jax.numpy as jnp
from jax import lax
from jax.experimental import pallas as pl
from jax.experimental.pallas import tpu as pltpu
from jax.sharding import PartitionSpec as P

D = 2048
HEAD = 128
STREAMS = 4
MICRO = 2


norm_eps = 1e-05
beta_first = 0.9
beta_second = 0.95
adam_eps = 1e-08
learning_rate = 0.05
weight_decay = 0.1

LOW = jnp.bfloat16
FULL = jnp.float32
DMA = pltpu.SemaphoreType.DMA
ANY = pl.BlockSpec(memory_space=pl.ANY)
VMEM = pl.BlockSpec(memory_space=pltpu.VMEM)
SMEM = pl.BlockSpec(memory_space=pltpu.SMEM)
ROOM = 60 * 2**20


def rotary_tables(segment):
    length = segment.shape[0]
    places = jnp.arange(length, dtype=jnp.int32)
    starts = jnp.sum((segment[None, :] < segment[:, None]).astype(jnp.int32), axis=1)
    offsets = (places - starts).astype(jnp.float32)
    halves = jnp.arange(HEAD // 2, dtype=jnp.float32)
    inverse = jnp.exp(halves * (-2.0 * math.log(10000.0) / HEAD))
    angles = offsets[:, None] * inverse[None, :]
    cosine, sine = jnp.cos(angles), jnp.sin(angles)
    return (
        jnp.concatenate([cosine, cosine], axis=1),
        jnp.concatenate([-sine, sine], axis=1),
        starts[:, None],
    )


def norm_forward(hidden):
    means = jnp.sum(hidden, axis=-1, keepdims=True) / D
    squares = jnp.sum(hidden * hidden, axis=-1, keepdims=True) / D
    inverse = lax.rsqrt(squares - means * means + norm_eps)
    return ((hidden - means) * inverse, inverse)


def norm_backward(upstream, hidden):
    normed, inverse = norm_forward(hidden)
    mean_one = jnp.sum(upstream, axis=-1, keepdims=True) / D
    mean_two = jnp.sum(upstream * normed, axis=-1, keepdims=True) / D
    return inverse * (upstream - mean_one - normed * mean_two)


def hyper_parts(hyper):
    width = STREAMS + 2
    parts = []
    for layer in range(2):
        at = [[hyper[(layer * STREAMS + i) * width + k] for k in range(width)] for i in range(STREAMS)]
        parts.append(
            ([row[0] for row in at], [row[1 : STREAMS + 1] for row in at], [row[-1] for row in at])
        )
    return parts


def dot_of(left, right):
    total = left[0] * right[0]
    for a, b in zip(left[1:], right[1:]):
        total = total + a * b
    return total


def column(matrix, index):
    return [row[index] for row in matrix]


def branch_weight(hyper):
    (_, _, c0), (a1, _, _) = hyper_parts(hyper)
    return dot_of(a1, c0)


def combine(weights, stream_set):
    return dot_of(weights, stream_set)


def fold(product):
    rows, width = product.shape
    return jnp.sum(product.reshape(rows // 8, 8, width), axis=0)


def place_rows(match, values_in):
    if values_in.dtype == LOW:
        return jnp.dot(match.astype(LOW), values_in, preferred_element_type=FULL)
    return jnp.dot(
        match.astype(FULL), values_in, precision=lax.Precision.HIGHEST, preferred_element_type=FULL
    )


def prepare_kernel(hyper, streams, cotangent, sent, h_out, mix_out, back_out, gy_out, gram_out):
    rows, width = streams.shape[2:]
    parts, slot = h_out.shape[0], h_out.shape[2]
    (a0, m0, c0), (a1, m1, c1) = hyper_parts(hyper)
    first = [streams[0, i] for i in range(STREAMS)]
    second = [cotangent[0, j] for j in range(STREAMS)]
    match = lax.broadcasted_iota(jnp.int32, (rows, rows), 0) == sent[0]

    def put(out, values_in):
        moved = place_rows(match, values_in)
        for part in range(parts):
            out[part, 0] = moved[part * slot : (part + 1) * slot].astype(out.dtype)

    put(h_out, combine(a0, first))
    put(mix_out, combine([dot_of(row, a1) for row in m0], first))
    put(gy_out, combine(c1, second).astype(LOW))
    put(back_out, combine([dot_of(c0, column(m1, k)) for k in range(STREAMS)], second))

    @pl.when((pl.program_id(0) == 0) & (pl.program_id(1) == 0))
    def _():
        gram_out[...] = jnp.zeros_like(gram_out)

    for i in range(STREAMS):
        for j in range(STREAMS):
            gram_out[i * STREAMS + j] += fold(first[i] * second[j])


def prepare(hyper, streams, cotangent, sent, n_dp, travel):
    micro, _, rows, width = streams.shape
    slot, wide = rows // n_dp, 256
    block = pl.BlockSpec((1, STREAMS, rows, wide), lambda m, f: (m, 0, 0, f))
    home = pl.BlockSpec((n_dp, 1, slot, wide), lambda m, f: (0, m, 0, f))
    shape = (n_dp, micro, slot, width)
    return pl.pallas_call(
        prepare_kernel,
        grid=(micro, width // wide),
        in_specs=[SMEM, block, block, pl.BlockSpec((1, 1, rows), lambda m, f: (m, 0, 0))],
        out_specs=[home] * 4 + [pl.BlockSpec((STREAMS * STREAMS, 8, wide), lambda m, f: (0, 0, 0))],
        out_shape=[jax.ShapeDtypeStruct(shape, FULL)] * 3
        + [
            jax.ShapeDtypeStruct(shape, travel),
            jax.ShapeDtypeStruct((STREAMS * STREAMS, 8, wide), FULL),
        ],
        compiler_params=pltpu.CompilerParams(vmem_limit_bytes=ROOM),
    )(hyper, streams, cotangent, sent[:, None, :])


def finish_kernel(
    hyper, streams, cotangent, sent, y_att, y_ffn, gh_ffn, gh_att, streams_out, grad_out, dots_out
):
    rows, width = streams.shape[2:]
    (a0, m0, c0), (a1, m1, c1) = hyper_parts(hyper)
    first = [streams[0, i] for i in range(STREAMS)]
    second = [cotangent[0, j] for j in range(STREAMS)]
    match = lax.broadcasted_iota(jnp.int32, (rows, rows), 1) == sent[0]
    home_att, home_ffn, back_ffn, back_att = (
        place_rows(match, value[:, 0].reshape(rows, width)) for value in (y_att, y_ffn, gh_ffn, gh_att)
    )
    for j in range(STREAMS):
        mixed = combine([dot_of(m0[k], column(m1, j)) for k in range(STREAMS)], first)
        streams_out[0, j] = mixed + dot_of(c0, column(m1, j)) * home_att + c1[j] * home_ffn
    for i in range(STREAMS):
        mixed = combine([dot_of(m0[i], column(m1, k)) for k in range(STREAMS)], second)
        grad_out[0, i] = mixed + dot_of(m0[i], a1) * back_ffn + a0[i] * back_att

    @pl.when((pl.program_id(0) == 0) & (pl.program_id(1) == 0))
    def _():
        dots_out[...] = jnp.zeros_like(dots_out)

    pairs = (
        [(value, home_att) for value in second]
        + [(value, home_ffn) for value in second]
        + [(value, back_ffn) for value in first]
        + [(value, back_att) for value in first]
        + [(home_att, back_ffn)]
    )
    for index, (left, right) in enumerate(pairs):
        dots_out[index] += fold(left * right)


def finish(hyper, streams, cotangent, sent, homes):
    micro, _, rows, width = streams.shape
    n_dp, _, slot, _ = homes[0].shape
    wide = 256
    block = pl.BlockSpec((1, STREAMS, rows, wide), lambda m, f: (m, 0, 0, f))
    home = pl.BlockSpec((n_dp, 1, slot, wide), lambda m, f: (0, m, 0, f))
    count = 4 * STREAMS + 1
    return pl.pallas_call(
        finish_kernel,
        grid=(micro, width // wide),
        in_specs=[SMEM, block, block, pl.BlockSpec((1, rows, 1), lambda m, f: (m, 0, 0))] + [home] * 4,
        out_specs=[block, block, pl.BlockSpec((count, 8, wide), lambda m, f: (0, 0, 0))],
        out_shape=[
            jax.ShapeDtypeStruct(streams.shape, FULL),
            jax.ShapeDtypeStruct(streams.shape, FULL),
            jax.ShapeDtypeStruct((count, 8, wide), FULL),
        ],
        compiler_params=pltpu.CompilerParams(vmem_limit_bytes=ROOM),
    )(hyper, streams, cotangent, sent[:, :, None], *homes)


def turn(values_in, cosine, sine):
    half = HEAD // 2
    swapped = jnp.concatenate([values_in[:, half:], values_in[:, :half]], axis=1)
    return values_in * cosine + swapped * sine


def dot_last(left, right):
    return lax.dot_general(left, right, (((1,), (1,)), ((), ())), preferred_element_type=jnp.float32)


def dot_first(left, right):
    return lax.dot_general(left, right, (((0,), (0,)), ((), ())), preferred_element_type=jnp.float32)


def allowed_pairs(start_ref, base, block, keys):
    column = lax.broadcasted_iota(jnp.int32, (block, keys), 1)
    row = lax.broadcasted_iota(jnp.int32, (block, keys), 0) + base
    return (column >= start_ref[pl.ds(base, block)]) & (column <= row)


def attend_forward_kernel(
    block, q_in, k_in, v_in, cosine, sine, start, out, log_out, q_out, k_out, v_out
):
    length = q_in.shape[0]
    q_out[...] = turn(q_in[...], cosine[...], sine[...]).astype(jnp.bfloat16)
    k_out[...] = turn(k_in[...], cosine[...], sine[...]).astype(jnp.bfloat16)
    v_out[...] = v_in[...].astype(jnp.bfloat16)
    for base in range(0, length, block):
        keys = base + block
        scores = dot_last(q_out[pl.ds(base, block)], k_out[pl.ds(0, keys)]) * HEAD ** (-0.5)
        scores = jnp.where(allowed_pairs(start, base, block, keys), scores, -1e30)
        largest = jnp.max(scores, axis=1, keepdims=True)
        weights = jnp.exp(scores - largest)
        totals = jnp.sum(weights, axis=1, keepdims=True)
        probs = (weights * (1.0 / totals)).astype(jnp.bfloat16)
        out[pl.ds(base, block)] = jnp.dot(
            probs, v_out[pl.ds(0, keys)], preferred_element_type=jnp.float32
        ).astype(jnp.bfloat16)
        log_out[0, pl.ds(base, block)] = largest + jnp.log(totals)


def attend_backward_kernel(
    block, grad, q, k, v, log_in, cosine, sine, start, q_out, k_out, v_out, k_sum, v_sum
):
    length = q.shape[0]
    k_sum[...] = jnp.zeros_like(k_sum)
    v_sum[...] = jnp.zeros_like(v_sum)
    for base in range(0, length, block):
        keys = base + block
        rows, span = pl.ds(base, block), pl.ds(0, keys)
        scores = dot_last(q[rows], k[span]) * HEAD ** (-0.5)
        probs = jnp.where(
            allowed_pairs(start, base, block, keys), jnp.exp(scores - log_in[0, rows]), 0.0
        )
        grad_probs = dot_last(grad[rows], v[span])
        inner = jnp.sum(probs * grad_probs, axis=1, keepdims=True)
        grad_scores = (probs * (grad_probs - inner) * HEAD ** (-0.5)).astype(jnp.bfloat16)
        grad_query = jnp.dot(grad_scores, k[span], preferred_element_type=jnp.float32)
        q_out[rows] = turn(grad_query, cosine[rows], -sine[rows]).astype(jnp.bfloat16)
        k_sum[span] += dot_first(grad_scores, q[rows])
        v_sum[span] += dot_first(probs.astype(jnp.bfloat16), grad[rows])
    k_out[...] = turn(k_sum[...], cosine[...], -sine[...]).astype(jnp.bfloat16)
    v_out[...] = v_sum[...].astype(jnp.bfloat16)


def attend_forward(qkv, cosine, sine, start):
    length, width = qkv.shape
    heads = width // (3 * HEAD)
    block = min(256, length)

    def part(offset):
        return pl.BlockSpec((length, HEAD), lambda h: (0, offset + h))

    whole = pl.BlockSpec((length, HEAD), lambda h: (0, 0))
    low = jax.ShapeDtypeStruct((length, heads * HEAD), jnp.bfloat16)
    return pl.pallas_call(
        functools.partial(attend_forward_kernel, block),
        grid=(heads,),
        in_specs=[part(0), part(heads), part(2 * heads), whole, whole,
                  pl.BlockSpec((length, 1), lambda h: (0, 0))],
        out_specs=[part(0), pl.BlockSpec((1, length, 1), lambda h: (h, 0, 0)), part(0), part(0), part(0)],
        out_shape=[low, jax.ShapeDtypeStruct((heads, length, 1), jnp.float32), low, low, low],
        compiler_params=pltpu.CompilerParams(vmem_limit_bytes=40 * 2**20),
    )(qkv, qkv, qkv, cosine, sine, start)


def attend_backward(grad, q, k, v, log_totals, cosine, sine, start):
    length, width = q.shape
    heads = width // HEAD
    block = min(256, length)
    part = pl.BlockSpec((length, HEAD), lambda h: (0, h))
    whole = pl.BlockSpec((length, HEAD), lambda h: (0, 0))
    low = jax.ShapeDtypeStruct((length, width), jnp.bfloat16)
    return pl.pallas_call(
        functools.partial(attend_backward_kernel, block),
        grid=(heads,),
        in_specs=[part, part, part, part, pl.BlockSpec((1, length, 1), lambda h: (h, 0, 0)), whole, whole,
                  pl.BlockSpec((length, 1), lambda h: (0, 0))],
        out_specs=[part, part, part],
        out_shape=[low, low, low],
        scratch_shapes=[pltpu.VMEM((length, HEAD), jnp.float32)] * 2,
        compiler_params=pltpu.CompilerParams(vmem_limit_bytes=40 * 2**20),
    )(grad, q, k, v, log_totals, cosine, sine, start)


def remote(source, target, send_sem, recv_sem, device):
    return pltpu.make_async_remote_copy(
        src_ref=source,
        dst_ref=target,
        send_sem=send_sem,
        recv_sem=recv_sem,
        device_id=device,
        device_id_type=pl.DeviceIdType.MESH,
    )


def line_place():
    me = lax.axis_index("row")
    return me, me // 2, me % 2


def greet(pairs, plane=None):
    me, place, side = line_place()
    barrier = pltpu.get_barrier_semaphore()

    def signal(device):
        pl.semaphore_signal(barrier, inc=1, device_id=device, device_id_type=pl.DeviceIdType.MESH)

    signal({"row": me + 1 - 2 * side})

    @pl.when(place < pairs - 1)
    def _():
        signal({"row": me + 2})

    @pl.when(place > 0)
    def _():
        signal({"row": me - 2})

    count = 1
    if plane is not None:
        for offset in offsets(plane):
            signal(peer(plane, offset))
            count += 1
    last = pairs - 1
    neighbours = (place + last) // pairs + (2 * last - place) // pairs
    pl.semaphore_wait(barrier, count + neighbours)


def offsets(plane):
    n_dp, n_col = plane
    return [(d, c) for d in range(n_dp) for c in range(n_col) if (d, c) != (0, 0)]


def peer(plane, offset):
    n_dp, n_col = plane
    return {
        "dp": (lax.axis_index("dp") + offset[0]) % n_dp,
        "col": (lax.axis_index("col") + offset[1]) % n_col,
    }


class Exchange:
    def __init__(self, plane, source_of, target, sends, receives, keep):
        self.plane, self.source_of, self.target = plane, source_of, target
        self.sends, self.receives, self.keep = sends, receives, keep

    def move(self, offset):
        device = peer(self.plane, offset)
        return remote(
            self.source_of(device["dp"], device["col"]),
            self.target,
            self.sends.at[offset[0], offset[1]],
            self.receives.at[offset[0], offset[1]],
            device,
        )

    def stay(self):
        return pltpu.make_async_copy(
            self.source_of(lax.axis_index("dp"), lax.axis_index("col")), self.target, self.keep
        )

    def start(self):
        for offset in offsets(self.plane):
            self.move(offset).start()
        self.stay().start()

    def arrive(self):
        for offset in offsets(self.plane):
            self.move(offset).wait_recv()
        self.stay().wait()

    def leave(self):
        for offset in offsets(self.plane):
            self.move(offset).wait_send()


def exchange_sems(plane, count):
    return [DMA((count,) + plane), DMA((count,) + plane), DMA((count,))]


def work_block(work, slot, width, part, side):
    return work.at[
        pl.ds(pl.multiple_of(part * slot, slot), slot), pl.ds(pl.multiple_of(side * width, width), width)
    ]


def to_work(plane, home, work, sems, index):
    slot, width = home.shape[2:]
    return Exchange(
        plane,
        lambda b, c: home.at[b, c],
        work_block(work, slot, width, lax.axis_index("dp"), lax.axis_index("col")),
        sems[0].at[index],
        sems[1].at[index],
        sems[2].at[index],
    )


def to_home(plane, work, home, sems, index):
    slot, width = home.shape[2:]
    return Exchange(
        plane,
        lambda b, c: work_block(work, slot, width, b, c),
        home.at[lax.axis_index("dp"), lax.axis_index("col")],
        sems[0].at[index],
        sems[1].at[index],
        sems[2].at[index],
    )


class Gather:
    def __init__(self, pairs, cuts, own, out, sems):
        self.pairs, self.cuts, self.own, self.out = pairs, cuts, own, out
        self.right, self.left, self.twin_send, self.line, self.twin_recv, self.keep = sems
        self.height = own.shape[0] // cuts

    def piece(self, ref, cut):
        return ref.at[pl.ds(cut * self.height, self.height)]

    def move(self, row, sends, receives, origin, cut, first):
        _, _, side = line_place()
        block = self.piece(self.out.at[origin * 2 + side], cut)
        return remote(
            self.piece(self.own, cut) if first else block,
            block,
            sends.at[origin, cut],
            receives.at[origin, cut],
            {"row": row},
        )

    def to_twin(self, origin, cut, first=False):
        me, _, side = line_place()
        return self.move(me + 1 - 2 * side, self.twin_send, self.twin_recv, origin, cut, first)

    def to_right(self, origin, cut, first=False):
        return self.move(line_place()[0] + 2, self.right, self.line, origin, cut, first)

    def to_left(self, origin, cut, first=False):
        return self.move(line_place()[0] - 2, self.left, self.line, origin, cut, first)

    def stay(self):
        return pltpu.make_async_copy(self.own, self.out.at[line_place()[0]], self.keep)

    def start(self):
        _, place, _ = line_place()
        for cut in range(self.cuts):
            @pl.when(place < self.pairs - 1)
            def _():
                self.to_right(place, cut, True).start()

            @pl.when(place > 0)
            def _():
                self.to_left(place, cut, True).start()

        for cut in range(self.cuts):
            self.to_twin(place, cut, True).start()
        self.stay().start()

    def step(self, step, cut):
        _, place, _ = line_place()

        @pl.when(place >= step)
        def _():
            origin = place - step
            self.to_right(origin, cut).wait_recv()

            @pl.when(place < self.pairs - 1)
            def _():
                self.to_right(origin, cut).start()

            self.to_twin(origin, cut).start()

        @pl.when(place + step <= self.pairs - 1)
        def _():
            origin = place + step
            self.to_left(origin, cut).wait_recv()

            @pl.when(place > 0)
            def _():
                self.to_left(origin, cut).start()

            self.to_twin(origin, cut).start()

    def twin_arrive(self, origin):
        me, _, side = line_place()
        for cut in range(self.cuts):
            other = self.piece(self.out.at[origin * 2 + 1 - side], cut)
            remote(
                other,
                other,
                self.twin_send.at[origin, cut],
                self.twin_recv.at[origin, cut],
                {"row": me + 1 - 2 * side},
            ).wait_recv()

    def finish(self):
        self.stay().wait()
        for origin in range(self.pairs):
            self.twin_arrive(origin)
        self.leave()

    def leave(self):
        _, place, _ = line_place()
        for origin in range(self.pairs):
            for cut in range(self.cuts):
                self.to_twin(origin, cut).wait_send()

                @pl.when((place < self.pairs - 1) & (origin <= place))
                def _():
                    self.to_right(origin, cut).wait_send()

                @pl.when((place > 0) & (origin >= place))
                def _():
                    self.to_left(origin, cut).wait_send()


def gather_sems(pairs, cuts):
    return [DMA((pairs, cuts))] * 5 + [DMA]


class Scatter:
    def __init__(self, pairs, cuts, part, buffers, sems):
        self.pairs, self.cuts, self.part = pairs, cuts, part
        self.own, self.twin, self.from_left, self.from_right, self.out_right, self.out_left = buffers
        (
            self.right_send,
            self.left_send,
            self.twin_send,
            self.right_recv,
            self.left_recv,
            self.twin_recv,
            self.loaded,
        ) = sems
        self.height = part.shape[1] // cuts
        self.ready = set()

    def piece(self, ref, dest, cut):
        return ref.at[dest, pl.ds(cut * self.height, self.height)]

    def value(self, ref, dest, cut):
        return ref[dest, pl.ds(cut * self.height, self.height)].astype(FULL)

    def load(self, dest, cut):
        _, _, side = line_place()
        return pltpu.make_async_copy(
            self.piece(self.part, dest * 2 + side, cut),
            self.piece(self.own, dest, cut),
            self.loaded.at[dest, cut],
        )

    def to_twin(self, dest, cut):
        me, _, side = line_place()
        return remote(
            self.piece(self.part, dest * 2 + 1 - side, cut),
            self.piece(self.twin, dest, cut),
            self.twin_send.at[dest, cut],
            self.twin_recv.at[dest, cut],
            {"row": me + 1 - 2 * side},
        )

    def to_right(self, dest, cut):
        return remote(
            self.piece(self.out_right, dest, cut),
            self.piece(self.from_left, dest, cut),
            self.right_send.at[dest, cut],
            self.right_recv.at[dest, cut],
            {"row": line_place()[0] + 2},
        )

    def to_left(self, dest, cut):
        return remote(
            self.piece(self.out_left, dest, cut),
            self.piece(self.from_right, dest, cut),
            self.left_send.at[dest, cut],
            self.left_recv.at[dest, cut],
            {"row": line_place()[0] - 2},
        )

    def start(self):
        order = []
        for step in range(self.pairs):
            for dest in (self.pairs - 1 - step, step):
                if dest not in order:
                    order.append(dest)
        for dest in order:
            for cut in range(self.cuts):
                self.to_twin(dest, cut).start()
                self.load(dest, cut).start()

    def here(self, dest, cut):
        return self.value(self.own, dest, cut) + self.value(self.twin, dest, cut)

    def step(self, step, cut):
        _, place, _ = line_place()
        last = self.pairs - 1
        span = pl.ds(cut * self.height, self.height)
        for dest, sending, first, out, arrived, copy in (
            (last - step, place < last - step, place == 0, self.out_right, self.from_left, self.to_right),
            (step, place > step, place == last, self.out_left, self.from_right, self.to_left),
        ):
            if (dest, cut) not in self.ready:
                self.ready.add((dest, cut))
                self.to_twin(dest, cut).wait_recv()
                self.load(dest, cut).wait()

            @pl.when(sending & first)
            def _():
                out[dest, span] = self.here(dest, cut).astype(out.dtype)
                copy(dest, cut).start()

            @pl.when(sending & jnp.logical_not(first))
            def _():
                copy(dest, cut).wait_recv()
                out[dest, span] = (self.here(dest, cut) + self.value(arrived, dest, cut)).astype(out.dtype)
                copy(dest, cut).start()

    def finish(self, total):
        _, place, _ = line_place()
        last = self.pairs - 1
        for cut in range(self.cuts):
            span = pl.ds(cut * self.height, self.height)
            total[span] = self.here(place, cut)

            @pl.when(place > 0)
            def _():
                self.to_right(place, cut).wait_recv()
                total[span] += self.value(self.from_left, place, cut)

            @pl.when(place < last)
            def _():
                self.to_left(place, cut).wait_recv()
                total[span] += self.value(self.from_right, place, cut)

        for dest in range(self.pairs):
            for cut in range(self.cuts):
                self.to_twin(dest, cut).wait_send()

                @pl.when(place < dest)
                def _():
                    self.to_right(dest, cut).wait_send()

                @pl.when(place > dest)
                def _():
                    self.to_left(dest, cut).wait_send()


def scatter_buffers(pairs, rows, width):
    return [pltpu.VMEM((pairs, rows, width), LOW)] * 6


def scatter_sems(pairs, cuts):
    return [DMA((pairs, cuts))] * 7


class PlaneScatter:
    def __init__(self, block_of, out, buffers, sems):
        self.block_of, self.out = block_of, out
        self.arrived, self.mine, self.onward, self.final = buffers
        self.send, self.recv, self.loaded, self.send_on, self.recv_on = sems
        self.height = out.shape[0] // 2

    def places(self, half, index):
        d, c = lax.axis_index("dp"), lax.axis_index("col")
        if half == 0:
            there = 1 - c if index == 0 else c
            return {"dp": 1 - d}, self.block_of(there, 1 - d, 0), self.block_of(there, d, 0)
        there = 1 - d if index == 0 else d
        return {"col": 1 - c}, self.block_of(1 - c, there, 1), self.block_of(c, there, 1)

    def move(self, half, index):
        device, block, _ = self.places(half, index)
        return remote(
            block, self.arrived.at[half, index], self.send.at[half, index], self.recv.at[half, index], device
        )

    def load(self, half, index):
        _, _, block = self.places(half, index)
        return pltpu.make_async_copy(block, self.mine.at[half, index], self.loaded.at[half, index])

    def move_on(self, half):
        device = (
            {"col": 1 - lax.axis_index("col")} if half == 0 else {"dp": 1 - lax.axis_index("dp")}
        )
        return remote(
            self.onward.at[half], self.final.at[half], self.send_on.at[half], self.recv_on.at[half], device
        )

    def start(self):
        for index in range(2):
            for half in range(2):
                self.move(half, index).start()
                self.load(half, index).start()

    def sum_of(self, half, index):
        self.move(half, index).wait_recv()
        self.load(half, index).wait()
        return self.mine[half, index].astype(FULL) + self.arrived[half, index].astype(FULL)

    def forward(self):
        for half in range(2):
            self.onward[half] = self.sum_of(half, 0).astype(LOW)
            self.move_on(half).start()

    def finish(self):
        for half in range(2):
            total = self.sum_of(half, 1)
            self.move_on(half).wait_recv()
            self.out[pl.ds(half * self.height, self.height)] = total + self.final[half].astype(FULL)
        for half in range(2):
            for index in range(2):
                self.move(half, index).wait_send()
            self.move_on(half).wait_send()


def by_rows(part, height):
    half_height = height // 2
    return lambda c, d, half: part.at[pl.ds((c * 2 + d) * height + half * half_height, half_height)]


def by_tiles(part, height, width):
    half_height = height // 2
    return lambda c, d, half: part.at[
        pl.ds(d * height + half * half_height, half_height), pl.ds(pl.multiple_of(c * width, width), width)
    ]


def plane_scratch(rows, width):
    half = (rows // 2, width)
    return [
        pltpu.VMEM((2, 2) + half, LOW),
        pltpu.VMEM((2, 2) + half, LOW),
        pltpu.VMEM((2,) + half, LOW),
        pltpu.VMEM((2,) + half, LOW),
        DMA((2, 2)),
        DMA((2, 2)),
        DMA((2, 2)),
        DMA((2,)),
        DMA((2,)),
    ]


CUTS = 2


def call_remote(kernel, collective, **options):
    return pl.pallas_call(
        kernel,
        compiler_params=pltpu.CompilerParams(
            collective_id=collective, has_side_effects=True, vmem_limit_bytes=ROOM
        ),
        **options,
    )


def enter_kernel(plane, pairs, h_home, mix_home, back_home, gy_home, rows_out, h, mix, back, gy, own, *sems):
    plane_sems, line_sems = sems[:3], sems[3:]
    greet(pairs, plane)
    first = to_work(plane, h_home, h, plane_sems, 0)
    others = [
        to_work(plane, home, work, plane_sems, index)
        for index, (home, work) in enumerate(((mix_home, mix), (back_home, back), (gy_home, gy)), 1)
    ]
    first.start()
    first.arrive()
    for other in others:
        other.start()
    own[...] = norm_forward(h[...])[0].astype(LOW)
    gather = Gather(pairs, CUTS, own, rows_out, line_sems)
    gather.start()
    for step in range(1, pairs):
        for cut in range(CUTS):
            gather.step(step, cut)
    gather.finish()
    for other in others:
        other.arrive()
        other.leave()
    first.leave()


def enter(plane, pairs, h_home, mix_home, back_home, gy_home, collective):
    n_dp, n_col, slot, width = h_home.shape
    rows = n_dp * slot
    work = jax.ShapeDtypeStruct((rows, n_col * width), FULL)
    outs = call_remote(
        functools.partial(enter_kernel, plane, pairs),
        collective,
        in_specs=[ANY] * 4,
        out_specs=[ANY, VMEM, ANY, ANY, ANY],
        out_shape=[
            jax.ShapeDtypeStruct((2 * pairs, rows, n_col * width), LOW),
            work,
            work,
            work,
            jax.ShapeDtypeStruct(work.shape, gy_home.dtype),
        ],
        scratch_shapes=[pltpu.VMEM(work.shape, LOW)] + exchange_sems(plane, 4) + gather_sems(pairs, CUTS),
    )(h_home, mix_home, back_home, gy_home)
    return [outs[0].reshape(2 * pairs * rows, n_col * width)] + list(outs[1:])


def duplex_kernel(pairs, plane, count, part, gathered, *rest):
    grads, rest = rest[:count], rest[count:]
    (rows_out, low_out), rest = rest[:2], rest[2:]
    sums, rest = rest[:count], rest[count:]
    total, scratch, rest = rest[0], rest[1:], rest[20:]
    scatter = Scatter(pairs, CUTS, part, scratch[:6], scratch[6:13])
    gather = Gather(pairs, CUTS, gathered, rows_out, scratch[13:19])
    planes = plane_sums(grads, sums, rest)
    greet(pairs, plane if count else None)
    scatter.start()
    gather.start()
    for one in planes:
        one.start()
    for step in range(pairs - 1):
        for cut in range(CUTS):
            scatter.step(step, cut)
            gather.step(step + 1, cut)
        if 0 < step <= len(planes):
            planes[step - 1].forward()
    scatter.finish(total)
    low_out[...] = total[...].astype(LOW)
    gather.finish()
    for one in planes:
        one.finish()


def plane_sums(grads, sums, scratch):
    planes = []
    for index, (grad, total) in enumerate(zip(grads, sums)):
        rows, width = total.shape
        block_of = by_rows(grad, rows) if grad.shape[1] == width else by_tiles(grad, rows, width)
        planes.append(
            PlaneScatter(
                block_of, total, scratch[9 * index : 9 * index + 4], scratch[9 * index + 4 : 9 * index + 9]
            )
        )
    return planes


def owned_shape(grad):
    rows, width = grad.shape
    return (rows // 4, width) if rows == D else (rows // 2, width // 2)


def duplex(pairs, plane, partial, gathered, grads, collective):
    rows, width = gathered.shape
    whole = jax.ShapeDtypeStruct((2 * pairs, rows, width), LOW)
    owned = [owned_shape(grad) for grad in grads]
    outs = call_remote(
        functools.partial(duplex_kernel, pairs, plane, len(grads)),
        collective,
        in_specs=[ANY] * (2 + len(grads)),
        out_specs=[ANY] + [VMEM] * (2 + len(grads)),
        out_shape=[whole, jax.ShapeDtypeStruct((rows, width), LOW)]
        + [jax.ShapeDtypeStruct(shape, FULL) for shape in owned]
        + [jax.ShapeDtypeStruct((rows, width), FULL)],
        scratch_shapes=scatter_buffers(pairs, rows, width)
        + scatter_sems(pairs, CUTS)
        + gather_sems(pairs, CUTS)
        + sum([plane_scratch(*shape) for shape in owned], []),
    )(partial.reshape(whole.shape), gathered, *grads)
    return outs[0].reshape(2 * pairs * rows, width), outs[1], outs[-1], outs[2:-1]


def arrival(place, pairs, step):
    chosen = jnp.int32(0)
    for here in range(pairs):
        order = sorted(range(pairs), key=lambda there: abs(there - here))
        chosen = jnp.where(place == here, order[step], chosen)
    return chosen


UNIT = 256


def ffn_kernel(
    pairs, hyper, mix, branch, back, w_in, w_out, gy_rows,
    rows_out, hid_out, units_out, y_out, h, gh_out, gy_out,
    own, x, wd, gy, hid, units, y, part, twin, from_left, from_right, total, upstream,
    load_sem, gy_sem, hid_sem, units_sem, y_sem, x_sem,
    twin_send, twin_recv, right_send, right_recv, left_send, left_recv, *line_sems,
):
    me, place, side = line_place()
    last = pairs - 1
    rows = own.shape[0]
    height = rows // CUTS
    n_col, n_dp, owned, width = w_out.shape
    half = units.shape[2] // 2
    greet(pairs)
    loads = [
        pltpu.make_async_copy(mix, h, load_sem.at[0]),
        pltpu.make_async_copy(branch, total, load_sem.at[1]),
        pltpu.make_async_copy(back, upstream, load_sem.at[2]),
    ]
    for load in loads:
        load.start()
    tiles = [
        pltpu.make_async_copy(
            w_out.at[c, d],
            wd.at[pl.ds(d * owned, owned), pl.ds(c * width, width)],
            load_sem.at[3 + c * n_dp + d],
        )
        for c in range(n_col)
        for d in range(n_dp)
    ]
    for tile in tiles:
        tile.start()
    order = [arrival(place, pairs, step) for step in range(pairs)]

    def load_gy(step):
        return pltpu.make_async_copy(gy_rows.at[order[step]], gy.at[step % 2], gy_sem.at[step % 2])

    load_gy(0).start()
    loads[0].wait()
    loads[1].wait()
    h[...] = h[...] + branch_weight(hyper) * total[...]
    own[...] = norm_forward(h[...])[0].astype(LOW)
    gather = Gather(pairs, CUTS, own, x, line_sems)
    gather.start()
    for tile in tiles:
        tile.wait()

    def saves(step):
        slot = step % 2
        return [
            pltpu.make_async_copy(hid.at[slot], hid_out.at[order[step]], hid_sem.at[slot]),
            pltpu.make_async_copy(units.at[slot], units_out.at[order[step]], units_sem.at[slot]),
            pltpu.make_async_copy(y.at[slot], y_out.at[order[step]], y_sem.at[slot]),
        ]

    def save_x(step):
        return pltpu.make_async_copy(
            x.at[pl.ds(order[step] * 2, 2)], rows_out.at[pl.ds(order[step] * 2, 2)], x_sem.at[step]
        )

    def work(step):
        slot = step % 2
        x_block = x.at[pl.ds(order[step] * 2, 2)]

        @pl.loop(0, half // UNIT)
        def _(unit):
            at = pl.multiple_of(unit * UNIT, UNIT)
            rows_in = x_block[...].reshape(2 * rows, -1)
            gate = jnp.dot(rows_in, w_in[:, pl.ds(at, UNIT)], preferred_element_type=FULL)
            up = jnp.dot(rows_in, w_in[:, pl.ds(half + at, UNIT)], preferred_element_type=FULL)
            grad = dot_last(gy[slot], wd[pl.ds(at, UNIT)])
            sigma = 1.0 / (1.0 + jnp.exp(-gate))
            silu = gate * sigma
            hid[slot, :, pl.ds(at, UNIT)] = (silu * up).astype(LOW)
            units[slot, :, pl.ds(at, UNIT)] = (
                grad * up * sigma * (1.0 + gate * (1.0 - sigma))
            ).astype(LOW)
            units[slot, :, pl.ds(half + at, UNIT)] = (grad * silu).astype(LOW)

        @pl.loop(0, D // UNIT)
        def _(unit):
            at = pl.multiple_of(unit * UNIT, UNIT)
            y_tile = jnp.dot(hid[slot], wd[:, pl.ds(at, UNIT)], preferred_element_type=FULL)
            y[slot, :, pl.ds(at, UNIT)] = y_tile.astype(LOW)
            tile = dot_last(units[slot], w_in[pl.ds(at, UNIT)]).astype(LOW)
            part[pl.ds(order[step] * 2, 2), :, pl.ds(at, UNIT)] = tile.reshape(2, rows, UNIT)

    def to_twin(dest):
        return remote(
            part.at[dest * 2 + 1 - side],
            twin.at[dest],
            twin_send.at[dest],
            twin_recv.at[dest],
            {"row": me + 1 - 2 * side},
        )

    def line(dest, cut, rightward):
        span = pl.ds(cut * height, height)
        return remote(
            part.at[dest * 2 + side, span],
            (from_left if rightward else from_right).at[dest, span],
            (right_send if rightward else left_send).at[dest, cut],
            (right_recv if rightward else left_recv).at[dest, cut],
            {"row": me + 2 if rightward else me - 2},
        )

    def here(dest, span):
        return part[dest * 2 + side, span].astype(FULL) + twin[dest, span].astype(FULL)

    def send_first(step):
        dest = order[step]
        to_twin(dest).wait_recv()
        for at_end, rightward in ((place == 0, True), (place == last, False)):
            @pl.when(at_end & (dest != place))
            def _():
                for cut in range(CUTS):
                    span = pl.ds(cut * height, height)
                    part[dest * 2 + side, span] = here(dest, span).astype(LOW)
                    line(dest, cut, rightward).start()

    for step in range(pairs):
        if step > 0:
            for cut in range(CUTS):
                gather.step(step, cut)
        else:
            gather.stay().wait()
        if step + 1 < pairs:
            load_gy(step + 1).start()
        gather.twin_arrive(order[step])
        save_x(step).start()
        load_gy(step).wait()
        if step >= 2:
            for save in saves(step - 2):
                save.wait()
        work(step)
        to_twin(order[step]).start()
        for save in saves(step):
            save.start()
        if step > 0:
            send_first(step - 1)
    send_first(pairs - 1)

    def pass_on(dest, rightward):
        arrived = from_left if rightward else from_right
        for cut in range(CUTS):
            span = pl.ds(cut * height, height)
            line(dest, cut, rightward).wait_recv()
            part[dest * 2 + side, span] = (here(dest, span) + arrived[dest, span].astype(FULL)).astype(LOW)
            line(dest, cut, rightward).start()

    for reach in range(2, pairs):
        rightward, leftward = (place > 0) & (place < reach), (place < last) & (place > last - reach)
        pl.when(rightward & (place < pairs // 2))(functools.partial(pass_on, reach, True))
        pl.when(leftward)(functools.partial(pass_on, last - reach, False))
        pl.when(rightward & (place >= pairs // 2))(functools.partial(pass_on, reach, True))

    for cut in range(CUTS):
        span = pl.ds(cut * height, height)
        total[span] = here(place, span)

        @pl.when(place > 0)
        def _():
            line(place, cut, True).wait_recv()
            total[span] += from_left[place, span].astype(FULL)

        @pl.when(place < last)
        def _():
            line(place, cut, False).wait_recv()
            total[span] += from_right[place, span].astype(FULL)

    loads[2].wait()
    grad = norm_backward(total[...], h[...])
    gh_out[...] = grad.astype(LOW)
    gy_out[...] = (upstream[...] + branch_weight(hyper) * grad).astype(LOW)

    gather.leave()
    for step in range(pairs):
        save_x(step).wait()
    for step in range(pairs - 2, pairs):
        for save in saves(step):
            save.wait()
    for dest in range(pairs):
        to_twin(dest).wait_send()
        for cut in range(CUTS):
            @pl.when(place < dest)
            def _():
                line(dest, cut, True).wait_send()

            @pl.when(place > dest)
            def _():
                line(dest, cut, False).wait_send()


def feed_forward(pairs, hyper, mix, branch, back, w_in, w_out, gy_rows, collective):
    rows, width = mix.shape
    units = w_in.shape[1]
    half = units // 2
    n_col, n_dp = w_out.shape[:2]
    low = jax.ShapeDtypeStruct((rows, width), LOW)

    def by_pair(last_width):
        return jax.ShapeDtypeStruct((pairs, 2 * rows, last_width), LOW)

    blocks = pltpu.VMEM((pairs, rows, width), LOW)
    full = pltpu.VMEM((rows, width), FULL)
    outs = call_remote(
        functools.partial(ffn_kernel, pairs),
        collective,
        in_specs=[SMEM, ANY, ANY, ANY, VMEM, ANY, ANY],
        out_specs=[ANY, ANY, ANY, ANY, VMEM, VMEM, VMEM],
        out_shape=[
            jax.ShapeDtypeStruct((2 * pairs, rows, width), LOW),
            by_pair(half),
            by_pair(units),
            by_pair(width),
            jax.ShapeDtypeStruct((rows, width), FULL),
            low,
            low,
        ],
        scratch_shapes=[
            pltpu.VMEM((rows, width), LOW),
            pltpu.VMEM((2 * pairs, rows, width), LOW),
            pltpu.VMEM((half, width), LOW),
            pltpu.VMEM((2, 2 * rows, width), LOW),
            pltpu.VMEM((2, 2 * rows, half), LOW),
            pltpu.VMEM((2, 2 * rows, units), LOW),
            pltpu.VMEM((2, 2 * rows, width), LOW),
            pltpu.VMEM((2 * pairs, rows, width), LOW),
            blocks,
            blocks,
            blocks,
            full,
            full,
            DMA((3 + n_col * n_dp,)),
            DMA((2,)),
            DMA((2,)),
            DMA((2,)),
            DMA((2,)),
            DMA((pairs,)),
            DMA((pairs,)),
            DMA((pairs,)),
        ]
        + [DMA((pairs, CUTS))] * 4
        + gather_sems(pairs, CUTS),
    )(hyper, mix, branch, back, w_in, w_out, gy_rows.reshape(pairs, 2 * rows, width))
    tokens = 2 * pairs * rows
    return [value.reshape(tokens, -1) for value in outs[:4]] + list(outs[5:])


def leave_kernel(plane, pairs, count, part, h, y_att, y_ffn, gh_ffn, *rest):
    grads, rest = rest[:count], rest[count:]
    homes, sums, rest = rest[:4], rest[4 : 4 + count], rest[4 + count :]
    (total, last), plane_sems, scratch, rest = rest[:2], rest[2:5], rest[5:18], rest[18:]
    scatter = Scatter(pairs, CUTS, part, scratch[:6], scratch[6:])
    planes = plane_sums(grads, sums, rest)
    greet(pairs, plane)
    scatter.start()
    for one in planes:
        one.start()
    ways = [
        to_home(plane, work, home, plane_sems, index)
        for index, (work, home) in enumerate(zip((y_att, y_ffn, gh_ffn, last), homes))
    ]
    for way in ways[:3]:
        way.start()
    for step in range(pairs - 1):
        for cut in range(CUTS):
            scatter.step(step, cut)
        if 0 < step <= len(planes):
            planes[step - 1].forward()
    scatter.finish(total)
    last[...] = norm_backward(total[...], h[...]).astype(last.dtype)
    ways[3].start()
    for one in planes:
        one.finish()
    for way in ways:
        way.arrive()
        way.leave()


def leave(plane, pairs, partial, h, works, grads, collective):
    rows, width = h.shape
    n_dp, n_col = plane
    home = jax.ShapeDtypeStruct((n_dp, n_col, rows // n_dp, width // n_col), works[0].dtype)
    owned = [owned_shape(grad) for grad in grads]
    outs = call_remote(
        functools.partial(leave_kernel, plane, pairs, len(grads)),
        collective,
        in_specs=[ANY, VMEM, ANY, ANY, ANY] + [ANY] * len(grads),
        out_specs=[ANY] * 4 + [VMEM] * len(grads),
        out_shape=[home] * 4 + [jax.ShapeDtypeStruct(shape, FULL) for shape in owned],
        scratch_shapes=[pltpu.VMEM((rows, width), FULL), pltpu.VMEM((rows, width), works[0].dtype)]
        + exchange_sems(plane, 4)
        + scatter_buffers(pairs, rows, width)
        + scatter_sems(pairs, CUTS)
        + sum([plane_scratch(*shape) for shape in owned], []),
    )(partial.reshape(2 * pairs, rows, width), h, *works, *grads)
    return outs[:4], outs[4:]


def total_kernel(plane, count, own, out, line, flat, line_send, line_recv, flat_send, flat_recv):
    n_dp, n_col = plane
    me = lax.axis_index("row")
    here = lax.axis_index("dp") * n_col + lax.axis_index("col")
    barrier = pltpu.get_barrier_semaphore()
    rows = [(me + step) % count for step in range(1, count)]
    for row in rows:
        pl.semaphore_signal(barrier, inc=1, device_id={"row": row}, device_id_type=pl.DeviceIdType.MESH)
    for offset in offsets(plane):
        pl.semaphore_signal(
            barrier, inc=1, device_id=peer(plane, offset), device_id_type=pl.DeviceIdType.MESH
        )
    pl.semaphore_wait(barrier, count - 1 + n_dp * n_col - 1)
    line[me] = own[...]
    copies = [
        remote(line.at[me], line.at[me], line_send.at[step], line_recv.at[step], {"row": row})
        for step, row in enumerate(rows)
    ]
    for copy in copies:
        copy.start()
    for copy in copies:
        copy.wait()
    sums = line[0]
    for row in range(1, count):
        sums = sums + line[row]
    flat[here] = sums
    copies = [
        remote(
            flat.at[here],
            flat.at[here],
            flat_send.at[offset[0], offset[1]],
            flat_recv.at[offset[0], offset[1]],
            peer(plane, offset),
        )
        for offset in offsets(plane)
    ]
    for copy in copies:
        copy.start()
    for copy in copies:
        copy.wait()
    sums = flat[0]
    for index in range(1, n_dp * n_col):
        sums = sums + flat[index]
    out[...] = sums


def sum_everywhere(plane, values_in, collective):
    count = lax.axis_size("row")
    shape = values_in.shape
    return call_remote(
        functools.partial(total_kernel, plane, count),
        collective,
        in_specs=[VMEM],
        out_specs=VMEM,
        out_shape=jax.ShapeDtypeStruct(shape, FULL),
        scratch_shapes=[
            pltpu.VMEM((count,) + shape, FULL),
            pltpu.VMEM((plane[0] * plane[1],) + shape, FULL),
            DMA((count - 1,)),
            DMA((count - 1,)),
            DMA(plane),
            DMA(plane),
        ],
    )(values_in)


def mat(left, right):
    return jnp.sum(left[:, :, None] * right[None, :, :], axis=1)


def gather_blocks(weight_low):
    return lax.all_gather(weight_low, ("col", "dp"), axis=0, tiled=True)


def scatter_blocks(grad_low):
    return lax.psum_scatter(grad_low, ("col", "dp"), scatter_dimension=0, tiled=True).astype(FULL)


def side_by_side(weight):
    return jnp.concatenate([weight[index] for index in range(weight.shape[0])], axis=1)


def apart(weight, count):
    width = weight.shape[1] // count
    return jnp.stack([weight[:, index * width : (index + 1) * width] for index in range(count)])


def whole_out(weight_low, n_dp, n_col):
    rows, width = weight_low.shape
    blocks = gather_blocks(weight_low).reshape(n_col, n_dp, rows, width)
    return blocks.transpose(1, 2, 0, 3).reshape(n_dp * rows, n_col * width)


def own_out(grad, n_dp, n_col):
    rows, width = grad.shape[0] // n_dp, grad.shape[1] // n_col
    blocks = grad.astype(LOW).reshape(n_dp, rows, n_col, width).transpose(2, 0, 1, 3)
    return scatter_blocks(blocks.reshape(n_col * n_dp * rows, width))


def adam_update(weight, grad_sum, moment_one, moment_two, clip_factor, step_value):
    clipped = grad_sum * clip_factor
    new_one = beta_first * moment_one + (1.0 - beta_first) * clipped
    new_two = beta_second * moment_two + (1.0 - beta_second) * clipped * clipped
    fix_one = 1.0 - jnp.power(beta_first, step_value)
    fix_two = 1.0 - jnp.power(beta_second, step_value)
    new_weight = weight - learning_rate * (
        new_one / fix_one / (jnp.sqrt(new_two / fix_two) + adam_eps) + weight_decay * weight
    )
    return (new_weight, new_one, new_two)


def body(
    streams,
    cotangent,
    destination,
    segments,
    attention_in,
    feedforward_in,
    attention_out,
    feedforward_out,
    attention_in_moment,
    feedforward_in_moment,
    attention_out_moment,
    feedforward_out_moment,
    attention_in_second,
    feedforward_in_second,
    attention_out_second,
    feedforward_out_second,
    hyper_weights,
    hyper_moment,
    hyper_second,
    step_count,
):
    n_dp, n_col, count = lax.axis_size("dp"), lax.axis_size("col"), lax.axis_size("row")
    plane, pairs = (n_dp, n_col), count // 2
    rows = destination.shape[1]
    group_tokens = segments.shape[2]
    slot = rows // n_dp
    travel = LOW if slot % 16 == 0 else FULL
    attention_in_low = gather_blocks(side_by_side(attention_in).astype(LOW))
    attention_out_low = whole_out(attention_out.astype(LOW), n_dp, n_col)
    feedforward_in_low = gather_blocks(side_by_side(feedforward_in).astype(LOW))
    feedforward_out_low = gather_blocks(feedforward_out.astype(LOW)).reshape(
        n_col, n_dp, *feedforward_out.shape
    )

    group = destination // group_tokens
    sent = (
        group * slot
        + (destination - group * group_tokens)
        - lax.axis_index("row") * rows
        - lax.axis_index("dp") * slot
    )
    hyper = hyper_weights.reshape(-1)
    h_home, mix_home, back_home, gy_home, gram = prepare(
        hyper, streams, cotangent, sent, n_dp, travel
    )
    segment = lax.dynamic_index_in_dim(segments[:, 0], lax.axis_index("col"), 0, keepdims=False)
    cosine, sine, start = rotary_tables(segment)

    rows_att, hidden_att, mix_work, back_work, gy_work = enter(
        plane, pairs, h_home, mix_home, back_home, gy_home, 1
    )
    qkv = jnp.dot(rows_att, attention_in_low, preferred_element_type=FULL)
    heads_low, log_totals, query_low, key_low, value_low = attend_forward(qkv, cosine, sine, start)
    partial_att = jnp.dot(heads_low, attention_out_low, preferred_element_type=FULL).astype(LOW)
    grad_rows_ffn, branch_low, branch_att, _ = duplex(
        pairs, plane, partial_att, gy_work.astype(LOW), [], 2
    )
    rows_ffn, hidden_low, grad_units, partial_ffn, grad_hidden_ffn, grad_branch = feed_forward(
        pairs,
        hyper,
        mix_work,
        branch_att,
        back_work,
        feedforward_in_low,
        feedforward_out_low,
        grad_rows_ffn,
        3,
    )
    in_kernel = plane == (2, 2)
    grads_ffn = [
        jnp.einsum("td,tu->du", rows_ffn, grad_units, preferred_element_type=FULL).astype(LOW),
        jnp.einsum("tu,td->ud", hidden_low, grad_rows_ffn, preferred_element_type=FULL).astype(LOW),
    ]
    grad_rows_att, branch_ffn, _, sums_ffn = duplex(
        pairs, plane, partial_ffn, grad_branch, grads_ffn if in_kernel else [], 5
    )

    grad_heads = jnp.einsum(
        "td,ud->tu", grad_rows_att, attention_out_low, preferred_element_type=FULL
    ).astype(LOW)
    grad_units_att = jnp.concatenate(
        attend_backward(grad_heads, query_low, key_low, value_low, log_totals, cosine, sine, start),
        axis=1,
    )
    grads_att = [
        jnp.einsum("td,tu->du", rows_att, grad_units_att, preferred_element_type=FULL).astype(LOW),
        jnp.einsum("tu,td->ud", heads_low, grad_rows_att, preferred_element_type=FULL).astype(LOW),
    ]
    partial_grad = jnp.einsum(
        "tu,du->td", grad_units_att, attention_in_low, preferred_element_type=FULL
    ).astype(LOW)
    homes, sums_att = leave(
        plane,
        pairs,
        partial_grad,
        hidden_att,
        [value.astype(travel) for value in (branch_low, branch_ffn, grad_hidden_ffn)],
        grads_att if in_kernel else [],
        6,
    )
    if not in_kernel:
        sums_ffn, sums_att = (
            [scatter_blocks(grads[0]), own_out(grads[1], n_dp, n_col)] for grads in (grads_ffn, grads_att)
        )
    shard_feedforward_in, shard_feedforward_out = apart(sums_ffn[0], 2), sums_ffn[1]
    shard_attention_in, shard_attention_out = apart(sums_att[0], 3), sums_att[1]
    streams_out, stream_grad, dots = finish(hyper, streams, cotangent, sent, homes)
    square = (
        jnp.sum(shard_attention_in * shard_attention_in)
        + jnp.sum(shard_feedforward_in * shard_feedforward_in)
        + jnp.sum(shard_attention_out * shard_attention_out)
        + jnp.sum(shard_feedforward_out * shard_feedforward_out)
    )
    dots = jnp.concatenate([jnp.sum(gram, axis=(1, 2)), jnp.sum(dots, axis=(1, 2)), square[None]])
    totals = sum_everywhere(plane, jnp.pad(dots, (0, 128 - dots.shape[0])).reshape(1, 128), 7)[0]
    a0, m0, c0 = hyper_weights[0, :, 0], hyper_weights[0, :, 1:5], hyper_weights[0, :, 5]
    a1, m1, c1 = hyper_weights[1, :, 0], hyper_weights[1, :, 1:5], hyper_weights[1, :, 5]
    gram = totals[:16].reshape(STREAMS, STREAMS)
    att_cot, ffn_cot = totals[16:20], totals[20:24]
    streams_ffn, streams_att = totals[24:28], totals[28:32]
    att_ffn, square_total = totals[32], totals[33]
    grad_m1 = mat(m0.T, gram) + c0[:, None] * att_cot[None, :]
    grad_a1 = jnp.sum(m0 * streams_ffn[:, None], axis=0) + c0 * att_ffn
    grad_m0 = mat(gram, m1.T) + streams_ffn[:, None] * a1[None, :]
    grad_c0 = jnp.sum(m1 * att_cot[None, :], axis=1) + a1 * att_ffn
    hyper_grad = jnp.stack(
        [
            jnp.concatenate([streams_att[:, None], grad_m0, grad_c0[:, None]], axis=1),
            jnp.concatenate([grad_a1[:, None], grad_m1, ffn_cot[:, None]], axis=1),
        ]
    )
    grad_norm = jnp.sqrt(square_total + jnp.sum(hyper_grad * hyper_grad))
    clip_factor = 1.0 / jnp.maximum(grad_norm, 1.0)
    step_value = step_count[0].astype(jnp.float32)
    attention_in_new = adam_update(
        attention_in,
        shard_attention_in,
        attention_in_moment,
        attention_in_second,
        clip_factor,
        step_value,
    )
    feedforward_in_new = adam_update(
        feedforward_in,
        shard_feedforward_in,
        feedforward_in_moment,
        feedforward_in_second,
        clip_factor,
        step_value,
    )
    attention_out_new = adam_update(
        attention_out,
        shard_attention_out,
        attention_out_moment,
        attention_out_second,
        clip_factor,
        step_value,
    )
    feedforward_out_new = adam_update(
        feedforward_out,
        shard_feedforward_out,
        feedforward_out_moment,
        feedforward_out_second,
        clip_factor,
        step_value,
    )
    hyper_new = adam_update(
        hyper_weights, hyper_grad, hyper_moment, hyper_second, clip_factor, step_value
    )
    return (
        streams_out,
        stream_grad,
        grad_norm.reshape(1),
        shard_attention_in,
        shard_feedforward_in,
        shard_attention_out,
        shard_feedforward_out,
        hyper_grad,
        attention_in_new[0],
        feedforward_in_new[0],
        attention_out_new[0],
        feedforward_out_new[0],
        hyper_new[0],
        attention_in_new[1],
        feedforward_in_new[1],
        attention_out_new[1],
        feedforward_out_new[1],
        hyper_new[1],
        attention_in_new[2],
        feedforward_in_new[2],
        attention_out_new[2],
        feedforward_out_new[2],
        hyper_new[2],
    )


def solution(mesh):
    placed = (
        P(None, None, ("dp", "row"), "col"),
        P(None, None, ("dp", "row"), "col"),
        P(None, ("dp", "row")),
        P(None, "dp", None),
        P(None, ("col", "dp"), "row"),
        P(None, ("col", "dp"), "row"),
        P(("row", "dp"), "col"),
        P(("row", "dp"), "col"),
        P(None, ("col", "dp"), "row"),
        P(None, ("col", "dp"), "row"),
        P(("row", "dp"), "col"),
        P(("row", "dp"), "col"),
        P(None, ("col", "dp"), "row"),
        P(None, ("col", "dp"), "row"),
        P(("row", "dp"), "col"),
        P(("row", "dp"), "col"),
        P(),
        P(),
        P(),
        P(),
    )
    return jax.shard_map(
        body,
        mesh=mesh,
        in_specs=placed,
        out_specs=(
            P(None, None, ("dp", "row"), "col"),
            P(None, None, ("dp", "row"), "col"),
            P(),
            P(None, ("col", "dp"), "row"),
            P(None, ("col", "dp"), "row"),
            P(("row", "dp"), "col"),
            P(("row", "dp"), "col"),
            P(),
            P(None, ("col", "dp"), "row"),
            P(None, ("col", "dp"), "row"),
            P(("row", "dp"), "col"),
            P(("row", "dp"), "col"),
            P(),
            P(None, ("col", "dp"), "row"),
            P(None, ("col", "dp"), "row"),
            P(("row", "dp"), "col"),
            P(("row", "dp"), "col"),
            P(),
            P(None, ("col", "dp"), "row"),
            P(None, ("col", "dp"), "row"),
            P(("row", "dp"), "col"),
            P(("row", "dp"), "col"),
            P(),
        ),
        check_vma=False,
    )
```

```python
import functools
import math

import jax
import jax.numpy as jnp
from jax import lax
from jax.experimental import pallas as pl
from jax.experimental.pallas import tpu as pltpu
from jax.sharding import PartitionSpec as P

D = 2048
HEAD = 128
STREAMS = 4
MICRO = 2


norm_eps = 1e-05
beta_first = 0.9
beta_second = 0.95
adam_eps = 1e-08
learning_rate = 0.05
weight_decay = 0.1

LOW = jnp.bfloat16
FULL = jnp.float32
DMA = pltpu.SemaphoreType.DMA
ANY = pl.BlockSpec(memory_space=pl.ANY)
VMEM = pl.BlockSpec(memory_space=pltpu.VMEM)
SMEM = pl.BlockSpec(memory_space=pltpu.SMEM)
ROOM = 63 * 2**20


def rotary_tables(segment):
    length = segment.shape[0]
    places = jnp.arange(length, dtype=jnp.int32)
    starts = jnp.sum((segment[None, :] < segment[:, None]).astype(jnp.int32), axis=1)
    offsets = (places - starts).astype(jnp.float32)
    halves = jnp.arange(HEAD // 2, dtype=jnp.float32)
    inverse = jnp.exp(halves * (-2.0 * math.log(10000.0) / HEAD))
    angles = offsets[:, None] * inverse[None, :]
    cosine, sine = jnp.cos(angles), jnp.sin(angles)
    return (
        jnp.concatenate([cosine, cosine], axis=1),
        jnp.concatenate([-sine, sine], axis=1),
        starts[:, None],
    )


def norm_forward(hidden):
    means = jnp.sum(hidden, axis=-1, keepdims=True) / D
    squares = jnp.sum(hidden * hidden, axis=-1, keepdims=True) / D
    inverse = lax.rsqrt(squares - means * means + norm_eps)
    return ((hidden - means) * inverse, inverse)


def norm_backward(upstream, hidden):
    normed, inverse = norm_forward(hidden)
    mean_one = jnp.sum(upstream, axis=-1, keepdims=True) / D
    mean_two = jnp.sum(upstream * normed, axis=-1, keepdims=True) / D
    return inverse * (upstream - mean_one - normed * mean_two)


def hyper_parts(hyper):
    width = STREAMS + 2
    parts = []
    for layer in range(2):
        at = [[hyper[(layer * STREAMS + i) * width + k] for k in range(width)] for i in range(STREAMS)]
        parts.append(
            ([row[0] for row in at], [row[1 : STREAMS + 1] for row in at], [row[-1] for row in at])
        )
    return parts


def dot_of(left, right):
    total = left[0] * right[0]
    for a, b in zip(left[1:], right[1:]):
        total = total + a * b
    return total


def column(matrix, index):
    return [row[index] for row in matrix]


def branch_weight(hyper):
    (_, _, c0), (a1, _, _) = hyper_parts(hyper)
    return dot_of(a1, c0)


def combine(weights, stream_set):
    return dot_of(weights, stream_set)


def fold(product):
    rows, width = product.shape
    return jnp.sum(product.reshape(rows // 8, 8, width), axis=0)


def place_rows(match, values_in):
    if values_in.dtype == LOW:
        return jnp.dot(match.astype(LOW), values_in, preferred_element_type=FULL)
    return jnp.dot(
        match.astype(FULL), values_in, precision=lax.Precision.HIGHEST, preferred_element_type=FULL
    )


def prepare_kernel(hyper, streams, cotangent, sent, h_out, mix_out, back_out, gy_out, gram_out):
    rows, width = streams.shape[2:]
    parts, slot = h_out.shape[0], h_out.shape[2]
    (a0, m0, c0), (a1, m1, c1) = hyper_parts(hyper)
    first = [streams[0, i] for i in range(STREAMS)]
    second = [cotangent[0, j] for j in range(STREAMS)]
    match = lax.broadcasted_iota(jnp.int32, (rows, rows), 0) == sent[0]

    def put(out, values_in):
        moved = place_rows(match, values_in)
        for part in range(parts):
            out[part, 0] = moved[part * slot : (part + 1) * slot].astype(out.dtype)

    put(h_out, combine(a0, first))
    put(mix_out, combine([dot_of(row, a1) for row in m0], first))
    put(gy_out, combine(c1, second).astype(LOW))
    put(back_out, combine([dot_of(c0, column(m1, k)) for k in range(STREAMS)], second))

    @pl.when((pl.program_id(0) == 0) & (pl.program_id(1) == 0))
    def _():
        gram_out[...] = jnp.zeros_like(gram_out)

    for i in range(STREAMS):
        for j in range(STREAMS):
            gram_out[i * STREAMS + j] += fold(first[i] * second[j])


def prepare(hyper, streams, cotangent, sent, n_dp, travel):
    micro, _, rows, width = streams.shape
    slot, wide = rows // n_dp, 256
    block = pl.BlockSpec((1, STREAMS, rows, wide), lambda m, f: (m, 0, 0, f))
    home = pl.BlockSpec((n_dp, 1, slot, wide), lambda m, f: (0, m, 0, f))
    shape = (n_dp, micro, slot, width)
    return pl.pallas_call(
        prepare_kernel,
        grid=(micro, width // wide),
        in_specs=[SMEM, block, block, pl.BlockSpec((1, 1, rows), lambda m, f: (m, 0, 0))],
        out_specs=[home] * 4 + [pl.BlockSpec((STREAMS * STREAMS, 8, wide), lambda m, f: (0, 0, 0))],
        out_shape=[jax.ShapeDtypeStruct(shape, FULL)] * 3
        + [
            jax.ShapeDtypeStruct(shape, travel),
            jax.ShapeDtypeStruct((STREAMS * STREAMS, 8, wide), FULL),
        ],
        compiler_params=pltpu.CompilerParams(vmem_limit_bytes=ROOM),
    )(hyper, streams, cotangent, sent[:, None, :])


def finish_kernel(
    hyper, streams, cotangent, sent, y_att, y_ffn, gh_ffn, gh_att, streams_out, grad_out, dots_out
):
    rows, width = streams.shape[2:]
    (a0, m0, c0), (a1, m1, c1) = hyper_parts(hyper)
    first = [streams[0, i] for i in range(STREAMS)]
    second = [cotangent[0, j] for j in range(STREAMS)]
    match = lax.broadcasted_iota(jnp.int32, (rows, rows), 1) == sent[0]
    home_att, home_ffn, back_ffn, back_att = (
        place_rows(match, value[:, 0].reshape(rows, width)) for value in (y_att, y_ffn, gh_ffn, gh_att)
    )
    for j in range(STREAMS):
        mixed = combine([dot_of(m0[k], column(m1, j)) for k in range(STREAMS)], first)
        streams_out[0, j] = mixed + dot_of(c0, column(m1, j)) * home_att + c1[j] * home_ffn
    for i in range(STREAMS):
        mixed = combine([dot_of(m0[i], column(m1, k)) for k in range(STREAMS)], second)
        grad_out[0, i] = mixed + dot_of(m0[i], a1) * back_ffn + a0[i] * back_att

    @pl.when((pl.program_id(0) == 0) & (pl.program_id(1) == 0))
    def _():
        dots_out[...] = jnp.zeros_like(dots_out)

    pairs = (
        [(value, home_att) for value in second]
        + [(value, home_ffn) for value in second]
        + [(value, back_ffn) for value in first]
        + [(value, back_att) for value in first]
        + [(home_att, back_ffn)]
    )
    for index, (left, right) in enumerate(pairs):
        dots_out[index] += fold(left * right)


def finish(hyper, streams, cotangent, sent, homes):
    micro, _, rows, width = streams.shape
    n_dp, _, slot, _ = homes[0].shape
    wide = 256
    block = pl.BlockSpec((1, STREAMS, rows, wide), lambda m, f: (m, 0, 0, f))
    home = pl.BlockSpec((n_dp, 1, slot, wide), lambda m, f: (0, m, 0, f))
    count = 4 * STREAMS + 1
    return pl.pallas_call(
        finish_kernel,
        grid=(micro, width // wide),
        in_specs=[SMEM, block, block, pl.BlockSpec((1, rows, 1), lambda m, f: (m, 0, 0))] + [home] * 4,
        out_specs=[block, block, pl.BlockSpec((count, 8, wide), lambda m, f: (0, 0, 0))],
        out_shape=[
            jax.ShapeDtypeStruct(streams.shape, FULL),
            jax.ShapeDtypeStruct(streams.shape, FULL),
            jax.ShapeDtypeStruct((count, 8, wide), FULL),
        ],
        compiler_params=pltpu.CompilerParams(vmem_limit_bytes=ROOM),
    )(hyper, streams, cotangent, sent[:, :, None], *homes)


def turn(values_in, cosine, sine):
    half = HEAD // 2
    swapped = jnp.concatenate([values_in[:, half:], values_in[:, :half]], axis=1)
    return values_in * cosine + swapped * sine


def dot_last(left, right):
    return lax.dot_general(left, right, (((1,), (1,)), ((), ())), preferred_element_type=jnp.float32)


def dot_first(left, right):
    return lax.dot_general(left, right, (((0,), (0,)), ((), ())), preferred_element_type=jnp.float32)


def allowed_pairs(start_ref, base, block, keys):
    column = lax.broadcasted_iota(jnp.int32, (block, keys), 1)
    row = lax.broadcasted_iota(jnp.int32, (block, keys), 0) + base
    return (column >= start_ref[pl.ds(base, block)]) & (column <= row)


def attend_head(head, q, k, v, start, out, log_out):
    length = q.shape[0]
    block = min(256, length)
    at = pl.ds(head * HEAD, HEAD)
    for base in range(0, length, block):
        keys = base + block
        rows, span = pl.ds(base, block), pl.ds(0, keys)
        scores = dot_last(q[rows, at], k[span, at]) * HEAD ** (-0.5)
        scores = jnp.where(allowed_pairs(start, base, block, keys), scores, -1e30)
        largest = jnp.max(scores, axis=1, keepdims=True)
        weights = jnp.exp(scores - largest)
        totals = jnp.sum(weights, axis=1, keepdims=True)
        probs = (weights * (1.0 / totals)).astype(LOW)
        out[rows, at] = jnp.dot(probs, v[span, at], preferred_element_type=FULL).astype(LOW)
        log_out[rows, pl.ds(head, 1)] = largest + jnp.log(totals)


def attend_head_back(head, grad, q, k, v, log_in, cosine, sine, start, units, k_sum, v_sum):
    length, width = q.shape
    block = min(256, length)
    at = pl.ds(head * HEAD, HEAD)
    k_sum[...] = jnp.zeros_like(k_sum)
    v_sum[...] = jnp.zeros_like(v_sum)
    for base in range(0, length, block):
        keys = base + block
        rows, span = pl.ds(base, block), pl.ds(0, keys)
        scores = dot_last(q[rows, at], k[span, at]) * HEAD ** (-0.5)
        probs = jnp.where(
            allowed_pairs(start, base, block, keys), jnp.exp(scores - log_in[rows, pl.ds(head, 1)]), 0.0
        )
        grad_probs = dot_last(grad[rows, at], v[span, at])
        inner = jnp.sum(probs * grad_probs, axis=1, keepdims=True)
        grad_scores = (probs * (grad_probs - inner) * HEAD ** (-0.5)).astype(LOW)
        grad_query = jnp.dot(grad_scores, k[span, at], preferred_element_type=FULL)
        units[rows, at] = turn(grad_query, cosine[rows], -sine[rows]).astype(LOW)
        k_sum[span] += dot_first(grad_scores, q[rows, at])
        v_sum[span] += dot_first(probs.astype(LOW), grad[rows, at])
    units[:, pl.ds(width + head * HEAD, HEAD)] = turn(k_sum[...], cosine[...], -sine[...]).astype(LOW)
    units[:, pl.ds(2 * width + head * HEAD, HEAD)] = v_sum[...].astype(LOW)


def remote(source, target, send_sem, recv_sem, device):
    return pltpu.make_async_remote_copy(
        src_ref=source,
        dst_ref=target,
        send_sem=send_sem,
        recv_sem=recv_sem,
        device_id=device,
        device_id_type=pl.DeviceIdType.MESH,
    )


def line_place():
    me = lax.axis_index("row")
    return me, me // 2, me % 2


def greet(pairs, plane=None):
    me, place, side = line_place()
    barrier = pltpu.get_barrier_semaphore()

    def signal(device):
        pl.semaphore_signal(barrier, inc=1, device_id=device, device_id_type=pl.DeviceIdType.MESH)

    signal({"row": me + 1 - 2 * side})

    @pl.when(place < pairs - 1)
    def _():
        signal({"row": me + 2})

    @pl.when(place > 0)
    def _():
        signal({"row": me - 2})

    count = 1
    if plane is not None:
        for offset in offsets(plane):
            signal(peer(plane, offset))
            count += 1
    last = pairs - 1
    neighbours = (place + last) // pairs + (2 * last - place) // pairs
    pl.semaphore_wait(barrier, count + neighbours)


def offsets(plane):
    n_dp, n_col = plane
    return [(d, c) for d in range(n_dp) for c in range(n_col) if (d, c) != (0, 0)]


def peer(plane, offset):
    n_dp, n_col = plane
    return {
        "dp": (lax.axis_index("dp") + offset[0]) % n_dp,
        "col": (lax.axis_index("col") + offset[1]) % n_col,
    }


class Exchange:
    def __init__(self, plane, source_of, target, sends, receives, keep):
        self.plane, self.source_of, self.target = plane, source_of, target
        self.sends, self.receives, self.keep = sends, receives, keep

    def move(self, offset):
        device = peer(self.plane, offset)
        return remote(
            self.source_of(device["dp"], device["col"]),
            self.target,
            self.sends.at[offset[0], offset[1]],
            self.receives.at[offset[0], offset[1]],
            device,
        )

    def stay(self):
        return pltpu.make_async_copy(
            self.source_of(lax.axis_index("dp"), lax.axis_index("col")), self.target, self.keep
        )

    def start(self):
        for offset in offsets(self.plane):
            self.move(offset).start()
        self.stay().start()

    def arrive(self):
        for offset in offsets(self.plane):
            self.move(offset).wait_recv()
        self.stay().wait()

    def leave(self):
        for offset in offsets(self.plane):
            self.move(offset).wait_send()


def exchange_sems(plane, count):
    return [DMA((count,) + plane), DMA((count,) + plane), DMA((count,))]


def work_block(work, slot, width, part, side):
    return work.at[
        pl.ds(pl.multiple_of(part * slot, slot), slot), pl.ds(pl.multiple_of(side * width, width), width)
    ]


def to_work(plane, home, work, sems, index):
    slot, width = home.shape[2:]
    return Exchange(
        plane,
        lambda b, c: home.at[b, c],
        work_block(work, slot, width, lax.axis_index("dp"), lax.axis_index("col")),
        sems[0].at[index],
        sems[1].at[index],
        sems[2].at[index],
    )


def to_home(plane, work, home, sems, index):
    slot, width = home.shape[2:]
    return Exchange(
        plane,
        lambda b, c: work_block(work, slot, width, b, c),
        home.at[lax.axis_index("dp"), lax.axis_index("col")],
        sems[0].at[index],
        sems[1].at[index],
        sems[2].at[index],
    )


class Gather:
    def __init__(self, pairs, cuts, own, out, sems):
        self.pairs, self.cuts, self.own, self.out = pairs, cuts, own, out
        self.right, self.left, self.twin_send, self.line, self.twin_recv, self.keep = sems
        self.height = own.shape[0] // cuts

    def piece(self, ref, cut):
        return ref.at[pl.ds(cut * self.height, self.height)]

    def move(self, row, sends, receives, origin, cut, first):
        _, _, side = line_place()
        block = self.piece(self.out.at[origin * 2 + side], cut)
        return remote(
            self.piece(self.own, cut) if first else block,
            block,
            sends.at[origin, cut],
            receives.at[origin, cut],
            {"row": row},
        )

    def to_twin(self, origin, cut, first=False):
        me, _, side = line_place()
        return self.move(me + 1 - 2 * side, self.twin_send, self.twin_recv, origin, cut, first)

    def to_right(self, origin, cut, first=False):
        return self.move(line_place()[0] + 2, self.right, self.line, origin, cut, first)

    def to_left(self, origin, cut, first=False):
        return self.move(line_place()[0] - 2, self.left, self.line, origin, cut, first)

    def stay(self):
        return pltpu.make_async_copy(self.own, self.out.at[line_place()[0]], self.keep)

    def start(self):
        _, place, _ = line_place()
        for cut in range(self.cuts):
            @pl.when(place < self.pairs - 1)
            def _():
                self.to_right(place, cut, True).start()

            @pl.when(place > 0)
            def _():
                self.to_left(place, cut, True).start()

        for cut in range(self.cuts):
            self.to_twin(place, cut, True).start()
        self.stay().start()

    def step(self, step, cut):
        _, place, _ = line_place()

        @pl.when(place >= step)
        def _():
            origin = place - step
            self.to_right(origin, cut).wait_recv()

            @pl.when(place < self.pairs - 1)
            def _():
                self.to_right(origin, cut).start()

            self.to_twin(origin, cut).start()

        @pl.when(place + step <= self.pairs - 1)
        def _():
            origin = place + step
            self.to_left(origin, cut).wait_recv()

            @pl.when(place > 0)
            def _():
                self.to_left(origin, cut).start()

            self.to_twin(origin, cut).start()

    def twin_arrive(self, origin):
        me, _, side = line_place()
        for cut in range(self.cuts):
            other = self.piece(self.out.at[origin * 2 + 1 - side], cut)
            remote(
                other,
                other,
                self.twin_send.at[origin, cut],
                self.twin_recv.at[origin, cut],
                {"row": me + 1 - 2 * side},
            ).wait_recv()

    def finish(self):
        self.stay().wait()
        for origin in range(self.pairs):
            self.twin_arrive(origin)
        self.leave()

    def leave(self):
        _, place, _ = line_place()
        for origin in range(self.pairs):
            for cut in range(self.cuts):
                self.to_twin(origin, cut).wait_send()

                @pl.when((place < self.pairs - 1) & (origin <= place))
                def _():
                    self.to_right(origin, cut).wait_send()

                @pl.when((place > 0) & (origin >= place))
                def _():
                    self.to_left(origin, cut).wait_send()


def gather_sems(pairs, cuts):
    return [DMA((pairs, cuts))] * 5 + [DMA]


def inner_order(pairs, cuts, inner):
    near = [(True, dest, cut) for dest in range(pairs - 1, inner, -1) for cut in range(cuts)]
    far = [(False, dest, cut) for dest in range(inner) for cut in range(cuts)]
    hops = pairs - 1 - 2 * inner
    timed = [(index, 0) + one for index, one in enumerate(near)]
    timed += [(index + hops, 1) + one for index, one in enumerate(far)]
    return [one[2:] for one in sorted(timed, key=lambda one: one[:2])]


class Scatter:
    def __init__(self, pairs, cuts, part, buffers, sems):
        self.pairs, self.cuts, self.part = pairs, cuts, part
        self.twin, self.from_left, self.from_right = buffers[:3]
        self.own = buffers[3] if len(buffers) > 3 else None
        (
            self.right_send,
            self.left_send,
            self.twin_send,
            self.right_recv,
            self.left_recv,
            self.twin_recv,
            self.loaded,
        ) = sems
        self.height = part.shape[1] // cuts

    def span(self, cut):
        return pl.ds(cut * self.height, self.height)

    def mine(self, dest, cut):
        _, _, side = line_place()
        if self.own is None:
            return self.part.at[dest * 2 + side, self.span(cut)]
        return self.own.at[dest, self.span(cut)]

    def load(self, dest, cut):
        _, _, side = line_place()
        return pltpu.make_async_copy(
            self.part.at[dest * 2 + side, self.span(cut)], self.mine(dest, cut), self.loaded.at[dest, cut]
        )

    def to_twin(self, dest, cut):
        me, _, side = line_place()
        return remote(
            self.part.at[dest * 2 + 1 - side, self.span(cut)],
            self.twin.at[dest, self.span(cut)],
            self.twin_send.at[dest, cut],
            self.twin_recv.at[dest, cut],
            {"row": me + 1 - 2 * side},
        )

    def to_right(self, dest, cut):
        return remote(
            self.mine(dest, cut),
            self.from_left.at[dest, self.span(cut)],
            self.right_send.at[dest, cut],
            self.right_recv.at[dest, cut],
            {"row": line_place()[0] + 2},
        )

    def to_left(self, dest, cut):
        return remote(
            self.mine(dest, cut),
            self.from_right.at[dest, self.span(cut)],
            self.left_send.at[dest, cut],
            self.left_recv.at[dest, cut],
            {"row": line_place()[0] - 2},
        )

    def start(self):
        order = []
        for step in range(self.pairs):
            for dest in (self.pairs - 1 - step, step):
                if dest not in order:
                    order.append(dest)
        for dest in order:
            for cut in range(self.cuts):
                self.to_twin(dest, cut).start()
                if self.own is not None:
                    self.load(dest, cut).start()

    def here(self, dest, cut):
        return self.mine(dest, cut)[...].astype(FULL) + self.twin[dest, self.span(cut)].astype(FULL)

    def flows(self, step, place):
        last = self.pairs - 1
        return (
            (last - step, place < last - step, place == 0, self.from_left, self.to_right),
            (step, place > step, place == last, self.from_right, self.to_left),
        )

    def begin(self):
        _, place, _ = line_place()
        ready = []
        for step in range(self.pairs - 1):
            for dest, sending, first, _, copy in self.flows(step, place):
                for cut in range(self.cuts):
                    if (dest, cut) not in ready:
                        ready.append((dest, cut))
                        self.to_twin(dest, cut).wait_recv()
                        if self.own is not None:
                            self.load(dest, cut).wait()

                    @pl.when(sending & first)
                    def _():
                        self.mine(dest, cut)[...] = self.here(dest, cut).astype(LOW)
                        copy(dest, cut).start()

    def pass_on(self, dest, cut, rightward):
        copy, arrived = (self.to_right, self.from_left) if rightward else (self.to_left, self.from_right)
        copy(dest, cut).wait_recv()
        self.mine(dest, cut)[...] = (
            self.here(dest, cut) + arrived[dest, self.span(cut)].astype(FULL)
        ).astype(LOW)
        copy(dest, cut).start()

    def poll(self, index):
        _, place, _ = line_place()
        last = self.pairs - 1
        for inner in range(1, self.pairs // 2):
            order = inner_order(self.pairs, self.cuts, inner)
            if index < len(order):
                near, dest, cut = order[index]

                @pl.when(place == inner)
                def _():
                    self.pass_on(dest, cut, near)

                @pl.when(place == last - inner)
                def _():
                    self.pass_on(last - dest, cut, not near)

    def polls(self):
        return max(
            len(inner_order(self.pairs, self.cuts, inner)) for inner in range(1, self.pairs // 2)
        )

    def finish(self, total):
        _, place, _ = line_place()
        last = self.pairs - 1
        for cut in range(self.cuts):
            span = self.span(cut)
            total[span] = self.here(place, cut)

            @pl.when(place > 0)
            def _():
                self.to_right(place, cut).wait_recv()
                total[span] += self.from_left[place, span].astype(FULL)

            @pl.when(place < last)
            def _():
                self.to_left(place, cut).wait_recv()
                total[span] += self.from_right[place, span].astype(FULL)

        for dest in range(self.pairs):
            for cut in range(self.cuts):
                self.to_twin(dest, cut).wait_send()

                @pl.when(place < dest)
                def _():
                    self.to_right(dest, cut).wait_send()

                @pl.when(place > dest)
                def _():
                    self.to_left(dest, cut).wait_send()


def scatter_buffers(pairs, rows, width, loaded=True):
    return [pltpu.VMEM((pairs, rows, width), LOW)] * (4 if loaded else 3)


def scatter_sems(pairs, cuts):
    return [DMA((pairs, cuts))] * 7


class PlaneScatter:
    def __init__(self, block_of, out, square, buffers, sems):
        self.block_of, self.out, self.square = block_of, out, square
        self.arrived, self.mine, self.onward, self.final = buffers
        self.send, self.recv, self.loaded, self.send_on, self.recv_on = sems
        self.height = out.shape[-2] // 2

    def places(self, half, index):
        d, c = lax.axis_index("dp"), lax.axis_index("col")
        if half == 0:
            there = 1 - c if index == 0 else c
            return {"dp": 1 - d}, self.block_of(there, 1 - d, 0), self.block_of(there, d, 0)
        there = 1 - d if index == 0 else d
        return {"col": 1 - c}, self.block_of(1 - c, there, 1), self.block_of(c, there, 1)

    def move(self, half, index):
        device, block, _ = self.places(half, index)
        return remote(
            block, self.arrived.at[half, index], self.send.at[half, index], self.recv.at[half, index], device
        )

    def load(self, half, index):
        _, _, block = self.places(half, index)
        return pltpu.make_async_copy(block, self.mine.at[half, index], self.loaded.at[half, index])

    def move_on(self, half):
        device = (
            {"col": 1 - lax.axis_index("col")} if half == 0 else {"dp": 1 - lax.axis_index("dp")}
        )
        return remote(
            self.onward.at[half], self.final.at[half], self.send_on.at[half], self.recv_on.at[half], device
        )

    def start(self):
        for index in range(2):
            for half in range(2):
                self.move(half, index).start()
                if self.mine is not None:
                    self.load(half, index).start()

    def sum_of(self, half, index):
        self.move(half, index).wait_recv()
        if self.mine is None:
            _, _, block = self.places(half, index)
            mine = block[...]
        else:
            self.load(half, index).wait()
            mine = self.mine[half, index]
        return mine.astype(FULL) + self.arrived[half, index].astype(FULL)

    def forward(self):
        for half in range(2):
            self.onward[half] = self.sum_of(half, 0).astype(LOW)
            self.move_on(half).start()

    def finish(self):
        for half in range(2):
            total = self.sum_of(half, 1)
            self.move_on(half).wait_recv()
            total = total + self.final[half].astype(FULL)
            width = self.out.shape[-1]
            for index in range(self.out.shape[0]):
                self.out[index, pl.ds(half * self.height, self.height)] = total[
                    :, index * width : (index + 1) * width
                ]
            self.square[half] = fold(total * total)
        for half in range(2):
            for index in range(2):
                self.move(half, index).wait_send()
            self.move_on(half).wait_send()


class PlaneGather:
    def __init__(self, own, block_of, sems):
        self.own, self.block_of = own, block_of
        self.send, self.recv, self.send_on, self.recv_on, self.keep = sems
        self.height = own.shape[0] // 2

    def direct(self, axis, half):
        d, c = lax.axis_index("dp"), lax.axis_index("col")
        return remote(
            self.own.at[pl.ds(half * self.height, self.height)],
            self.block_of(c, d, half),
            self.send.at[axis, half],
            self.recv.at[axis, half],
            {"dp": 1 - d} if axis == 0 else {"col": 1 - c},
        )

    def onward(self, half):
        d, c = lax.axis_index("dp"), lax.axis_index("col")
        block = self.block_of(c, 1 - d, 0) if half == 0 else self.block_of(1 - c, d, 1)
        return remote(
            block,
            block,
            self.send_on.at[half],
            self.recv_on.at[half],
            {"col": 1 - c} if half == 0 else {"dp": 1 - d},
        )

    def stay(self, half):
        d, c = lax.axis_index("dp"), lax.axis_index("col")
        return pltpu.make_async_copy(
            self.own.at[pl.ds(half * self.height, self.height)], self.block_of(c, d, half), self.keep.at[half]
        )

    def start(self):
        for swap in range(2):
            for half in range(2):
                self.direct(half ^ swap, half).start()
        for half in range(2):
            self.stay(half).start()

    def forward(self):
        for half in range(2):
            self.direct(half, half).wait_recv()
            self.onward(half).start()

    def finish(self):
        for half in range(2):
            self.direct(1 - half, half).wait_recv()
            self.onward(half).wait_recv()
            self.stay(half).wait()
        for half in range(2):
            for axis in range(2):
                self.direct(axis, half).wait_send()
            self.onward(half).wait_send()


def plane_gather_sems():
    return [DMA((2, 2)), DMA((2, 2)), DMA((2,)), DMA((2,)), DMA((2,))]


def by_rows(part, height):
    half_height = height // 2
    return lambda c, d, half: part.at[pl.ds((c * 2 + d) * height + half * half_height, half_height)]


def by_owner(part, height):
    half_height = height // 2
    return lambda c, d, half: part.at[c, d, pl.ds(half * half_height, half_height)]


def by_tiles(part, height, width):
    half_height = height // 2
    return lambda c, d, half: part.at[
        pl.ds(d * height + half * half_height, half_height), pl.ds(pl.multiple_of(c * width, width), width)
    ]


CUTS = 2
SUM_CUTS = 4


def call_remote(kernel, collective, **options):
    return pl.pallas_call(
        kernel,
        compiler_params=pltpu.CompilerParams(
            collective_id=collective, has_side_effects=True, vmem_limit_bytes=ROOM
        ),
        **options,
    )


def block_view(whole, rows, width):
    return by_rows(whole, rows) if whole.shape[1] == width else by_tiles(whole, rows, width)


def plane_gathers(weights, wholes, sems):
    return [
        PlaneGather(weight, block_view(whole, *weight.shape), sems[5 * index : 5 * index + 5])
        for index, (weight, whole) in enumerate(zip(weights, wholes))
    ]


def whole_shapes(weights):
    return [
        jax.ShapeDtypeStruct((4 * rows, width) if width != D // 2 else (2 * rows, 2 * width), LOW)
        for rows, width in (weight.shape for weight in weights)
    ]


def enter_kernel(plane, pairs, count, h_home, gy_home, *rest):
    weights, rest = rest[:count], rest[count:]
    (rows_out, h, gy), rest = rest[:3], rest[3:]
    wholes, rest = rest[:count], rest[count:]
    own, plane_sems, line_sems, rest = rest[0], rest[1:4], rest[4:10], rest[10:]
    gathers = plane_gathers(weights, wholes, rest)
    greet(pairs, plane)
    first = to_work(plane, h_home, h, plane_sems, 0)
    second = to_work(plane, gy_home, gy, plane_sems, 1)
    first.start()
    first.arrive()
    for one in gathers:
        one.start()
    own[...] = norm_forward(h[...])[0].astype(LOW)
    gather = Gather(pairs, CUTS, own, rows_out, line_sems)
    gather.start()
    for step in range(1, pairs):
        for cut in range(CUTS):
            gather.step(step, cut)
        if step == 1:
            second.start()
        if step == 2:
            for one in gathers:
                one.forward()
    gather.finish()
    for one in gathers:
        one.finish()
    second.arrive()
    second.leave()
    first.leave()


def enter(plane, pairs, h_home, gy_home, weights, collective):
    n_dp, n_col, slot, width = h_home.shape
    rows = n_dp * slot
    work = jax.ShapeDtypeStruct((rows, n_col * width), FULL)
    outs = call_remote(
        functools.partial(enter_kernel, plane, pairs, len(weights)),
        collective,
        in_specs=[ANY] * (2 + len(weights)),
        out_specs=[ANY, VMEM, ANY] + [ANY] * len(weights),
        out_shape=[
            jax.ShapeDtypeStruct((2 * pairs, rows, n_col * width), LOW),
            work,
            jax.ShapeDtypeStruct(work.shape, gy_home.dtype),
        ]
        + whole_shapes(weights),
        scratch_shapes=[pltpu.VMEM(work.shape, LOW)]
        + exchange_sems(plane, 2)
        + gather_sems(pairs, CUTS)
        + plane_gather_sems() * len(weights),
    )(h_home, gy_home, *weights)
    return outs[0].reshape(2 * pairs * rows, n_col * width), outs[1], outs[2], outs[3:]


def attend_kernel(
    plane, pairs, count, x_in, w_in, w_out, cosine, sine, start, gathered, mix_home,
    *rest,
):
    weights, rest = rest[:count], rest[count:]
    (rows_out, mix, heads_out, log_out, q, k, v, low_out, total), rest = rest[:9], rest[9:]
    wholes, rest = rest[:count], rest[count:]
    (x, part, load_sem), plane_sems, scratch, line_sems = rest[:3], rest[3:6], rest[6:16], rest[16:22]
    scatter = Scatter(pairs, SUM_CUTS, part, scratch[:3], scratch[3:])
    gather = Gather(pairs, CUTS, gathered, rows_out, line_sems)
    gathers = plane_gathers(weights, wholes, rest[22:])
    load = pltpu.make_async_copy(x_in, x, load_sem)
    load.start()
    greet(pairs, plane)
    gather.start()
    exchange = to_work(plane, mix_home, mix, plane_sems, 0)
    for one in gathers:
        one.start()
    exchange.start()
    load.wait()
    width = q.shape[1]
    heads = width // HEAD
    for index, out in enumerate((q, k, v)):
        value = jnp.dot(x[...], w_in[:, index * width : (index + 1) * width], preferred_element_type=FULL)
        for head in range(heads):
            at = slice(head * HEAD, (head + 1) * HEAD)
            one = value[:, at]
            out[:, at] = (one if index == 2 else turn(one, cosine[...], sine[...])).astype(LOW)
    for head in range(heads):
        attend_head(head, q, k, v, start, heads_out, log_out)
        if head == 0:
            for cut in range(CUTS):
                gather.step(1, cut)
    rows = total.shape[0]
    for owner in range(2 * pairs):
        part[owner] = jnp.dot(
            heads_out[pl.ds(owner * rows, rows)], w_out[...], preferred_element_type=FULL
        ).astype(LOW)
    scatter.start()
    scatter.begin()
    polls = list(range(scatter.polls()))
    for step in range(2, pairs):
        for cut in range(CUTS):
            gather.step(step, cut)
            for index in polls[:2]:
                scatter.poll(index)
            polls = polls[2:]
        if step == 2:
            for one in gathers:
                one.forward()
    for index in polls:
        scatter.poll(index)
    scatter.finish(total)
    low_out[...] = total[...].astype(LOW)
    gather.finish()
    for one in gathers:
        one.finish()
    exchange.arrive()
    exchange.leave()


def attend(plane, pairs, x, w_in, w_out, cosine, sine, start, gathered, mix_home, weights, collective):
    tokens, width = x.shape
    rows = tokens // (2 * pairs)
    local = w_out.shape[0]
    low = jax.ShapeDtypeStruct((tokens, local), LOW)
    full = jax.ShapeDtypeStruct((rows, width), FULL)
    outs = call_remote(
        functools.partial(attend_kernel, plane, pairs, len(weights)),
        collective,
        in_specs=[ANY, VMEM, VMEM, VMEM, VMEM, VMEM, ANY, ANY] + [ANY] * len(weights),
        out_specs=[ANY, ANY] + [VMEM] * 7 + [ANY] * len(weights),
        out_shape=[
            jax.ShapeDtypeStruct((2 * pairs, rows, width), LOW),
            full,
            low,
            jax.ShapeDtypeStruct((tokens, local // HEAD), FULL),
            low,
            low,
            low,
            jax.ShapeDtypeStruct((rows, width), LOW),
            full,
        ]
        + whole_shapes(weights),
        scratch_shapes=[pltpu.VMEM(x.shape, LOW), pltpu.VMEM((2 * pairs, rows, width), LOW), DMA]
        + exchange_sems(plane, 1)
        + scatter_buffers(pairs, rows, width, False)
        + scatter_sems(pairs, SUM_CUTS)
        + gather_sems(pairs, CUTS)
        + plane_gather_sems() * len(weights),
    )(x, w_in, w_out, cosine, sine, start, gathered, mix_home, *weights)
    return [outs[0].reshape(tokens, width)] + list(outs[1:9]), outs[9:]


def back_kernel(
    pairs, plane, gathered, part, x_in, units_in, hid_in, gy_in,
    rows_out, low_out, out_grad, in_sum, square,
    total, left, right, grad, arrived, onward, final, load_sem,
    send, recv, loaded, send_on, recv_on, *rest,
):
    d, c = lax.axis_index("dp"), lax.axis_index("col")
    scatter = Scatter(pairs, SUM_CUTS, part, rest[:4], rest[4:11])
    gather = Gather(pairs, CUTS, gathered, rows_out, rest[11:])
    height = in_sum.shape[1]
    one = PlaneScatter(
        by_rows(grad, height),
        in_sum,
        square,
        (arrived, None, onward, final),
        (send, recv, loaded, send_on, recv_on),
    )
    narrow = hid_in.shape[1]
    loads = [
        pltpu.make_async_copy(x_in, left, load_sem.at[0]),
        pltpu.make_async_copy(units_in, right, load_sem.at[1]),
        pltpu.make_async_copy(hid_in, left.at[:, pl.ds(0, narrow)], load_sem.at[2]),
        pltpu.make_async_copy(gy_in, right, load_sem.at[3]),
    ]
    loads[0].start()
    loads[1].start()
    greet(pairs, plane)
    gather.start()
    scatter.start()

    def in_block(there, across):
        @pl.loop(0, height // UNIT)
        def _(index):
            at = pl.multiple_of((there * 2 + across) * height + index * UNIT, UNIT)
            grad[pl.ds(at, UNIT)] = dot_first(left[:, pl.ds(at, UNIT)], right[...]).astype(LOW)

    owned, width = out_grad.shape[2:]

    def out_block(part):
        @pl.loop(0, owned // UNIT)
        def _(index):
            at = pl.multiple_of(part * owned + index * UNIT, UNIT)
            tile = dot_first(left[:, pl.ds(at, UNIT)], right[...]).astype(LOW)
            for side in range(2):
                out_grad[side, part, pl.ds(pl.multiple_of(index * UNIT, UNIT), UNIT)] = tile[
                    :, side * width : (side + 1) * width
                ]

    each = -(-scatter.polls() // (CUTS * (pairs - 1)))

    def both(step):
        for cut in range(CUTS):
            gather.step(step + 1, cut)
            for index in range(each):
                scatter.poll((step * CUTS + cut) * each + index)

    scatter.begin()
    loads[0].wait()
    loads[1].wait()
    in_block(1 - c, 1 - d)
    one.move(0, 0).start()
    one.move(1, 0).start()
    in_block(c, 1 - d)
    one.move(0, 1).start()
    in_block(1 - c, d)
    one.move(1, 1).start()
    both(0)
    in_block(c, d)
    loads[2].start()
    loads[3].start()
    both(1)
    loads[2].wait()
    loads[3].wait()
    out_block(0)
    one.forward()
    out_block(1)
    for step in range(2, pairs - 1):
        both(step)
    scatter.finish(total)
    low_out[...] = total[...].astype(LOW)
    gather.finish()
    one.finish()


def back_gather(pairs, plane, gathered, partial, x, units, hid, gy, collective):
    rows, width = gathered.shape
    wide, narrow = units.shape[1], hid.shape[1]
    height = width // 4
    half = (height // 2, wide)
    whole = jax.ShapeDtypeStruct((2 * pairs, rows, width), LOW)
    outs = call_remote(
        functools.partial(back_kernel, pairs, plane),
        collective,
        in_specs=[ANY] * 6,
        out_specs=[ANY, VMEM, VMEM, VMEM, VMEM],
        out_shape=[
            whole,
            jax.ShapeDtypeStruct((rows, width), LOW),
            jax.ShapeDtypeStruct((2, 2, narrow // 2, width // 2), LOW),
            jax.ShapeDtypeStruct((2, height, wide // 2), FULL),
            jax.ShapeDtypeStruct((2, 8, wide), FULL),
        ],
        scratch_shapes=[
            pltpu.VMEM((rows, width), FULL),
            pltpu.VMEM(x.shape, LOW),
            pltpu.VMEM(units.shape, LOW),
            pltpu.VMEM((width, wide), LOW),
            pltpu.VMEM((2, 2) + half, LOW),
            pltpu.VMEM((2,) + half, LOW),
            pltpu.VMEM((2,) + half, LOW),
            DMA((4,)),
            DMA((2, 2)),
            DMA((2, 2)),
            DMA((2, 2)),
            DMA((2,)),
            DMA((2,)),
        ]
        + scatter_buffers(pairs, rows, width)
        + scatter_sems(pairs, SUM_CUTS)
        + gather_sems(pairs, CUTS),
    )(gathered, partial.reshape(whole.shape), x, units, hid, gy)
    return [outs[0].reshape(2 * pairs * rows, width)] + list(outs[1:])


def row_gather_kernel(pairs, gathered, rows_out, *line_sems):
    gather = Gather(pairs, CUTS, gathered, rows_out, line_sems)
    greet(pairs)
    gather.start()
    for step in range(1, pairs):
        for cut in range(CUTS):
            gather.step(step, cut)
    gather.finish()


def row_gather(pairs, gathered, collective):
    rows, width = gathered.shape
    out = call_remote(
        functools.partial(row_gather_kernel, pairs),
        collective,
        in_specs=[ANY],
        out_specs=ANY,
        out_shape=jax.ShapeDtypeStruct((2 * pairs, rows, width), LOW),
        scratch_shapes=gather_sems(pairs, CUTS),
    )(gathered)
    return out.reshape(2 * pairs * rows, width)


def arrival(place, pairs, step):
    chosen = jnp.int32(0)
    for here in range(pairs):
        order = sorted(range(pairs), key=lambda there: abs(there - here))
        chosen = jnp.where(place == here, order[step], chosen)
    return chosen


UNIT = 256


def ffn_kernel(
    plane, pairs, hyper, mix, branch, back_home, w_in, w_out, gy_rows,
    rows_out, hid_out, units_out, y_out, h, gh_out, gy_out,
    own, x, wd, gy, hid, units, y, part, twin, from_left, from_right, total, upstream,
    load_sem, gy_sem, hid_sem, units_sem, y_sem, x_sem,
    twin_send, twin_recv, right_send, right_recv, left_send, left_recv, *rest,
):
    plane_sems, line_sems = rest[:3], rest[3:]
    me, place, side = line_place()
    last = pairs - 1
    rows = own.shape[0]
    height = rows // SUM_CUTS
    half = units.shape[2] // 2
    n_col, n_dp, owned, width = w_out.shape
    tiles = [
        pltpu.make_async_copy(
            w_out.at[c, d],
            wd.at[pl.ds(d * owned, owned), pl.ds(c * width, width)],
            load_sem.at[2 + c * n_dp + d],
        )
        for c in range(n_col)
        for d in range(n_dp)
    ]
    for tile in tiles:
        tile.start()
    greet(pairs, plane)
    loads = [
        pltpu.make_async_copy(mix, h, load_sem.at[0]),
        pltpu.make_async_copy(branch, total, load_sem.at[1]),
    ]
    for load in loads:
        load.start()
    exchange = to_work(plane, back_home, upstream, plane_sems, 0)
    exchange.start()
    order = [arrival(place, pairs, step) for step in range(pairs)]

    def load_gy(step):
        return pltpu.make_async_copy(gy_rows.at[order[step]], gy.at[step % 2], gy_sem.at[step % 2])

    load_gy(0).start()
    loads[0].wait()
    loads[1].wait()
    h[...] = h[...] + branch_weight(hyper) * total[...]
    own[...] = norm_forward(h[...])[0].astype(LOW)
    gather = Gather(pairs, CUTS, own, x, line_sems)
    gather.start()
    for tile in tiles:
        tile.wait()

    def saves(step):
        slot = step % 2
        return [
            pltpu.make_async_copy(hid.at[slot], hid_out.at[order[step]], hid_sem.at[slot]),
            pltpu.make_async_copy(units.at[slot], units_out.at[order[step]], units_sem.at[slot]),
            pltpu.make_async_copy(y.at[slot], y_out.at[order[step]], y_sem.at[slot]),
        ]

    def save_x(step):
        return pltpu.make_async_copy(
            x.at[pl.ds(order[step] * 2, 2)], rows_out.at[pl.ds(order[step] * 2, 2)], x_sem.at[step]
        )

    def work(step):
        slot = step % 2
        x_block = x.at[pl.ds(order[step] * 2, 2)]

        @pl.loop(0, half // UNIT)
        def _(unit):
            at = pl.multiple_of(unit * UNIT, UNIT)
            rows_in = x_block[...].reshape(2 * rows, -1)
            gate = jnp.dot(rows_in, w_in[:, pl.ds(at, UNIT)], preferred_element_type=FULL)
            up = jnp.dot(rows_in, w_in[:, pl.ds(half + at, UNIT)], preferred_element_type=FULL)
            grad = dot_last(gy[slot], wd[pl.ds(at, UNIT)])
            sigma = 1.0 / (1.0 + jnp.exp(-gate))
            silu = gate * sigma
            hid[slot, :, pl.ds(at, UNIT)] = (silu * up).astype(LOW)
            units[slot, :, pl.ds(at, UNIT)] = (
                grad * up * sigma * (1.0 + gate * (1.0 - sigma))
            ).astype(LOW)
            units[slot, :, pl.ds(half + at, UNIT)] = (grad * silu).astype(LOW)

        @pl.loop(0, D // UNIT)
        def _(unit):
            at = pl.multiple_of(unit * UNIT, UNIT)
            y_tile = jnp.dot(hid[slot], wd[:, pl.ds(at, UNIT)], preferred_element_type=FULL)
            y[slot, :, pl.ds(at, UNIT)] = y_tile.astype(LOW)
            tile = dot_last(units[slot], w_in[pl.ds(at, UNIT)]).astype(LOW)
            part[pl.ds(order[step] * 2, 2), :, pl.ds(at, UNIT)] = tile.reshape(2, rows, UNIT)

    def to_twin(dest):
        return remote(
            part.at[dest * 2 + 1 - side],
            twin.at[dest],
            twin_send.at[dest],
            twin_recv.at[dest],
            {"row": me + 1 - 2 * side},
        )

    def line(dest, cut, rightward):
        span = pl.ds(cut * height, height)
        return remote(
            part.at[dest * 2 + side, span],
            (from_left if rightward else from_right).at[dest, span],
            (right_send if rightward else left_send).at[dest, cut],
            (right_recv if rightward else left_recv).at[dest, cut],
            {"row": me + 2 if rightward else me - 2},
        )

    def here(dest, span):
        return part[dest * 2 + side, span].astype(FULL) + twin[dest, span].astype(FULL)

    def send_first(step):
        dest = order[step]
        to_twin(dest).wait_recv()
        for at_end, rightward in ((place == 0, True), (place == last, False)):
            @pl.when(at_end & (dest != place))
            def _():
                for cut in range(SUM_CUTS):
                    span = pl.ds(cut * height, height)
                    part[dest * 2 + side, span] = here(dest, span).astype(LOW)
                    line(dest, cut, rightward).start()

    for step in range(pairs):
        if step > 0:
            for cut in range(CUTS):
                gather.step(step, cut)
        else:
            gather.stay().wait()
        if step + 1 < pairs:
            load_gy(step + 1).start()
        gather.twin_arrive(order[step])
        save_x(step).start()
        load_gy(step).wait()
        if step >= 2:
            for save in saves(step - 2):
                save.wait()
        work(step)
        to_twin(order[step]).start()
        for save in saves(step):
            save.start()
        if step > 0:
            send_first(step - 1)
    send_first(pairs - 1)

    def pass_on(dest, cut, rightward):
        arrived = from_left if rightward else from_right
        span = pl.ds(cut * height, height)
        line(dest, cut, rightward).wait_recv()
        part[dest * 2 + side, span] = (here(dest, span) + arrived[dest, span].astype(FULL)).astype(LOW)
        line(dest, cut, rightward).start()

    for inner in range(1, pairs // 2):
        order_here = [(reach, cut, 0, True, reach) for reach in range(inner + 1, pairs) for cut in range(SUM_CUTS)]
        order_here += [
            (last - dest, cut + last - 2 * inner, 1, False, dest) for dest in range(inner) for cut in range(SUM_CUTS)
        ]
        for reach, at, late, near, dest in sorted(order_here):
            cut = at - (last - 2 * inner) * late

            @pl.when(place == inner)
            def _():
                pass_on(dest, cut, near)

            @pl.when(place == last - inner)
            def _():
                pass_on(last - dest, cut, not near)

    for cut in range(SUM_CUTS):
        span = pl.ds(cut * height, height)
        total[span] = here(place, span)

        @pl.when(place > 0)
        def _():
            line(place, cut, True).wait_recv()
            total[span] += from_left[place, span].astype(FULL)

        @pl.when(place < last)
        def _():
            line(place, cut, False).wait_recv()
            total[span] += from_right[place, span].astype(FULL)

    exchange.arrive()
    grad = norm_backward(total[...], h[...])
    gh_out[...] = grad.astype(LOW)
    gy_out[...] = (upstream[...] + branch_weight(hyper) * grad).astype(LOW)

    exchange.leave()
    gather.leave()
    for step in range(pairs):
        save_x(step).wait()
    for step in range(pairs - 2, pairs):
        for save in saves(step):
            save.wait()
    for dest in range(pairs):
        to_twin(dest).wait_send()
        for cut in range(SUM_CUTS):
            @pl.when(place < dest)
            def _():
                line(dest, cut, True).wait_send()

            @pl.when(place > dest)
            def _():
                line(dest, cut, False).wait_send()


def feed_forward(plane, pairs, hyper, mix, branch, back_home, w_in, w_out, gy_rows, collective):
    rows, width = mix.shape
    units = w_in.shape[1]
    half = units // 2
    low = jax.ShapeDtypeStruct((rows, width), LOW)

    def by_pair(last_width):
        return jax.ShapeDtypeStruct((pairs, 2 * rows, last_width), LOW)

    blocks = pltpu.VMEM((pairs, rows, width), LOW)
    full = pltpu.VMEM((rows, width), FULL)
    outs = call_remote(
        functools.partial(ffn_kernel, plane, pairs),
        collective,
        in_specs=[SMEM, ANY, ANY, ANY, VMEM, ANY, ANY],
        out_specs=[ANY, ANY, ANY, ANY, VMEM, VMEM, VMEM],
        out_shape=[
            jax.ShapeDtypeStruct((2 * pairs, rows, width), LOW),
            by_pair(half),
            by_pair(units),
            by_pair(width),
            jax.ShapeDtypeStruct((rows, width), FULL),
            low,
            low,
        ],
        scratch_shapes=[
            pltpu.VMEM((rows, width), LOW),
            pltpu.VMEM((2 * pairs, rows, width), LOW),
            pltpu.VMEM((half, width), LOW),
            pltpu.VMEM((2, 2 * rows, width), LOW),
            pltpu.VMEM((2, 2 * rows, half), LOW),
            pltpu.VMEM((2, 2 * rows, units), LOW),
            pltpu.VMEM((2, 2 * rows, width), LOW),
            pltpu.VMEM((2 * pairs, rows, width), LOW),
            blocks,
            blocks,
            blocks,
            full,
            full,
            DMA((2 + plane[0] * plane[1],)),
            DMA((2,)),
            DMA((2,)),
            DMA((2,)),
            DMA((2,)),
            DMA((pairs,)),
            DMA((pairs,)),
            DMA((pairs,)),
        ]
        + [DMA((pairs, SUM_CUTS))] * 4
        + exchange_sems(plane, 1)
        + gather_sems(pairs, CUTS),
    )(hyper, mix, branch, back_home, w_in, w_out, gy_rows.reshape(pairs, 2 * rows, width))
    tokens = 2 * pairs * rows
    return [value.reshape(tokens, -1) for value in outs[:4]] + list(outs[5:])


def leave_kernel(
    plane, pairs, in_kernel, gy_in, x_in, heads_in, log_in, q, k, v, cosine, sine, start, w_in, w_out, h,
    y_att, y_ffn, gh_ffn, *rest,
):
    if in_kernel:
        ffn_grad, rest = rest[0], rest[1:]
    homes, rest = rest[:4], rest[4:]
    if in_kernel:
        sums, rest = rest[:6], rest[6:]
    (grad_in, grad_out, rows_in, units, back, k_sum, v_sum, part, total, last, load_sem), rest = (
        rest[:11],
        rest[11:],
    )
    plane_sems, scratch, rest = rest[:3], rest[3:13], rest[13:]
    scatter = Scatter(pairs, SUM_CUTS, part, scratch[:3], scratch[3:])
    load_gy = pltpu.make_async_copy(gy_in, rows_in, load_sem.at[0])
    load_x = pltpu.make_async_copy(x_in, rows_in, load_sem.at[1])
    load_gy.start()
    planes = []
    if in_kernel:
        own_ffn, rest = rest[0], rest[1:]
        for index, block_of in enumerate(
            (
                by_owner(ffn_grad, sums[0].shape[1]),
                by_tiles(grad_out, *sums[2].shape[1:]),
                by_rows(grad_in, sums[4].shape[1]),
            )
        ):
            one = rest[8 * index : 8 * index + 8]
            planes.append(
                PlaneScatter(
                    block_of,
                    sums[2 * index],
                    sums[2 * index + 1],
                    (one[0], None if index else own_ffn, one[1], one[2]),
                    one[3:],
                )
            )
    greet(pairs, plane)
    ways = [
        to_home(plane, work, home, plane_sems, index)
        for index, (work, home) in enumerate(zip((y_att, y_ffn, gh_ffn, last), homes))
    ]
    for one in planes[:1]:
        one.start()
    for way in ways[:3]:
        way.start()
    load_gy.wait()
    back[...] = dot_last(rows_in[...], w_out[...]).astype(LOW)
    width = q.shape[1]
    for head in range(width // HEAD):
        attend_head_back(
            head, back, q, k, v, log_in, cosine, sine, start, units, k_sum, v_sum
        )
    rows = total.shape[0]
    for owner in range(2 * pairs):
        part[owner] = dot_last(units[pl.ds(owner * rows, rows)], w_in[...]).astype(LOW)
    scatter.start()
    scatter.begin()
    grad_out[...] = dot_first(heads_in[...], rows_in[...]).astype(LOW)
    load_x.start()
    for one in planes[1:2]:
        one.start()
    load_x.wait()
    quarter = D // SUM_CUTS
    polls = list(range(scatter.polls()))
    for cut in range(SUM_CUTS):
        for index in polls[:2]:
            scatter.poll(index)
        polls = polls[2:]

        @pl.loop(0, quarter // UNIT)
        def _(index):
            at = pl.multiple_of(cut * quarter + index * UNIT, UNIT)
            grad_in[pl.ds(at, UNIT)] = dot_first(rows_in[:, pl.ds(at, UNIT)], units[...]).astype(LOW)

    for one in planes[2:]:
        one.start()
    for one in planes[:1]:
        one.forward()
    for index in polls:
        scatter.poll(index)
    for one in planes[1:]:
        one.forward()
    scatter.finish(total)
    last[...] = norm_backward(total[...], h[...]).astype(last.dtype)
    ways[3].start()
    for one in planes:
        one.finish()
    for way in ways:
        way.arrive()
        way.leave()


def leave(
    plane, pairs, ffn_grad, gy, x, heads, log_totals, q, k, v, tables, w_in, w_out, h, works, collective
):
    in_kernel = len(ffn_grad) > 0
    rows, width = h.shape
    n_dp, n_col = plane
    tokens, local = q.shape
    home = jax.ShapeDtypeStruct((n_dp, n_col, rows // n_dp, width // n_col), works[0].dtype)
    grads = [(width, 3 * local), (local, width)]
    extra, planes = [], []
    if in_kernel:
        owned = [(1,) + ffn_grad[0].shape[2:], (1, local // 2, width // 2), (3, width // 4, local)]
        planes.append(pltpu.VMEM((2, 2, owned[0][1] // 2, owned[0][2]), LOW))
        for shape in owned:
            extra += [shape, (2, 8, shape[0] * shape[2])]
            half = (shape[1] // 2, shape[0] * shape[2])
            planes += [
                pltpu.VMEM((2, 2) + half, LOW),
                pltpu.VMEM((2,) + half, LOW),
                pltpu.VMEM((2,) + half, LOW),
                DMA((2, 2)),
                DMA((2, 2)),
                DMA((2, 2)),
                DMA((2,)),
                DMA((2,)),
            ]
    grad_refs = [pltpu.VMEM(shape, LOW) for shape in grads]
    grad_outs = [] if in_kernel else [jax.ShapeDtypeStruct(shape, LOW) for shape in grads]
    outs = call_remote(
        functools.partial(leave_kernel, plane, pairs, in_kernel),
        collective,
        in_specs=[ANY, ANY] + [VMEM] * 11 + [ANY] * (3 + len(ffn_grad)),
        out_specs=[ANY] * 4 + [VMEM] * (len(extra) + len(grad_outs)),
        out_shape=[home] * 4 + [jax.ShapeDtypeStruct(shape, FULL) for shape in extra] + grad_outs,
        scratch_shapes=(grad_refs if in_kernel else [])
        + [
            pltpu.VMEM(x.shape, LOW),
            pltpu.VMEM((tokens, 3 * local), LOW),
            pltpu.VMEM((tokens, local), LOW),
            pltpu.VMEM((tokens, HEAD), FULL),
            pltpu.VMEM((tokens, HEAD), FULL),
            pltpu.VMEM((2 * pairs, rows, width), LOW),
            pltpu.VMEM((rows, width), FULL),
            pltpu.VMEM((rows, width), works[0].dtype),
            DMA((2,)),
        ]
        + exchange_sems(plane, 4)
        + scatter_buffers(pairs, rows, width, False)
        + scatter_sems(pairs, SUM_CUTS)
        + planes,
    )(gy, x, heads, log_totals, q, k, v, *tables, w_in, w_out, h, *works, *ffn_grad)
    return outs[:4], outs[4:]


def total_kernel(plane, count, own, out, line, flat, line_send, line_recv, flat_send, flat_recv):
    n_dp, n_col = plane
    me = lax.axis_index("row")
    here = lax.axis_index("dp") * n_col + lax.axis_index("col")
    barrier = pltpu.get_barrier_semaphore()
    rows = [(me + step) % count for step in range(1, count)]
    for row in rows:
        pl.semaphore_signal(barrier, inc=1, device_id={"row": row}, device_id_type=pl.DeviceIdType.MESH)
    for offset in offsets(plane):
        pl.semaphore_signal(
            barrier, inc=1, device_id=peer(plane, offset), device_id_type=pl.DeviceIdType.MESH
        )
    pl.semaphore_wait(barrier, count - 1 + n_dp * n_col - 1)
    line[me] = own[...]
    copies = [
        remote(line.at[me], line.at[me], line_send.at[step], line_recv.at[step], {"row": row})
        for step, row in enumerate(rows)
    ]
    for copy in copies:
        copy.start()
    for copy in copies:
        copy.wait()
    sums = line[0]
    for row in range(1, count):
        sums = sums + line[row]
    flat[here] = sums
    copies = [
        remote(
            flat.at[here],
            flat.at[here],
            flat_send.at[offset[0], offset[1]],
            flat_recv.at[offset[0], offset[1]],
            peer(plane, offset),
        )
        for offset in offsets(plane)
    ]
    for copy in copies:
        copy.start()
    for copy in copies:
        copy.wait()
    sums = flat[0]
    for index in range(1, n_dp * n_col):
        sums = sums + flat[index]
    out[...] = sums


def sum_everywhere(plane, values_in, collective):
    count = lax.axis_size("row")
    shape = values_in.shape
    return call_remote(
        functools.partial(total_kernel, plane, count),
        collective,
        in_specs=[VMEM],
        out_specs=VMEM,
        out_shape=jax.ShapeDtypeStruct(shape, FULL),
        scratch_shapes=[
            pltpu.VMEM((count,) + shape, FULL),
            pltpu.VMEM((plane[0] * plane[1],) + shape, FULL),
            DMA((count - 1,)),
            DMA((count - 1,)),
            DMA(plane),
            DMA(plane),
        ],
    )(values_in)


def mat(left, right):
    return jnp.sum(left[:, :, None] * right[None, :, :], axis=1)


def gather_blocks(weight_low):
    return lax.all_gather(weight_low, ("col", "dp"), axis=0, tiled=True)


def scatter_blocks(grad_low):
    return lax.psum_scatter(grad_low, ("col", "dp"), scatter_dimension=0, tiled=True).astype(FULL)


def side_by_side(weight):
    return jnp.concatenate([weight[index] for index in range(weight.shape[0])], axis=1)


def apart(weight, count):
    width = weight.shape[1] // count
    return jnp.stack([weight[:, index * width : (index + 1) * width] for index in range(count)])


def whole_out(weight_low, n_dp, n_col):
    rows, width = weight_low.shape
    blocks = gather_blocks(weight_low).reshape(n_col, n_dp, rows, width)
    return blocks.transpose(1, 2, 0, 3).reshape(n_dp * rows, n_col * width)


def own_out(grad, n_dp, n_col):
    rows, width = grad.shape[0] // n_dp, grad.shape[1] // n_col
    blocks = grad.astype(LOW).reshape(n_dp, rows, n_col, width).transpose(2, 0, 1, 3)
    return scatter_blocks(blocks.reshape(n_col * n_dp * rows, width))


def adam_update(weight, grad_sum, moment_one, moment_two, clip_factor, step_value):
    clipped = grad_sum * clip_factor
    new_one = beta_first * moment_one + (1.0 - beta_first) * clipped
    new_two = beta_second * moment_two + (1.0 - beta_second) * clipped * clipped
    fix_one = 1.0 - jnp.power(beta_first, step_value)
    fix_two = 1.0 - jnp.power(beta_second, step_value)
    new_weight = weight - learning_rate * (
        new_one / fix_one / (jnp.sqrt(new_two / fix_two) + adam_eps) + weight_decay * weight
    )
    return (new_weight, new_one, new_two)


def body(
    streams,
    cotangent,
    destination,
    segments,
    attention_in,
    feedforward_in,
    attention_out,
    feedforward_out,
    attention_in_moment,
    feedforward_in_moment,
    attention_out_moment,
    feedforward_out_moment,
    attention_in_second,
    feedforward_in_second,
    attention_out_second,
    feedforward_out_second,
    hyper_weights,
    hyper_moment,
    hyper_second,
    step_count,
):
    n_dp, n_col, count = lax.axis_size("dp"), lax.axis_size("col"), lax.axis_size("row")
    plane, pairs = (n_dp, n_col), count // 2
    rows = destination.shape[1]
    group_tokens = segments.shape[2]
    slot = rows // n_dp
    travel = LOW if slot % 16 == 0 else FULL
    in_kernel = plane == (2, 2)
    attention_low = [side_by_side(attention_in).astype(LOW), attention_out.astype(LOW)]
    feedforward_low = [side_by_side(feedforward_in).astype(LOW), feedforward_out.astype(LOW)]

    group = destination // group_tokens
    sent = (
        group * slot
        + (destination - group * group_tokens)
        - lax.axis_index("row") * rows
        - lax.axis_index("dp") * slot
    )
    hyper = hyper_weights.reshape(-1)
    h_home, mix_home, back_home, gy_home, gram = prepare(
        hyper, streams, cotangent, sent, n_dp, travel
    )
    segment = lax.dynamic_index_in_dim(segments[:, 0], lax.axis_index("col"), 0, keepdims=False)
    cosine, sine, start = rotary_tables(segment)

    feedforward_out_low = gather_blocks(feedforward_low[1]).reshape(n_col, n_dp, *feedforward_out.shape)
    early = attention_low if in_kernel else []
    rows_att, hidden_att, gy_work, wholes = enter(plane, pairs, h_home, gy_home, early, 1)
    if not in_kernel:
        wholes = [gather_blocks(attention_low[0]), whole_out(attention_low[1], n_dp, n_col)]
    attention_in_low, attention_out_low = wholes
    (
        grad_rows_ffn,
        mix_work,
        heads_low,
        log_totals,
        query_low,
        key_low,
        value_low,
        branch_low,
        branch_att,
    ), wholes = attend(
        plane,
        pairs,
        rows_att,
        attention_in_low,
        attention_out_low,
        cosine,
        sine,
        start,
        gy_work.astype(LOW),
        mix_home,
        feedforward_low[:1] if in_kernel else [],
        2,
    )
    feedforward_in_low = wholes[0] if in_kernel else gather_blocks(feedforward_low[0])
    rows_ffn, hidden_low, grad_units, partial_ffn, grad_hidden_ffn, grad_branch = feed_forward(
        plane,
        pairs,
        hyper,
        mix_work,
        branch_att,
        back_home,
        feedforward_in_low,
        feedforward_out_low,
        grad_rows_ffn,
        3,
    )
    if in_kernel:
        grad_rows_att, branch_ffn, grad_out, sum_in, square = back_gather(
            pairs, plane, grad_branch, partial_ffn, rows_ffn, grad_units, hidden_low, grad_rows_ffn, 5
        )
        ffn_grad, squares = [grad_out], [square]
    else:
        grad_rows_att = row_gather(pairs, grad_branch, 5)
        branch_ffn = lax.psum_scatter(partial_ffn, "row", scatter_dimension=0, tiled=True)
        sums_ffn = [
            apart(
                scatter_blocks(
                    jnp.einsum("td,tu->du", rows_ffn, grad_units, preferred_element_type=FULL).astype(LOW)
                ),
                2,
            ),
            own_out(
                jnp.einsum("tu,td->ud", hidden_low, grad_rows_ffn, preferred_element_type=FULL), n_dp, n_col
            ),
        ]
        ffn_grad, squares = [], [value * value for value in sums_ffn]

    homes, sums_att = leave(
        plane,
        pairs,
        ffn_grad,
        grad_rows_att,
        rows_att,
        heads_low,
        log_totals,
        query_low,
        key_low,
        value_low,
        (cosine, sine, start),
        attention_in_low,
        attention_out_low,
        hidden_att,
        [value.astype(travel) for value in (branch_low, branch_ffn, grad_hidden_ffn)],
        6,
    )
    if in_kernel:
        squares += sums_att[1::2]
        shard_feedforward_out, shard_attention_out, shard_attention_in = sums_att[::2]
        shard_feedforward_out, shard_attention_out = shard_feedforward_out[0], shard_attention_out[0]
        shard_feedforward_in = sum_in
    else:
        shard_attention_in = apart(scatter_blocks(sums_att[0]), 3)
        shard_attention_out = own_out(sums_att[1], n_dp, n_col)
        squares += [value * value for value in (shard_attention_in, shard_attention_out)]
        shard_feedforward_in, shard_feedforward_out = sums_ffn
    square = sum(jnp.sum(value) for value in squares)
    streams_out, stream_grad, dots = finish(hyper, streams, cotangent, sent, homes)
    dots = jnp.concatenate([jnp.sum(gram, axis=(1, 2)), jnp.sum(dots, axis=(1, 2)), square[None]])
    totals = sum_everywhere(plane, jnp.pad(dots, (0, 128 - dots.shape[0])).reshape(1, 128), 7)[0]
    a0, m0, c0 = hyper_weights[0, :, 0], hyper_weights[0, :, 1:5], hyper_weights[0, :, 5]
    a1, m1, c1 = hyper_weights[1, :, 0], hyper_weights[1, :, 1:5], hyper_weights[1, :, 5]
    gram = totals[:16].reshape(STREAMS, STREAMS)
    att_cot, ffn_cot = totals[16:20], totals[20:24]
    streams_ffn, streams_att = totals[24:28], totals[28:32]
    att_ffn, square_total = totals[32], totals[33]
    grad_m1 = mat(m0.T, gram) + c0[:, None] * att_cot[None, :]
    grad_a1 = jnp.sum(m0 * streams_ffn[:, None], axis=0) + c0 * att_ffn
    grad_m0 = mat(gram, m1.T) + streams_ffn[:, None] * a1[None, :]
    grad_c0 = jnp.sum(m1 * att_cot[None, :], axis=1) + a1 * att_ffn
    hyper_grad = jnp.stack(
        [
            jnp.concatenate([streams_att[:, None], grad_m0, grad_c0[:, None]], axis=1),
            jnp.concatenate([grad_a1[:, None], grad_m1, ffn_cot[:, None]], axis=1),
        ]
    )
    grad_norm = jnp.sqrt(square_total + jnp.sum(hyper_grad * hyper_grad))
    clip_factor = 1.0 / jnp.maximum(grad_norm, 1.0)
    step_value = step_count[0].astype(jnp.float32)
    attention_in_new = adam_update(
        attention_in,
        shard_attention_in,
        attention_in_moment,
        attention_in_second,
        clip_factor,
        step_value,
    )
    feedforward_in_new = adam_update(
        feedforward_in,
        shard_feedforward_in,
        feedforward_in_moment,
        feedforward_in_second,
        clip_factor,
        step_value,
    )
    attention_out_new = adam_update(
        attention_out,
        shard_attention_out,
        attention_out_moment,
        attention_out_second,
        clip_factor,
        step_value,
    )
    feedforward_out_new = adam_update(
        feedforward_out,
        shard_feedforward_out,
        feedforward_out_moment,
        feedforward_out_second,
        clip_factor,
        step_value,
    )
    hyper_new = adam_update(
        hyper_weights, hyper_grad, hyper_moment, hyper_second, clip_factor, step_value
    )
    return (
        streams_out,
        stream_grad,
        grad_norm.reshape(1),
        shard_attention_in,
        shard_feedforward_in,
        shard_attention_out,
        shard_feedforward_out,
        hyper_grad,
        attention_in_new[0],
        feedforward_in_new[0],
        attention_out_new[0],
        feedforward_out_new[0],
        hyper_new[0],
        attention_in_new[1],
        feedforward_in_new[1],
        attention_out_new[1],
        feedforward_out_new[1],
        hyper_new[1],
        attention_in_new[2],
        feedforward_in_new[2],
        attention_out_new[2],
        feedforward_out_new[2],
        hyper_new[2],
    )


def solution(mesh):
    placed = (
        P(None, None, ("dp", "row"), "col"),
        P(None, None, ("dp", "row"), "col"),
        P(None, ("dp", "row")),
        P(None, "dp", None),
        P(None, ("col", "dp"), "row"),
        P(None, ("col", "dp"), "row"),
        P(("row", "dp"), "col"),
        P(("row", "dp"), "col"),
        P(None, ("col", "dp"), "row"),
        P(None, ("col", "dp"), "row"),
        P(("row", "dp"), "col"),
        P(("row", "dp"), "col"),
        P(None, ("col", "dp"), "row"),
        P(None, ("col", "dp"), "row"),
        P(("row", "dp"), "col"),
        P(("row", "dp"), "col"),
        P(),
        P(),
        P(),
        P(),
    )
    return jax.shard_map(
        body,
        mesh=mesh,
        in_specs=placed,
        out_specs=(
            P(None, None, ("dp", "row"), "col"),
            P(None, None, ("dp", "row"), "col"),
            P(),
            P(None, ("col", "dp"), "row"),
            P(None, ("col", "dp"), "row"),
            P(("row", "dp"), "col"),
            P(("row", "dp"), "col"),
            P(),
            P(None, ("col", "dp"), "row"),
            P(None, ("col", "dp"), "row"),
            P(("row", "dp"), "col"),
            P(("row", "dp"), "col"),
            P(),
            P(None, ("col", "dp"), "row"),
            P(None, ("col", "dp"), "row"),
            P(("row", "dp"), "col"),
            P(("row", "dp"), "col"),
            P(),
            P(None, ("col", "dp"), "row"),
            P(None, ("col", "dp"), "row"),
            P(("row", "dp"), "col"),
            P(("row", "dp"), "col"),
            P(),
        ),
        check_vma=False,
    )
```

```python
import functools
import math

import jax
import jax.numpy as jnp
from jax import lax
from jax.experimental import pallas as pl
from jax.experimental.pallas import tpu as pltpu
from jax.sharding import PartitionSpec as P

D = 2048
HEAD = 128
STREAMS = 4
MICRO = 2


norm_eps = 1e-05
beta_first = 0.9
beta_second = 0.95
adam_eps = 1e-08
learning_rate = 0.05
weight_decay = 0.1

LOW = jnp.bfloat16
FULL = jnp.float32
DMA = pltpu.SemaphoreType.DMA
ANY = pl.BlockSpec(memory_space=pl.ANY)
VMEM = pl.BlockSpec(memory_space=pltpu.VMEM)
SMEM = pl.BlockSpec(memory_space=pltpu.SMEM)
ROOM = 63 * 2**20


def rotary_parts(segment):
    starts = jnp.sum((segment[None, :] < segment[:, None]).astype(jnp.int32), axis=1)
    halves = jnp.tile(jnp.arange(HEAD // 2, dtype=jnp.float32), 2)
    return starts[:, None], jnp.exp(halves * (-2.0 * math.log(10000.0) / HEAD))[None, :]


def norm_forward(hidden):
    means = jnp.sum(hidden, axis=-1, keepdims=True) / D
    squares = jnp.sum(hidden * hidden, axis=-1, keepdims=True) / D
    inverse = lax.rsqrt(squares - means * means + norm_eps)
    return ((hidden - means) * inverse, inverse)


def norm_backward(upstream, hidden):
    normed, inverse = norm_forward(hidden)
    mean_one = jnp.sum(upstream, axis=-1, keepdims=True) / D
    mean_two = jnp.sum(upstream * normed, axis=-1, keepdims=True) / D
    return inverse * (upstream - mean_one - normed * mean_two)


def hyper_parts(hyper):
    width = STREAMS + 2
    parts = []
    for layer in range(2):
        at = [[hyper[(layer * STREAMS + i) * width + k] for k in range(width)] for i in range(STREAMS)]
        parts.append(
            ([row[0] for row in at], [row[1 : STREAMS + 1] for row in at], [row[-1] for row in at])
        )
    return parts


def dot_of(left, right):
    total = left[0] * right[0]
    for a, b in zip(left[1:], right[1:]):
        total = total + a * b
    return total


def column(matrix, index):
    return [row[index] for row in matrix]


def branch_weight(hyper):
    (_, _, c0), (a1, _, _) = hyper_parts(hyper)
    return dot_of(a1, c0)


def combine(weights, stream_set):
    return dot_of(weights, stream_set)


def fold(product):
    rows, width = product.shape
    return jnp.sum(product.reshape(rows // 8, 8, width), axis=0)


def place_rows(match, values_in):
    match = match.astype(LOW)
    if values_in.dtype == LOW:
        return jnp.dot(match, values_in, preferred_element_type=FULL)
    high = values_in.astype(LOW)
    rest = values_in - high.astype(FULL)
    middle = rest.astype(LOW)
    last = (rest - middle.astype(FULL)).astype(LOW)
    high, middle, last = (jnp.dot(match, piece, preferred_element_type=FULL) for piece in (high, middle, last))
    return high + (middle + last)


def prepare_kernel(hyper, streams, cotangent, sent, h_out, mix_out, back_out, gy_out, gram_out):
    rows, width = streams.shape[2:]
    parts, slot = h_out.shape[0], h_out.shape[2]
    (a0, m0, c0), (a1, m1, c1) = hyper_parts(hyper)
    first = [streams[0, i] for i in range(STREAMS)]
    second = [cotangent[0, j] for j in range(STREAMS)]
    match = lax.broadcasted_iota(jnp.int32, (rows, rows), 0) == sent[0]

    def put(out, values_in):
        moved = place_rows(match, values_in)
        for part in range(parts):
            out[part, 0] = moved[part * slot : (part + 1) * slot].astype(out.dtype)

    put(h_out, combine(a0, first))
    put(mix_out, combine([dot_of(row, a1) for row in m0], first))
    put(gy_out, combine(c1, second).astype(LOW))
    put(back_out, combine([dot_of(c0, column(m1, k)) for k in range(STREAMS)], second))

    @pl.when((pl.program_id(0) == 0) & (pl.program_id(1) == 0))
    def _():
        gram_out[...] = jnp.zeros_like(gram_out)

    for i in range(STREAMS):
        for j in range(STREAMS):
            gram_out[i * STREAMS + j] += fold(first[i] * second[j])


def prepare(hyper, streams, cotangent, sent, n_dp, travel):
    micro, _, rows, width = streams.shape
    slot, wide = rows // n_dp, 512
    block = pl.BlockSpec((1, STREAMS, rows, wide), lambda m, f: (m, 0, 0, f))
    home = pl.BlockSpec((n_dp, 1, slot, wide), lambda m, f: (0, m, 0, f))
    shape = (n_dp, micro, slot, width)
    return pl.pallas_call(
        prepare_kernel,
        grid=(micro, width // wide),
        in_specs=[SMEM, block, block, pl.BlockSpec((1, 1, rows), lambda m, f: (m, 0, 0))],
        out_specs=[home] * 4 + [pl.BlockSpec((STREAMS * STREAMS, 8, wide), lambda m, f: (0, 0, 0))],
        out_shape=[jax.ShapeDtypeStruct(shape, FULL)] * 3
        + [
            jax.ShapeDtypeStruct(shape, travel),
            jax.ShapeDtypeStruct((STREAMS * STREAMS, 8, wide), FULL),
        ],
        compiler_params=pltpu.CompilerParams(vmem_limit_bytes=ROOM),
    )(hyper, streams, cotangent, sent[:, None, :])


def finish_kernel(
    hyper, streams, cotangent, sent, y_att, y_ffn, gh_ffn, gh_att, streams_out, grad_out, dots_out
):
    rows, width = streams.shape[2:]
    (a0, m0, c0), (a1, m1, c1) = hyper_parts(hyper)
    first = [streams[0, i] for i in range(STREAMS)]
    second = [cotangent[0, j] for j in range(STREAMS)]
    match = lax.broadcasted_iota(jnp.int32, (rows, rows), 1) == sent[0]
    home_att, home_ffn, back_ffn, back_att = (
        place_rows(match, value[:, 0].reshape(rows, width)) for value in (y_att, y_ffn, gh_ffn, gh_att)
    )
    for j in range(STREAMS):
        mixed = combine([dot_of(m0[k], column(m1, j)) for k in range(STREAMS)], first)
        streams_out[0, j] = mixed + dot_of(c0, column(m1, j)) * home_att + c1[j] * home_ffn
    for i in range(STREAMS):
        mixed = combine([dot_of(m0[i], column(m1, k)) for k in range(STREAMS)], second)
        grad_out[0, i] = mixed + dot_of(m0[i], a1) * back_ffn + a0[i] * back_att

    @pl.when((pl.program_id(0) == 0) & (pl.program_id(1) == 0))
    def _():
        dots_out[...] = jnp.zeros_like(dots_out)

    pairs = (
        [(value, home_att) for value in second]
        + [(value, home_ffn) for value in second]
        + [(value, back_ffn) for value in first]
        + [(value, back_att) for value in first]
        + [(home_att, back_ffn)]
    )
    for index, (left, right) in enumerate(pairs):
        dots_out[index] += fold(left * right)


def finish(hyper, streams, cotangent, sent, homes):
    micro, _, rows, width = streams.shape
    n_dp, _, slot, _ = homes[0].shape
    wide = 512
    block = pl.BlockSpec((1, STREAMS, rows, wide), lambda m, f: (m, 0, 0, f))
    home = pl.BlockSpec((n_dp, 1, slot, wide), lambda m, f: (0, m, 0, f))
    count = 4 * STREAMS + 1
    return pl.pallas_call(
        finish_kernel,
        grid=(micro, width // wide),
        in_specs=[SMEM, block, block, pl.BlockSpec((1, rows, 1), lambda m, f: (m, 0, 0))] + [home] * 4,
        out_specs=[block, block, pl.BlockSpec((count, 8, wide), lambda m, f: (0, 0, 0))],
        out_shape=[
            jax.ShapeDtypeStruct(streams.shape, FULL),
            jax.ShapeDtypeStruct(streams.shape, FULL),
            jax.ShapeDtypeStruct((count, 8, wide), FULL),
        ],
        compiler_params=pltpu.CompilerParams(vmem_limit_bytes=ROOM),
    )(hyper, streams, cotangent, sent[:, :, None], *homes)


def turn(values_in, cosine, sine):
    half = HEAD // 2
    swapped = jnp.concatenate([values_in[:, half:], values_in[:, :half]], axis=1)
    return values_in * cosine + swapped * sine


def dot_last(left, right):
    return lax.dot_general(left, right, (((1,), (1,)), ((), ())), preferred_element_type=jnp.float32)


def dot_first(left, right):
    return lax.dot_general(left, right, (((0,), (0,)), ((), ())), preferred_element_type=jnp.float32)


def allowed_pairs(start_ref, base, block, keys):
    column = lax.broadcasted_iota(jnp.int32, (block, keys), 1)
    row = lax.broadcasted_iota(jnp.int32, (block, keys), 0) + base
    return (column >= start_ref[pl.ds(base, block)]) & (column <= row)


def attend_head(head, q, k, v, start, out, log_out):
    length = q.shape[0]
    block = min(256, length)
    at = pl.ds(head * HEAD, HEAD)
    for base in range(0, length, block):
        keys = base + block
        rows, span = pl.ds(base, block), pl.ds(0, keys)
        scores = dot_last(q[rows, at], k[span, at]) * HEAD ** (-0.5)
        scores = jnp.where(allowed_pairs(start, base, block, keys), scores, -1e30)
        largest = jnp.max(scores, axis=1, keepdims=True)
        weights = jnp.exp(scores - largest)
        totals = jnp.sum(weights, axis=1, keepdims=True)
        probs = (weights * (1.0 / totals)).astype(LOW)
        out[rows, at] = jnp.dot(probs, v[span, at], preferred_element_type=FULL).astype(LOW)
        log_out[rows, pl.ds(head, 1)] = largest + jnp.log(totals)


def attend_head_back(head, grad, q, k, v, log_in, cosine, sine, start, units, k_sum, v_sum):
    length, width = q.shape
    block = min(256, length)
    at = pl.ds(head * HEAD, HEAD)
    k_sum[...] = jnp.zeros_like(k_sum)
    v_sum[...] = jnp.zeros_like(v_sum)
    for base in range(0, length, block):
        keys = base + block
        rows, span = pl.ds(base, block), pl.ds(0, keys)
        scores = dot_last(q[rows, at], k[span, at]) * HEAD ** (-0.5)
        probs = jnp.where(
            allowed_pairs(start, base, block, keys), jnp.exp(scores - log_in[rows, pl.ds(head, 1)]), 0.0
        )
        grad_probs = dot_last(grad[rows, at], v[span, at])
        inner = jnp.sum(probs * grad_probs, axis=1, keepdims=True)
        grad_scores = (probs * (grad_probs - inner) * HEAD ** (-0.5)).astype(LOW)
        grad_query = jnp.dot(grad_scores, k[span, at], preferred_element_type=FULL)
        units[rows, at] = turn(grad_query, cosine[rows], -sine[rows]).astype(LOW)
        k_sum[span] += dot_first(grad_scores, q[rows, at])
        v_sum[span] += dot_first(probs.astype(LOW), grad[rows, at])
    units[:, pl.ds(width + head * HEAD, HEAD)] = turn(k_sum[...], cosine[...], -sine[...]).astype(LOW)
    units[:, pl.ds(2 * width + head * HEAD, HEAD)] = v_sum[...].astype(LOW)


def remote(source, target, send_sem, recv_sem, device):
    return pltpu.make_async_remote_copy(
        src_ref=source,
        dst_ref=target,
        send_sem=send_sem,
        recv_sem=recv_sem,
        device_id=device,
        device_id_type=pl.DeviceIdType.MESH,
    )


def line_place():
    me = lax.axis_index("row")
    return me, me // 2, me % 2


def greet(pairs, plane=None):
    me, place, side = line_place()
    barrier = pltpu.get_barrier_semaphore()

    def signal(device):
        pl.semaphore_signal(barrier, inc=1, device_id=device, device_id_type=pl.DeviceIdType.MESH)

    signal({"row": me + 1 - 2 * side})

    @pl.when(place < pairs - 1)
    def _():
        signal({"row": me + 2})

    @pl.when(place > 0)
    def _():
        signal({"row": me - 2})

    count = 1
    if plane is not None:
        for offset in offsets(plane):
            signal(peer(plane, offset))
            count += 1
    last = pairs - 1
    neighbours = (place + last) // pairs + (2 * last - place) // pairs
    pl.semaphore_wait(barrier, count + neighbours)


def offsets(plane):
    n_dp, n_col = plane
    return [(d, c) for d in range(n_dp) for c in range(n_col) if (d, c) != (0, 0)]


def peer(plane, offset):
    n_dp, n_col = plane
    return {
        "dp": (lax.axis_index("dp") + offset[0]) % n_dp,
        "col": (lax.axis_index("col") + offset[1]) % n_col,
    }


class Exchange:
    def __init__(self, plane, source_of, target, sends, receives, keep):
        self.plane, self.source_of, self.target = plane, source_of, target
        self.sends, self.receives, self.keep = sends, receives, keep

    def move(self, offset):
        device = peer(self.plane, offset)
        return remote(
            self.source_of(device["dp"], device["col"]),
            self.target,
            self.sends.at[offset[0], offset[1]],
            self.receives.at[offset[0], offset[1]],
            device,
        )

    def stay(self):
        return pltpu.make_async_copy(
            self.source_of(lax.axis_index("dp"), lax.axis_index("col")), self.target, self.keep
        )

    def start(self):
        for offset in offsets(self.plane):
            self.move(offset).start()
        self.stay().start()

    def arrive(self):
        for offset in offsets(self.plane):
            self.move(offset).wait_recv()
        self.stay().wait()

    def leave(self):
        for offset in offsets(self.plane):
            self.move(offset).wait_send()


def exchange_sems(plane, count):
    return [DMA((count,) + plane), DMA((count,) + plane), DMA((count,))]


def work_block(work, slot, width, part, side):
    return work.at[
        pl.ds(pl.multiple_of(part * slot, slot), slot), pl.ds(pl.multiple_of(side * width, width), width)
    ]


def to_work(plane, home, work, sems, index):
    slot, width = home.shape[2:]
    return Exchange(
        plane,
        lambda b, c: home.at[b, c],
        work_block(work, slot, width, lax.axis_index("dp"), lax.axis_index("col")),
        sems[0].at[index],
        sems[1].at[index],
        sems[2].at[index],
    )


def to_home(plane, work, home, sems, index):
    slot, width = home.shape[2:]
    return Exchange(
        plane,
        lambda b, c: work_block(work, slot, width, b, c),
        home.at[lax.axis_index("dp"), lax.axis_index("col")],
        sems[0].at[index],
        sems[1].at[index],
        sems[2].at[index],
    )


class Gather:
    def __init__(self, pairs, cuts, own, out, sems):
        self.pairs, self.cuts, self.own, self.out = pairs, cuts, own, out
        self.right, self.left, self.twin_send, self.line, self.twin_recv, self.keep = sems
        self.height = own.shape[0] // cuts

    def piece(self, ref, cut):
        return ref.at[pl.ds(cut * self.height, self.height)]

    def move(self, row, sends, receives, origin, cut, first):
        _, _, side = line_place()
        block = self.piece(self.out.at[origin * 2 + side], cut)
        return remote(
            self.piece(self.own, cut) if first else block,
            block,
            sends.at[origin, cut],
            receives.at[origin, cut],
            {"row": row},
        )

    def to_twin(self, origin, cut, first=False):
        me, _, side = line_place()
        return self.move(me + 1 - 2 * side, self.twin_send, self.twin_recv, origin, cut, first)

    def to_right(self, origin, cut, first=False):
        return self.move(line_place()[0] + 2, self.right, self.line, origin, cut, first)

    def to_left(self, origin, cut, first=False):
        return self.move(line_place()[0] - 2, self.left, self.line, origin, cut, first)

    def stay(self):
        return pltpu.make_async_copy(self.own, self.out.at[line_place()[0]], self.keep)

    def start(self):
        _, place, _ = line_place()
        for cut in range(self.cuts):
            @pl.when(place < self.pairs - 1)
            def _():
                self.to_right(place, cut, True).start()

            @pl.when(place > 0)
            def _():
                self.to_left(place, cut, True).start()

        for cut in range(self.cuts):
            self.to_twin(place, cut, True).start()
        self.stay().start()

    def step(self, step, cut):
        _, place, _ = line_place()

        @pl.when(place >= step)
        def _():
            origin = place - step
            self.to_right(origin, cut).wait_recv()

            @pl.when(place < self.pairs - 1)
            def _():
                self.to_right(origin, cut).start()

            self.to_twin(origin, cut).start()

        @pl.when(place + step <= self.pairs - 1)
        def _():
            origin = place + step
            self.to_left(origin, cut).wait_recv()

            @pl.when(place > 0)
            def _():
                self.to_left(origin, cut).start()

            self.to_twin(origin, cut).start()

    def twin_arrive(self, origin):
        me, _, side = line_place()
        for cut in range(self.cuts):
            other = self.piece(self.out.at[origin * 2 + 1 - side], cut)
            remote(
                other,
                other,
                self.twin_send.at[origin, cut],
                self.twin_recv.at[origin, cut],
                {"row": me + 1 - 2 * side},
            ).wait_recv()

    def finish(self):
        self.stay().wait()
        for origin in range(self.pairs):
            self.twin_arrive(origin)
        self.leave()

    def leave(self):
        _, place, _ = line_place()
        for origin in range(self.pairs):
            for cut in range(self.cuts):
                self.to_twin(origin, cut).wait_send()

                @pl.when((place < self.pairs - 1) & (origin <= place))
                def _():
                    self.to_right(origin, cut).wait_send()

                @pl.when((place > 0) & (origin >= place))
                def _():
                    self.to_left(origin, cut).wait_send()


def gather_sems(pairs, cuts):
    return [DMA((pairs, cuts))] * 5 + [DMA]


def inner_order(pairs, cuts, inner):
    near = [(True, dest, cut) for dest in range(pairs - 1, inner, -1) for cut in range(cuts)]
    far = [(False, dest, cut) for dest in range(inner) for cut in range(cuts)]
    hops = pairs - 1 - 2 * inner
    timed = [(index, 0) + one for index, one in enumerate(near)]
    timed += [(index + hops, 1) + one for index, one in enumerate(far)]
    return [one[2:] for one in sorted(timed, key=lambda one: one[:2])]


class Scatter:
    def __init__(self, pairs, cuts, part, buffers, sems):
        self.pairs, self.cuts, self.part = pairs, cuts, part
        self.twin, self.from_left, self.from_right = buffers[:3]
        self.own = buffers[3] if len(buffers) > 3 else None
        (
            self.right_send,
            self.left_send,
            self.twin_send,
            self.right_recv,
            self.left_recv,
            self.twin_recv,
            self.loaded,
        ) = sems
        self.height = part.shape[1] // cuts

    def span(self, cut):
        return pl.ds(cut * self.height, self.height)

    def mine(self, dest, cut):
        _, _, side = line_place()
        if self.own is None:
            return self.part.at[dest * 2 + side, self.span(cut)]
        return self.own.at[dest, self.span(cut)]

    def load(self, dest, cut):
        _, _, side = line_place()
        return pltpu.make_async_copy(
            self.part.at[dest * 2 + side, self.span(cut)], self.mine(dest, cut), self.loaded.at[dest, cut]
        )

    def to_twin(self, dest, cut):
        me, _, side = line_place()
        return remote(
            self.part.at[dest * 2 + 1 - side, self.span(cut)],
            self.twin.at[dest, self.span(cut)],
            self.twin_send.at[dest, cut],
            self.twin_recv.at[dest, cut],
            {"row": me + 1 - 2 * side},
        )

    def to_right(self, dest, cut):
        return remote(
            self.mine(dest, cut),
            self.from_left.at[dest, self.span(cut)],
            self.right_send.at[dest, cut],
            self.right_recv.at[dest, cut],
            {"row": line_place()[0] + 2},
        )

    def to_left(self, dest, cut):
        return remote(
            self.mine(dest, cut),
            self.from_right.at[dest, self.span(cut)],
            self.left_send.at[dest, cut],
            self.left_recv.at[dest, cut],
            {"row": line_place()[0] - 2},
        )

    def order(self):
        order = []
        for step in range(self.pairs):
            for dest in (self.pairs - 1 - step, step):
                if dest not in order:
                    order.append(dest)
        return order

    def offer(self, dest):
        for cut in range(self.cuts):
            self.to_twin(dest, cut).start()
            if self.own is not None:
                self.load(dest, cut).start()

    def start(self):
        for dest in self.order():
            self.offer(dest)

    def here(self, dest, cut):
        return self.mine(dest, cut)[...].astype(FULL) + self.twin[dest, self.span(cut)].astype(FULL)

    def flows(self, step, place):
        last = self.pairs - 1
        return (
            (last - step, place < last - step, place == 0, self.from_left, self.to_right),
            (step, place > step, place == last, self.from_right, self.to_left),
        )

    def begin(self):
        _, place, _ = line_place()
        ready = []
        for step in range(self.pairs - 1):
            for dest, sending, first, _, copy in self.flows(step, place):
                for cut in range(self.cuts):
                    if (dest, cut) not in ready:
                        ready.append((dest, cut))
                        self.to_twin(dest, cut).wait_recv()
                        if self.own is not None:
                            self.load(dest, cut).wait()

                    @pl.when(sending & first)
                    def _():
                        self.mine(dest, cut)[...] = self.here(dest, cut).astype(LOW)
                        copy(dest, cut).start()

    def pass_on(self, dest, cut, rightward):
        copy, arrived = (self.to_right, self.from_left) if rightward else (self.to_left, self.from_right)
        copy(dest, cut).wait_recv()
        self.mine(dest, cut)[...] = (
            self.here(dest, cut) + arrived[dest, self.span(cut)].astype(FULL)
        ).astype(LOW)
        copy(dest, cut).start()

    def poll(self, index):
        _, place, _ = line_place()
        last = self.pairs - 1
        for inner in range(1, self.pairs // 2):
            order = inner_order(self.pairs, self.cuts, inner)
            if index < len(order):
                near, dest, cut = order[index]

                @pl.when(place == inner)
                def _():
                    self.pass_on(dest, cut, near)

                @pl.when(place == last - inner)
                def _():
                    self.pass_on(last - dest, cut, not near)

    def polls(self):
        return max(
            len(inner_order(self.pairs, self.cuts, inner)) for inner in range(1, self.pairs // 2)
        )

    def finish(self, total):
        _, place, _ = line_place()
        last = self.pairs - 1
        for cut in range(self.cuts):
            span = self.span(cut)
            total[span] = self.here(place, cut)

            @pl.when(place > 0)
            def _():
                self.to_right(place, cut).wait_recv()
                total[span] += self.from_left[place, span].astype(FULL)

            @pl.when(place < last)
            def _():
                self.to_left(place, cut).wait_recv()
                total[span] += self.from_right[place, span].astype(FULL)

        for dest in range(self.pairs):
            for cut in range(self.cuts):
                self.to_twin(dest, cut).wait_send()

                @pl.when(place < dest)
                def _():
                    self.to_right(dest, cut).wait_send()

                @pl.when(place > dest)
                def _():
                    self.to_left(dest, cut).wait_send()


def scatter_buffers(pairs, rows, width, loaded=True):
    return [pltpu.VMEM((pairs, rows, width), LOW)] * (4 if loaded else 3)


def scatter_sems(pairs, cuts):
    return [DMA((pairs, cuts))] * 7


class PlaneScatter:
    def __init__(self, block_of, out, square, buffers, sems):
        self.block_of, self.out, self.square = block_of, out, square
        self.arrived, self.mine, self.onward, self.final = buffers
        self.send, self.recv, self.loaded, self.send_on, self.recv_on = sems
        self.height = out.shape[-2] // 2

    def places(self, half, index):
        d, c = lax.axis_index("dp"), lax.axis_index("col")
        if half == 0:
            there = 1 - c if index == 0 else c
            return {"dp": 1 - d}, self.block_of(there, 1 - d, 0), self.block_of(there, d, 0)
        there = 1 - d if index == 0 else d
        return {"col": 1 - c}, self.block_of(1 - c, there, 1), self.block_of(c, there, 1)

    def move(self, half, index):
        device, block, _ = self.places(half, index)
        return remote(
            block, self.arrived.at[half, index], self.send.at[half, index], self.recv.at[half, index], device
        )

    def load(self, half, index):
        _, _, block = self.places(half, index)
        return pltpu.make_async_copy(block, self.mine.at[half, index], self.loaded.at[half, index])

    def move_on(self, half):
        device = (
            {"col": 1 - lax.axis_index("col")} if half == 0 else {"dp": 1 - lax.axis_index("dp")}
        )
        return remote(
            self.onward.at[half], self.final.at[half], self.send_on.at[half], self.recv_on.at[half], device
        )

    def start(self):
        for index in range(2):
            for half in range(2):
                self.move(half, index).start()
                if self.mine is not None:
                    self.load(half, index).start()

    def sum_of(self, half, index):
        self.move(half, index).wait_recv()
        if self.mine is None:
            _, _, block = self.places(half, index)
            mine = block[...]
        else:
            self.load(half, index).wait()
            mine = self.mine[half, index]
        return mine.astype(FULL) + self.arrived[half, index].astype(FULL)

    def forward(self):
        for half in range(2):
            self.onward[half] = self.sum_of(half, 0).astype(LOW)
            self.move_on(half).start()

    def finish(self):
        for half in range(2):
            total = self.sum_of(half, 1)
            self.move_on(half).wait_recv()
            total = total + self.final[half].astype(FULL)
            width = self.out.shape[-1]
            for index in range(self.out.shape[0]):
                self.out[index, pl.ds(half * self.height, self.height)] = total[
                    :, index * width : (index + 1) * width
                ]
            squares = fold(total * total)
            self.square[half] = sum(
                squares[:, at : at + 128] for at in range(0, squares.shape[1], 128)
            )
        for half in range(2):
            for index in range(2):
                self.move(half, index).wait_send()
            self.move_on(half).wait_send()


class PlaneGather:
    def __init__(self, own, block_of, sems):
        self.own, self.block_of = own, block_of
        self.send, self.recv, self.send_on, self.recv_on, self.keep = sems
        self.height = own.shape[0] // 2

    def direct(self, axis, half):
        d, c = lax.axis_index("dp"), lax.axis_index("col")
        return remote(
            self.own.at[pl.ds(half * self.height, self.height)],
            self.block_of(c, d, half),
            self.send.at[axis, half],
            self.recv.at[axis, half],
            {"dp": 1 - d} if axis == 0 else {"col": 1 - c},
        )

    def onward(self, half):
        d, c = lax.axis_index("dp"), lax.axis_index("col")
        block = self.block_of(c, 1 - d, 0) if half == 0 else self.block_of(1 - c, d, 1)
        return remote(
            block,
            block,
            self.send_on.at[half],
            self.recv_on.at[half],
            {"col": 1 - c} if half == 0 else {"dp": 1 - d},
        )

    def stay(self, half):
        d, c = lax.axis_index("dp"), lax.axis_index("col")
        return pltpu.make_async_copy(
            self.own.at[pl.ds(half * self.height, self.height)], self.block_of(c, d, half), self.keep.at[half]
        )

    def start(self):
        for half in range(2):
            self.direct(half, half).start()
        for half in range(2):
            self.stay(half).start()

    def forward(self):
        for half in range(2):
            self.direct(half, half).wait_recv()
            self.onward(half).start()
            self.direct(1 - half, half).start()

    def finish(self):
        for half in range(2):
            self.direct(1 - half, half).wait_recv()
            self.onward(half).wait_recv()
            self.stay(half).wait()
        for half in range(2):
            for axis in range(2):
                self.direct(axis, half).wait_send()
            self.onward(half).wait_send()


def plane_gather_sems():
    return [DMA((2, 2)), DMA((2, 2)), DMA((2,)), DMA((2,)), DMA((2,))]


def by_rows(part, height):
    half_height = height // 2
    return lambda c, d, half: part.at[pl.ds((c * 2 + d) * height + half * half_height, half_height)]


def by_owner(part, height):
    half_height = height // 2
    return lambda c, d, half: part.at[c, d, pl.ds(half * half_height, half_height)]


def by_tiles(part, height, width):
    half_height = height // 2
    return lambda c, d, half: part.at[
        pl.ds(d * height + half * half_height, half_height), pl.ds(pl.multiple_of(c * width, width), width)
    ]


CUTS = 2
SUM_CUTS = 4


def call_remote(kernel, collective, **options):
    return pl.pallas_call(
        kernel,
        compiler_params=pltpu.CompilerParams(
            collective_id=collective, has_side_effects=True, vmem_limit_bytes=ROOM
        ),
        **options,
    )


def block_view(whole, rows, width):
    return by_rows(whole, rows) if whole.shape[1] == width else by_tiles(whole, rows, width)


def plane_gathers(weights, wholes, sems):
    return [
        PlaneGather(weight, block_view(whole, *weight.shape), sems[5 * index : 5 * index + 5])
        for index, (weight, whole) in enumerate(zip(weights, wholes))
    ]


def whole_shapes(weights):
    return [
        jax.ShapeDtypeStruct((4 * rows, width) if width != D // 2 else (2 * rows, 2 * width), LOW)
        for rows, width in (weight.shape for weight in weights)
    ]


def enter_kernel(plane, pairs, count, h_home, gy_home, start, inverse, w_in, *rest):
    weights, rest = rest[:count], rest[count:]
    (rows_out, h, gy, cosine, sine, w_low), rest = rest[:6], rest[6:]
    wholes, rest = rest[:count], rest[count:]
    (own, w_full, load_sem), plane_sems, line_sems, rest = rest[:3], rest[3:6], rest[6:12], rest[12:]
    load = pltpu.make_async_copy(w_in, w_full, load_sem)
    load.start()
    gathers = plane_gathers(weights, wholes, rest)
    greet(pairs, plane)
    first = to_work(plane, h_home, h, plane_sems, 0)
    second = to_work(plane, gy_home, gy, plane_sems, 1)
    first.start()
    first.arrive()
    for one in gathers:
        one.start()
    own[...] = norm_forward(h[...])[0].astype(LOW)
    gather = Gather(pairs, CUTS, own, rows_out, line_sems)
    gather.start()

    def cast():
        load.wait()
        width = w_in.shape[2]
        for index in range(w_in.shape[0]):
            w_low[:, index * width : (index + 1) * width] = w_full[index].astype(LOW)

    def angles():
        places = lax.broadcasted_iota(jnp.int32, cosine.shape, 0)
        return (places - start[...]).astype(FULL) * inverse[...]

    def put_cosine():
        cosine[...] = jnp.cos(angles())

    def put_sine():
        sign = 2 * (lax.broadcasted_iota(jnp.int32, sine.shape, 1) // (HEAD // 2)) - 1
        sine[...] = jnp.sin(angles()) * sign.astype(FULL)

    fillers = [cast, put_cosine, put_sine]
    for step in range(1, pairs):
        for cut in range(CUTS):
            if fillers:
                fillers.pop(0)()
            gather.step(step, cut)
        if step == 1:
            second.start()
        if step == 2:
            for one in gathers:
                one.forward()
    gather.finish()
    for one in gathers:
        one.finish()
    second.arrive()
    second.leave()
    first.leave()


def enter(plane, pairs, h_home, gy_home, start, inverse, w_in, weights, collective):
    n_dp, n_col, slot, width = h_home.shape
    rows = n_dp * slot
    work = jax.ShapeDtypeStruct((rows, n_col * width), FULL)
    table = jax.ShapeDtypeStruct((start.shape[0], HEAD), FULL)
    outs = call_remote(
        functools.partial(enter_kernel, plane, pairs, len(weights)),
        collective,
        in_specs=[ANY, ANY, VMEM, VMEM] + [ANY] * (1 + len(weights)),
        out_specs=[ANY, VMEM, ANY, VMEM, VMEM, VMEM] + [ANY] * len(weights),
        out_shape=[
            jax.ShapeDtypeStruct((2 * pairs, rows, n_col * width), LOW),
            work,
            jax.ShapeDtypeStruct(work.shape, gy_home.dtype),
            table,
            table,
            jax.ShapeDtypeStruct((w_in.shape[1], w_in.shape[0] * w_in.shape[2]), LOW),
        ]
        + whole_shapes(weights),
        scratch_shapes=[pltpu.VMEM(work.shape, LOW), pltpu.VMEM(w_in.shape, FULL), DMA]
        + exchange_sems(plane, 2)
        + gather_sems(pairs, CUTS)
        + plane_gather_sems() * len(weights),
    )(h_home, gy_home, start, inverse, w_in, *weights)
    return [outs[0].reshape(2 * pairs * rows, n_col * width)] + list(outs[1:6]), outs[6:]


def attend_kernel(
    plane, pairs, count, x_in, w_in, w_out, cosine, sine, start, gathered, mix_home,
    *rest,
):
    weights, rest = rest[:count], rest[count:]
    (rows_out, mix, heads_out, log_out, q, k, v, low_out, total), rest = rest[:9], rest[9:]
    wholes, rest = rest[:count], rest[count:]
    (x, part, load_sem), plane_sems, scratch, line_sems = rest[:3], rest[3:6], rest[6:16], rest[16:22]
    scatter = Scatter(pairs, SUM_CUTS, part, scratch[:3], scratch[3:])
    gather = Gather(pairs, CUTS, gathered, rows_out, line_sems)
    gathers = plane_gathers(weights, wholes, rest[22:])
    load = pltpu.make_async_copy(x_in, x, load_sem)
    load.start()
    greet(pairs, plane)
    gather.start()
    exchange = to_work(plane, mix_home, mix, plane_sems, 0)
    for one in gathers:
        one.start()
    load.wait()
    width = q.shape[1]
    heads = width // HEAD
    for index, out in enumerate((q, k, v)):
        value = jnp.dot(x[...], w_in[:, index * width : (index + 1) * width], preferred_element_type=FULL)
        for head in range(heads):
            at = slice(head * HEAD, (head + 1) * HEAD)
            one = value[:, at]
            out[:, at] = (one if index == 2 else turn(one, cosine[...], sine[...])).astype(LOW)
    for head in range(heads):
        attend_head(head, q, k, v, start, heads_out, log_out)
        if head == 0:
            for cut in range(CUTS):
                gather.step(1, cut)
    for one in gathers:
        one.forward()
    exchange.start()
    rows = total.shape[0]
    for dest in scatter.order():
        for owner in (2 * dest, 2 * dest + 1):
            part[owner] = jnp.dot(
                heads_out[pl.ds(owner * rows, rows)], w_out[...], preferred_element_type=FULL
            ).astype(LOW)
        scatter.offer(dest)
    scatter.begin()
    polls = list(range(scatter.polls()))
    for step in range(2, pairs):
        for cut in range(CUTS):
            gather.step(step, cut)
            for index in polls[:2]:
                scatter.poll(index)
            polls = polls[2:]
    for index in polls:
        scatter.poll(index)
    scatter.finish(total)
    low_out[...] = total[...].astype(LOW)
    gather.finish()
    for one in gathers:
        one.finish()
    exchange.arrive()
    exchange.leave()


def attend(plane, pairs, x, w_in, w_out, cosine, sine, start, gathered, mix_home, weights, collective):
    tokens, width = x.shape
    rows = tokens // (2 * pairs)
    local = w_out.shape[0]
    low = jax.ShapeDtypeStruct((tokens, local), LOW)
    full = jax.ShapeDtypeStruct((rows, width), FULL)
    outs = call_remote(
        functools.partial(attend_kernel, plane, pairs, len(weights)),
        collective,
        in_specs=[ANY, VMEM, VMEM, VMEM, VMEM, VMEM, ANY, ANY] + [ANY] * len(weights),
        out_specs=[ANY, ANY] + [VMEM] * 7 + [ANY] * len(weights),
        out_shape=[
            jax.ShapeDtypeStruct((2 * pairs, rows, width), LOW),
            full,
            low,
            jax.ShapeDtypeStruct((tokens, local // HEAD), FULL),
            low,
            low,
            low,
            jax.ShapeDtypeStruct((rows, width), LOW),
            full,
        ]
        + whole_shapes(weights),
        scratch_shapes=[pltpu.VMEM(x.shape, LOW), pltpu.VMEM((2 * pairs, rows, width), LOW), DMA]
        + exchange_sems(plane, 1)
        + scatter_buffers(pairs, rows, width, False)
        + scatter_sems(pairs, SUM_CUTS)
        + gather_sems(pairs, CUTS)
        + plane_gather_sems() * len(weights),
    )(x, w_in, w_out, cosine, sine, start, gathered, mix_home, *weights)
    return [outs[0].reshape(tokens, width)] + list(outs[1:9]), outs[9:]


def back_kernel(
    pairs, plane, gathered, part, x_in, units_in, hid_in, gy_in,
    rows_out, low_out, out_grad, in_sum, square,
    total, left, right, grad, arrived, onward, final, load_sem,
    send, recv, loaded, send_on, recv_on, *rest,
):
    d, c = lax.axis_index("dp"), lax.axis_index("col")
    scatter = Scatter(pairs, SUM_CUTS, part, rest[:4], rest[4:11])
    gather = Gather(pairs, CUTS, gathered, rows_out, rest[11:])
    height = in_sum.shape[1]
    one = PlaneScatter(
        by_rows(grad, height),
        in_sum,
        square,
        (arrived, None, onward, final),
        (send, recv, loaded, send_on, recv_on),
    )
    narrow = hid_in.shape[1]
    loads = [
        pltpu.make_async_copy(x_in, left, load_sem.at[0]),
        pltpu.make_async_copy(units_in, right, load_sem.at[1]),
        pltpu.make_async_copy(hid_in, left.at[:, pl.ds(0, narrow)], load_sem.at[2]),
        pltpu.make_async_copy(gy_in, right, load_sem.at[3]),
    ]
    loads[0].start()
    loads[1].start()
    greet(pairs, plane)
    gather.start()
    scatter.start()

    def in_block(there, across):
        @pl.loop(0, height // UNIT)
        def _(index):
            at = pl.multiple_of((there * 2 + across) * height + index * UNIT, UNIT)
            grad[pl.ds(at, UNIT)] = dot_first(left[:, pl.ds(at, UNIT)], right[...]).astype(LOW)

    owned, width = out_grad.shape[2:]

    def out_block(part):
        @pl.loop(0, owned // UNIT)
        def _(index):
            at = pl.multiple_of(part * owned + index * UNIT, UNIT)
            tile = dot_first(left[:, pl.ds(at, UNIT)], right[...]).astype(LOW)
            for side in range(2):
                out_grad[side, part, pl.ds(pl.multiple_of(index * UNIT, UNIT), UNIT)] = tile[
                    :, side * width : (side + 1) * width
                ]

    each = -(-scatter.polls() // (CUTS * (pairs - 1)))

    def both(step):
        for cut in range(CUTS):
            gather.step(step + 1, cut)
            for index in range(each):
                scatter.poll((step * CUTS + cut) * each + index)

    scatter.begin()
    loads[0].wait()
    loads[1].wait()
    in_block(1 - c, 1 - d)
    one.move(0, 0).start()
    one.move(1, 0).start()
    in_block(c, 1 - d)
    one.move(0, 1).start()
    in_block(1 - c, d)
    one.move(1, 1).start()
    both(0)
    in_block(c, d)
    loads[2].start()
    loads[3].start()
    both(1)
    loads[2].wait()
    loads[3].wait()
    out_block(0)
    one.forward()
    out_block(1)
    for step in range(2, pairs - 1):
        both(step)
    scatter.finish(total)
    low_out[...] = total[...].astype(LOW)
    gather.finish()
    one.finish()


def back_gather(pairs, plane, gathered, partial, x, units, hid, gy, collective):
    rows, width = gathered.shape
    wide, narrow = units.shape[1], hid.shape[1]
    height = width // 4
    half = (height // 2, wide)
    whole = jax.ShapeDtypeStruct((2 * pairs, rows, width), LOW)
    outs = call_remote(
        functools.partial(back_kernel, pairs, plane),
        collective,
        in_specs=[ANY] * 6,
        out_specs=[ANY, VMEM, VMEM, VMEM, VMEM],
        out_shape=[
            whole,
            jax.ShapeDtypeStruct((rows, width), LOW),
            jax.ShapeDtypeStruct((2, 2, narrow // 2, width // 2), LOW),
            jax.ShapeDtypeStruct((2, height, wide // 2), FULL),
            jax.ShapeDtypeStruct((2, 8, 128), FULL),
        ],
        scratch_shapes=[
            pltpu.VMEM((rows, width), FULL),
            pltpu.VMEM(x.shape, LOW),
            pltpu.VMEM(units.shape, LOW),
            pltpu.VMEM((width, wide), LOW),
            pltpu.VMEM((2, 2) + half, LOW),
            pltpu.VMEM((2,) + half, LOW),
            pltpu.VMEM((2,) + half, LOW),
            DMA((4,)),
            DMA((2, 2)),
            DMA((2, 2)),
            DMA((2, 2)),
            DMA((2,)),
            DMA((2,)),
        ]
        + scatter_buffers(pairs, rows, width)
        + scatter_sems(pairs, SUM_CUTS)
        + gather_sems(pairs, CUTS),
    )(gathered, partial.reshape(whole.shape), x, units, hid, gy)
    return [outs[0].reshape(2 * pairs * rows, width)] + list(outs[1:])


def row_gather_kernel(pairs, gathered, rows_out, *line_sems):
    gather = Gather(pairs, CUTS, gathered, rows_out, line_sems)
    greet(pairs)
    gather.start()
    for step in range(1, pairs):
        for cut in range(CUTS):
            gather.step(step, cut)
    gather.finish()


def row_gather(pairs, gathered, collective):
    rows, width = gathered.shape
    out = call_remote(
        functools.partial(row_gather_kernel, pairs),
        collective,
        in_specs=[ANY],
        out_specs=ANY,
        out_shape=jax.ShapeDtypeStruct((2 * pairs, rows, width), LOW),
        scratch_shapes=gather_sems(pairs, CUTS),
    )(gathered)
    return out.reshape(2 * pairs * rows, width)


def arrival(place, pairs, step):
    chosen = jnp.int32(0)
    for here in range(pairs):
        order = sorted(range(pairs), key=lambda there: abs(there - here))
        chosen = jnp.where(place == here, order[step], chosen)
    return chosen


UNIT = 256


def ffn_kernel(
    plane, pairs, hyper, mix, branch, back_home, w_in, w_out, gy_rows,
    rows_out, hid_out, units_out, y_out, h, gh_out, gy_out,
    own, x, wd, gy, hid, units, y, part, twin, from_left, from_right, total, upstream,
    load_sem, gy_sem, hid_sem, units_sem, y_sem, x_sem,
    twin_send, twin_recv, right_send, right_recv, left_send, left_recv, *rest,
):
    plane_sems, line_sems = rest[:3], rest[3:]
    me, place, side = line_place()
    last = pairs - 1
    rows = own.shape[0]
    height = rows // SUM_CUTS
    half = units.shape[2] // 2
    n_col, n_dp, owned, width = w_out.shape
    tiles = [
        pltpu.make_async_copy(
            w_out.at[c, d],
            wd.at[pl.ds(d * owned, owned), pl.ds(c * width, width)],
            load_sem.at[2 + c * n_dp + d],
        )
        for c in range(n_col)
        for d in range(n_dp)
    ]
    for tile in tiles:
        tile.start()
    greet(pairs, plane)
    loads = [
        pltpu.make_async_copy(mix, h, load_sem.at[0]),
        pltpu.make_async_copy(branch, total, load_sem.at[1]),
    ]
    for load in loads:
        load.start()
    exchange = to_work(plane, back_home, upstream, plane_sems, 0)
    exchange.start()
    order = [arrival(place, pairs, step) for step in range(pairs)]

    def load_gy(step):
        return pltpu.make_async_copy(gy_rows.at[order[step]], gy.at[step % 2], gy_sem.at[step % 2])

    load_gy(0).start()
    loads[0].wait()
    loads[1].wait()
    h[...] = h[...] + branch_weight(hyper) * total[...]
    own[...] = norm_forward(h[...])[0].astype(LOW)
    gather = Gather(pairs, CUTS, own, x, line_sems)
    gather.start()
    for tile in tiles:
        tile.wait()

    def saves(step):
        slot = step % 2
        return [
            pltpu.make_async_copy(hid.at[slot], hid_out.at[order[step]], hid_sem.at[slot]),
            pltpu.make_async_copy(units.at[slot], units_out.at[order[step]], units_sem.at[slot]),
            pltpu.make_async_copy(y.at[slot], y_out.at[order[step]], y_sem.at[slot]),
        ]

    def save_x(step):
        return pltpu.make_async_copy(
            x.at[pl.ds(order[step] * 2, 2)], rows_out.at[pl.ds(order[step] * 2, 2)], x_sem.at[step]
        )

    def work(step):
        slot = step % 2
        x_block = x.at[pl.ds(order[step] * 2, 2)]

        @pl.loop(0, half // UNIT)
        def _(unit):
            at = pl.multiple_of(unit * UNIT, UNIT)
            rows_in = x_block[...].reshape(2 * rows, -1)
            gate = jnp.dot(rows_in, w_in[:, pl.ds(at, UNIT)], preferred_element_type=FULL)
            up = jnp.dot(rows_in, w_in[:, pl.ds(half + at, UNIT)], preferred_element_type=FULL)
            grad = dot_last(gy[slot], wd[pl.ds(at, UNIT)])
            sigma = 1.0 / (1.0 + jnp.exp(-gate))
            silu = gate * sigma
            hid[slot, :, pl.ds(at, UNIT)] = (silu * up).astype(LOW)
            units[slot, :, pl.ds(at, UNIT)] = (
                grad * up * sigma * (1.0 + gate * (1.0 - sigma))
            ).astype(LOW)
            units[slot, :, pl.ds(half + at, UNIT)] = (grad * silu).astype(LOW)

        @pl.loop(0, D // UNIT)
        def _(unit):
            at = pl.multiple_of(unit * UNIT, UNIT)
            tile = dot_last(units[slot], w_in[pl.ds(at, UNIT)]).astype(LOW)
            part[pl.ds(order[step] * 2, 2), :, pl.ds(at, UNIT)] = tile.reshape(2, rows, UNIT)

    def work_out(step):
        slot = step % 2

        @pl.loop(0, D // UNIT)
        def _(unit):
            at = pl.multiple_of(unit * UNIT, UNIT)
            tile = jnp.dot(hid[slot], wd[:, pl.ds(at, UNIT)], preferred_element_type=FULL)
            y[slot, :, pl.ds(at, UNIT)] = tile.astype(LOW)

    def to_twin(dest):
        return remote(
            part.at[dest * 2 + 1 - side],
            twin.at[dest],
            twin_send.at[dest],
            twin_recv.at[dest],
            {"row": me + 1 - 2 * side},
        )

    def line(dest, cut, rightward):
        span = pl.ds(cut * height, height)
        return remote(
            part.at[dest * 2 + side, span],
            (from_left if rightward else from_right).at[dest, span],
            (right_send if rightward else left_send).at[dest, cut],
            (right_recv if rightward else left_recv).at[dest, cut],
            {"row": me + 2 if rightward else me - 2},
        )

    def here(dest, span):
        return part[dest * 2 + side, span].astype(FULL) + twin[dest, span].astype(FULL)

    def send_first(step):
        dest = order[step]
        to_twin(dest).wait_recv()
        for at_end, rightward in ((place == 0, True), (place == last, False)):
            @pl.when(at_end & (dest != place))
            def _():
                for cut in range(SUM_CUTS):
                    span = pl.ds(cut * height, height)
                    part[dest * 2 + side, span] = here(dest, span).astype(LOW)
                    line(dest, cut, rightward).start()

    for step in range(pairs):
        if step > 0:
            for cut in range(CUTS):
                gather.step(step, cut)
        else:
            gather.stay().wait()
        if step + 1 < pairs:
            load_gy(step + 1).start()
        gather.twin_arrive(order[step])
        save_x(step).start()
        load_gy(step).wait()
        if step >= 2:
            for save in saves(step - 2):
                save.wait()
        work(step)
        to_twin(order[step]).start()
        if step > 0:
            send_first(step - 1)
        if step == pairs - 1:
            send_first(step)
        work_out(step)
        for save in saves(step):
            save.start()

    def pass_on(dest, cut, rightward):
        arrived = from_left if rightward else from_right
        span = pl.ds(cut * height, height)
        line(dest, cut, rightward).wait_recv()
        part[dest * 2 + side, span] = (here(dest, span) + arrived[dest, span].astype(FULL)).astype(LOW)
        line(dest, cut, rightward).start()

    for inner in range(1, pairs // 2):
        order_here = [(reach, cut, 0, True, reach) for reach in range(inner + 1, pairs) for cut in range(SUM_CUTS)]
        order_here += [
            (last - dest, cut + last - 2 * inner, 1, False, dest) for dest in range(inner) for cut in range(SUM_CUTS)
        ]
        for reach, at, late, near, dest in sorted(order_here):
            cut = at - (last - 2 * inner) * late

            @pl.when(place == inner)
            def _():
                pass_on(dest, cut, near)

            @pl.when(place == last - inner)
            def _():
                pass_on(last - dest, cut, not near)

    for cut in range(SUM_CUTS):
        span = pl.ds(cut * height, height)
        total[span] = here(place, span)

        @pl.when(place > 0)
        def _():
            line(place, cut, True).wait_recv()
            total[span] += from_left[place, span].astype(FULL)

        @pl.when(place < last)
        def _():
            line(place, cut, False).wait_recv()
            total[span] += from_right[place, span].astype(FULL)

    exchange.arrive()
    grad = norm_backward(total[...], h[...])
    gh_out[...] = grad.astype(LOW)
    gy_out[...] = (upstream[...] + branch_weight(hyper) * grad).astype(LOW)

    exchange.leave()
    gather.leave()
    for step in range(pairs):
        save_x(step).wait()
    for step in range(pairs - 2, pairs):
        for save in saves(step):
            save.wait()
    for dest in range(pairs):
        to_twin(dest).wait_send()
        for cut in range(SUM_CUTS):
            @pl.when(place < dest)
            def _():
                line(dest, cut, True).wait_send()

            @pl.when(place > dest)
            def _():
                line(dest, cut, False).wait_send()


def feed_forward(plane, pairs, hyper, mix, branch, back_home, w_in, w_out, gy_rows, collective):
    rows, width = mix.shape
    units = w_in.shape[1]
    half = units // 2
    low = jax.ShapeDtypeStruct((rows, width), LOW)

    def by_pair(last_width):
        return jax.ShapeDtypeStruct((pairs, 2 * rows, last_width), LOW)

    blocks = pltpu.VMEM((pairs, rows, width), LOW)
    full = pltpu.VMEM((rows, width), FULL)
    outs = call_remote(
        functools.partial(ffn_kernel, plane, pairs),
        collective,
        in_specs=[SMEM, ANY, ANY, ANY, VMEM, ANY, ANY],
        out_specs=[ANY, ANY, ANY, ANY, VMEM, VMEM, VMEM],
        out_shape=[
            jax.ShapeDtypeStruct((2 * pairs, rows, width), LOW),
            by_pair(half),
            by_pair(units),
            by_pair(width),
            jax.ShapeDtypeStruct((rows, width), FULL),
            low,
            low,
        ],
        scratch_shapes=[
            pltpu.VMEM((rows, width), LOW),
            pltpu.VMEM((2 * pairs, rows, width), LOW),
            pltpu.VMEM((half, width), LOW),
            pltpu.VMEM((2, 2 * rows, width), LOW),
            pltpu.VMEM((2, 2 * rows, half), LOW),
            pltpu.VMEM((2, 2 * rows, units), LOW),
            pltpu.VMEM((2, 2 * rows, width), LOW),
            pltpu.VMEM((2 * pairs, rows, width), LOW),
            blocks,
            blocks,
            blocks,
            full,
            full,
            DMA((2 + plane[0] * plane[1],)),
            DMA((2,)),
            DMA((2,)),
            DMA((2,)),
            DMA((2,)),
            DMA((pairs,)),
            DMA((pairs,)),
            DMA((pairs,)),
        ]
        + [DMA((pairs, SUM_CUTS))] * 4
        + exchange_sems(plane, 1)
        + gather_sems(pairs, CUTS),
    )(hyper, mix, branch, back_home, w_in, w_out, gy_rows.reshape(pairs, 2 * rows, width))
    tokens = 2 * pairs * rows
    return [value.reshape(tokens, -1) for value in outs[:4]] + list(outs[5:])


def leave_kernel(
    plane, pairs, in_kernel, gy_in, x_in, heads_in, log_in, q, k, v, cosine, sine, start, w_in, w_out, h,
    y_att, y_ffn, gh_ffn, *rest,
):
    if in_kernel:
        ffn_grad, rest = rest[0], rest[1:]
    homes, rest = rest[:4], rest[4:]
    if in_kernel:
        sums, rest = rest[:6], rest[6:]
    (grad_in, grad_out, rows_in, units, back, k_sum, v_sum, part, total, last, load_sem), rest = (
        rest[:11],
        rest[11:],
    )
    plane_sems, scratch, rest = rest[:3], rest[3:13], rest[13:]
    scatter = Scatter(pairs, SUM_CUTS, part, scratch[:3], scratch[3:])
    load_gy = pltpu.make_async_copy(gy_in, rows_in, load_sem.at[0])
    load_x = pltpu.make_async_copy(x_in, rows_in, load_sem.at[1])
    load_gy.start()
    planes = []
    if in_kernel:
        own_ffn, rest = rest[0], rest[1:]
        for index, block_of in enumerate(
            (
                by_owner(ffn_grad, sums[0].shape[1]),
                by_tiles(grad_out, *sums[2].shape[1:]),
                by_rows(grad_in, sums[4].shape[1]),
            )
        ):
            one = rest[8 * index : 8 * index + 8]
            planes.append(
                PlaneScatter(
                    block_of,
                    sums[2 * index],
                    sums[2 * index + 1],
                    (one[0], None if index else own_ffn, one[1], one[2]),
                    one[3:],
                )
            )
    greet(pairs, plane)
    ways = [
        to_home(plane, work, home, plane_sems, index)
        for index, (work, home) in enumerate(zip((y_att, y_ffn, gh_ffn, last), homes))
    ]
    for one in planes[:1]:
        one.start()
    for way in ways[:3]:
        way.start()
    load_gy.wait()
    back[...] = dot_last(rows_in[...], w_out[...]).astype(LOW)
    width = q.shape[1]
    for head in range(width // HEAD):
        attend_head_back(
            head, back, q, k, v, log_in, cosine, sine, start, units, k_sum, v_sum
        )
    rows = total.shape[0]
    for dest in scatter.order():
        for owner in (2 * dest, 2 * dest + 1):
            part[owner] = dot_last(units[pl.ds(owner * rows, rows)], w_in[...]).astype(LOW)
        scatter.offer(dest)
    scatter.begin()
    grad_out[...] = dot_first(heads_in[...], rows_in[...]).astype(LOW)
    load_x.start()
    for one in planes[1:2]:
        one.start()
    load_x.wait()
    quarter = D // SUM_CUTS
    polls = list(range(scatter.polls()))
    for cut in range(SUM_CUTS):
        for index in polls[:2]:
            scatter.poll(index)
        polls = polls[2:]

        @pl.loop(0, quarter // UNIT)
        def _(index):
            at = pl.multiple_of(cut * quarter + index * UNIT, UNIT)
            grad_in[pl.ds(at, UNIT)] = dot_first(rows_in[:, pl.ds(at, UNIT)], units[...]).astype(LOW)

    for one in planes[2:]:
        one.start()
    for one in planes[:1]:
        one.forward()
    for index in polls:
        scatter.poll(index)
    for one in planes[1:]:
        one.forward()
    scatter.finish(total)
    last[...] = norm_backward(total[...], h[...]).astype(last.dtype)
    ways[3].start()
    for one in planes:
        one.finish()
    for way in ways:
        way.arrive()
        way.leave()


def leave(
    plane, pairs, ffn_grad, gy, x, heads, log_totals, q, k, v, tables, w_in, w_out, h, works, collective
):
    in_kernel = len(ffn_grad) > 0
    rows, width = h.shape
    n_dp, n_col = plane
    tokens, local = q.shape
    home = jax.ShapeDtypeStruct((n_dp, n_col, rows // n_dp, width // n_col), works[0].dtype)
    grads = [(width, 3 * local), (local, width)]
    extra, planes = [], []
    if in_kernel:
        owned = [(1,) + ffn_grad[0].shape[2:], (1, local // 2, width // 2), (3, width // 4, local)]
        planes.append(pltpu.VMEM((2, 2, owned[0][1] // 2, owned[0][2]), LOW))
        for shape in owned:
            extra += [shape, (2, 8, 128)]
            half = (shape[1] // 2, shape[0] * shape[2])
            planes += [
                pltpu.VMEM((2, 2) + half, LOW),
                pltpu.VMEM((2,) + half, LOW),
                pltpu.VMEM((2,) + half, LOW),
                DMA((2, 2)),
                DMA((2, 2)),
                DMA((2, 2)),
                DMA((2,)),
                DMA((2,)),
            ]
    grad_refs = [pltpu.VMEM(shape, LOW) for shape in grads]
    grad_outs = [] if in_kernel else [jax.ShapeDtypeStruct(shape, LOW) for shape in grads]
    outs = call_remote(
        functools.partial(leave_kernel, plane, pairs, in_kernel),
        collective,
        in_specs=[ANY, ANY] + [VMEM] * 11 + [ANY] * (3 + len(ffn_grad)),
        out_specs=[ANY] * 4 + [VMEM] * (len(extra) + len(grad_outs)),
        out_shape=[home] * 4 + [jax.ShapeDtypeStruct(shape, FULL) for shape in extra] + grad_outs,
        scratch_shapes=(grad_refs if in_kernel else [])
        + [
            pltpu.VMEM(x.shape, LOW),
            pltpu.VMEM((tokens, 3 * local), LOW),
            pltpu.VMEM((tokens, local), LOW),
            pltpu.VMEM((tokens, HEAD), FULL),
            pltpu.VMEM((tokens, HEAD), FULL),
            pltpu.VMEM((2 * pairs, rows, width), LOW),
            pltpu.VMEM((rows, width), FULL),
            pltpu.VMEM((rows, width), works[0].dtype),
            DMA((2,)),
        ]
        + exchange_sems(plane, 4)
        + scatter_buffers(pairs, rows, width, False)
        + scatter_sems(pairs, SUM_CUTS)
        + planes,
    )(gy, x, heads, log_totals, q, k, v, *tables, w_in, w_out, h, *works, *ffn_grad)
    return outs[:4], outs[4:]


def total_kernel(plane, count, own, out, line, flat, line_send, line_recv, flat_send, flat_recv):
    n_dp, n_col = plane
    me = lax.axis_index("row")
    here = lax.axis_index("dp") * n_col + lax.axis_index("col")
    barrier = pltpu.get_barrier_semaphore()
    rows = [(me + step) % count for step in range(1, count)]
    for row in rows:
        pl.semaphore_signal(barrier, inc=1, device_id={"row": row}, device_id_type=pl.DeviceIdType.MESH)
    for offset in offsets(plane):
        pl.semaphore_signal(
            barrier, inc=1, device_id=peer(plane, offset), device_id_type=pl.DeviceIdType.MESH
        )
    pl.semaphore_wait(barrier, count - 1 + n_dp * n_col - 1)
    line[me] = own[...]
    copies = [
        remote(line.at[me], line.at[me], line_send.at[step], line_recv.at[step], {"row": row})
        for step, row in enumerate(rows)
    ]
    for copy in copies:
        copy.start()
    for copy in copies:
        copy.wait()
    sums = line[0]
    for row in range(1, count):
        sums = sums + line[row]
    flat[here] = sums
    copies = [
        remote(
            flat.at[here],
            flat.at[here],
            flat_send.at[offset[0], offset[1]],
            flat_recv.at[offset[0], offset[1]],
            peer(plane, offset),
        )
        for offset in offsets(plane)
    ]
    for copy in copies:
        copy.start()
    for copy in copies:
        copy.wait()
    sums = flat[0]
    for index in range(1, n_dp * n_col):
        sums = sums + flat[index]
    out[...] = sums


def sum_everywhere(plane, values_in, collective):
    count = lax.axis_size("row")
    shape = values_in.shape
    return call_remote(
        functools.partial(total_kernel, plane, count),
        collective,
        in_specs=[VMEM],
        out_specs=VMEM,
        out_shape=jax.ShapeDtypeStruct(shape, FULL),
        scratch_shapes=[
            pltpu.VMEM((count,) + shape, FULL),
            pltpu.VMEM((plane[0] * plane[1],) + shape, FULL),
            DMA((count - 1,)),
            DMA((count - 1,)),
            DMA(plane),
            DMA(plane),
        ],
    )(values_in)


def mat(left, right):
    return jnp.sum(left[:, :, None] * right[None, :, :], axis=1)


def gather_blocks(weight_low):
    return lax.all_gather(weight_low, ("col", "dp"), axis=0, tiled=True)


def scatter_blocks(grad_low):
    return lax.psum_scatter(grad_low, ("col", "dp"), scatter_dimension=0, tiled=True).astype(FULL)


def side_by_side(weight):
    return jnp.concatenate([weight[index] for index in range(weight.shape[0])], axis=1)


def apart(weight, count):
    width = weight.shape[1] // count
    return jnp.stack([weight[:, index * width : (index + 1) * width] for index in range(count)])


def whole_out(weight_low, n_dp, n_col):
    rows, width = weight_low.shape
    blocks = gather_blocks(weight_low).reshape(n_col, n_dp, rows, width)
    return blocks.transpose(1, 2, 0, 3).reshape(n_dp * rows, n_col * width)


def own_out(grad, n_dp, n_col):
    rows, width = grad.shape[0] // n_dp, grad.shape[1] // n_col
    blocks = grad.astype(LOW).reshape(n_dp, rows, n_col, width).transpose(2, 0, 1, 3)
    return scatter_blocks(blocks.reshape(n_col * n_dp * rows, width))


def adam_update(weight, grad_sum, moment_one, moment_two, clip_factor, step_value):
    clipped = grad_sum * clip_factor
    new_one = beta_first * moment_one + (1.0 - beta_first) * clipped
    new_two = beta_second * moment_two + (1.0 - beta_second) * clipped * clipped
    fix_one = 1.0 - jnp.power(beta_first, step_value)
    fix_two = 1.0 - jnp.power(beta_second, step_value)
    new_weight = weight - learning_rate * (
        new_one / fix_one / (jnp.sqrt(new_two / fix_two) + adam_eps) + weight_decay * weight
    )
    return (new_weight, new_one, new_two)


def body(
    streams,
    cotangent,
    destination,
    segments,
    attention_in,
    feedforward_in,
    attention_out,
    feedforward_out,
    attention_in_moment,
    feedforward_in_moment,
    attention_out_moment,
    feedforward_out_moment,
    attention_in_second,
    feedforward_in_second,
    attention_out_second,
    feedforward_out_second,
    hyper_weights,
    hyper_moment,
    hyper_second,
    step_count,
):
    n_dp, n_col, count = lax.axis_size("dp"), lax.axis_size("col"), lax.axis_size("row")
    plane, pairs = (n_dp, n_col), count // 2
    rows = destination.shape[1]
    group_tokens = segments.shape[2]
    slot = rows // n_dp
    travel = LOW if slot % 16 == 0 else FULL
    in_kernel = plane == (2, 2)
    attention_low = [side_by_side(attention_in).astype(LOW), attention_out.astype(LOW)]
    feedforward_out_own = feedforward_out.astype(LOW)

    group = destination // group_tokens
    sent = (
        group * slot
        + (destination - group * group_tokens)
        - lax.axis_index("row") * rows
        - lax.axis_index("dp") * slot
    )
    hyper = hyper_weights.reshape(-1)
    h_home, mix_home, back_home, gy_home, gram = prepare(
        hyper, streams, cotangent, sent, n_dp, travel
    )
    segment = lax.dynamic_index_in_dim(segments[:, 0], lax.axis_index("col"), 0, keepdims=False)
    start, inverse = rotary_parts(segment)

    feedforward_out_low = gather_blocks(feedforward_out_own).reshape(n_col, n_dp, *feedforward_out.shape)
    early = attention_low if in_kernel else []
    (rows_att, hidden_att, gy_work, cosine, sine, feedforward_in_own), wholes = enter(
        plane, pairs, h_home, gy_home, start, inverse, feedforward_in, early, 1
    )
    if not in_kernel:
        wholes = [gather_blocks(attention_low[0]), whole_out(attention_low[1], n_dp, n_col)]
    attention_in_low, attention_out_low = wholes
    (
        grad_rows_ffn,
        mix_work,
        heads_low,
        log_totals,
        query_low,
        key_low,
        value_low,
        branch_low,
        branch_att,
    ), wholes = attend(
        plane,
        pairs,
        rows_att,
        attention_in_low,
        attention_out_low,
        cosine,
        sine,
        start,
        gy_work.astype(LOW),
        mix_home,
        [feedforward_in_own] if in_kernel else [],
        2,
    )
    feedforward_in_low = wholes[0] if in_kernel else gather_blocks(feedforward_in_own)
    rows_ffn, hidden_low, grad_units, partial_ffn, grad_hidden_ffn, grad_branch = feed_forward(
        plane,
        pairs,
        hyper,
        mix_work,
        branch_att,
        back_home,
        feedforward_in_low,
        feedforward_out_low,
        grad_rows_ffn,
        3,
    )
    if in_kernel:
        grad_rows_att, branch_ffn, grad_out, sum_in, square = back_gather(
            pairs, plane, grad_branch, partial_ffn, rows_ffn, grad_units, hidden_low, grad_rows_ffn, 5
        )
        ffn_grad, squares = [grad_out], [square]
    else:
        grad_rows_att = row_gather(pairs, grad_branch, 5)
        branch_ffn = lax.psum_scatter(partial_ffn, "row", scatter_dimension=0, tiled=True)
        sums_ffn = [
            apart(
                scatter_blocks(
                    jnp.einsum("td,tu->du", rows_ffn, grad_units, preferred_element_type=FULL).astype(LOW)
                ),
                2,
            ),
            own_out(
                jnp.einsum("tu,td->ud", hidden_low, grad_rows_ffn, preferred_element_type=FULL), n_dp, n_col
            ),
        ]
        ffn_grad, squares = [], [value * value for value in sums_ffn]

    homes, sums_att = leave(
        plane,
        pairs,
        ffn_grad,
        grad_rows_att,
        rows_att,
        heads_low,
        log_totals,
        query_low,
        key_low,
        value_low,
        (cosine, sine, start),
        attention_in_low,
        attention_out_low,
        hidden_att,
        [value.astype(travel) for value in (branch_low, branch_ffn, grad_hidden_ffn)],
        6,
    )
    if in_kernel:
        squares += sums_att[1::2]
        shard_feedforward_out, shard_attention_out, shard_attention_in = sums_att[::2]
        shard_feedforward_out, shard_attention_out = shard_feedforward_out[0], shard_attention_out[0]
        shard_feedforward_in = sum_in
    else:
        shard_attention_in = apart(scatter_blocks(sums_att[0]), 3)
        shard_attention_out = own_out(sums_att[1], n_dp, n_col)
        squares += [value * value for value in (shard_attention_in, shard_attention_out)]
        shard_feedforward_in, shard_feedforward_out = sums_ffn
    square = sum(jnp.sum(value) for value in squares)
    streams_out, stream_grad, dots = finish(hyper, streams, cotangent, sent, homes)
    dots = jnp.concatenate([jnp.sum(gram, axis=(1, 2)), jnp.sum(dots, axis=(1, 2)), square[None]])
    totals = sum_everywhere(plane, jnp.pad(dots, (0, 128 - dots.shape[0])).reshape(1, 128), 7)[0]
    a0, m0, c0 = hyper_weights[0, :, 0], hyper_weights[0, :, 1:5], hyper_weights[0, :, 5]
    a1, m1, c1 = hyper_weights[1, :, 0], hyper_weights[1, :, 1:5], hyper_weights[1, :, 5]
    gram = totals[:16].reshape(STREAMS, STREAMS)
    att_cot, ffn_cot = totals[16:20], totals[20:24]
    streams_ffn, streams_att = totals[24:28], totals[28:32]
    att_ffn, square_total = totals[32], totals[33]
    grad_m1 = mat(m0.T, gram) + c0[:, None] * att_cot[None, :]
    grad_a1 = jnp.sum(m0 * streams_ffn[:, None], axis=0) + c0 * att_ffn
    grad_m0 = mat(gram, m1.T) + streams_ffn[:, None] * a1[None, :]
    grad_c0 = jnp.sum(m1 * att_cot[None, :], axis=1) + a1 * att_ffn
    hyper_grad = jnp.stack(
        [
            jnp.concatenate([streams_att[:, None], grad_m0, grad_c0[:, None]], axis=1),
            jnp.concatenate([grad_a1[:, None], grad_m1, ffn_cot[:, None]], axis=1),
        ]
    )
    grad_norm = jnp.sqrt(square_total + jnp.sum(hyper_grad * hyper_grad))
    clip_factor = 1.0 / jnp.maximum(grad_norm, 1.0)
    step_value = step_count[0].astype(jnp.float32)
    attention_in_new = adam_update(
        attention_in,
        shard_attention_in,
        attention_in_moment,
        attention_in_second,
        clip_factor,
        step_value,
    )
    feedforward_in_new = adam_update(
        feedforward_in,
        shard_feedforward_in,
        feedforward_in_moment,
        feedforward_in_second,
        clip_factor,
        step_value,
    )
    attention_out_new = adam_update(
        attention_out,
        shard_attention_out,
        attention_out_moment,
        attention_out_second,
        clip_factor,
        step_value,
    )
    feedforward_out_new = adam_update(
        feedforward_out,
        shard_feedforward_out,
        feedforward_out_moment,
        feedforward_out_second,
        clip_factor,
        step_value,
    )
    hyper_new = adam_update(
        hyper_weights, hyper_grad, hyper_moment, hyper_second, clip_factor, step_value
    )
    return (
        streams_out,
        stream_grad,
        grad_norm.reshape(1),
        shard_attention_in,
        shard_feedforward_in,
        shard_attention_out,
        shard_feedforward_out,
        hyper_grad,
        attention_in_new[0],
        feedforward_in_new[0],
        attention_out_new[0],
        feedforward_out_new[0],
        hyper_new[0],
        attention_in_new[1],
        feedforward_in_new[1],
        attention_out_new[1],
        feedforward_out_new[1],
        hyper_new[1],
        attention_in_new[2],
        feedforward_in_new[2],
        attention_out_new[2],
        feedforward_out_new[2],
        hyper_new[2],
    )


def solution(mesh):
    placed = (
        P(None, None, ("dp", "row"), "col"),
        P(None, None, ("dp", "row"), "col"),
        P(None, ("dp", "row")),
        P(None, "dp", None),
        P(None, ("col", "dp"), "row"),
        P(None, ("col", "dp"), "row"),
        P(("row", "dp"), "col"),
        P(("row", "dp"), "col"),
        P(None, ("col", "dp"), "row"),
        P(None, ("col", "dp"), "row"),
        P(("row", "dp"), "col"),
        P(("row", "dp"), "col"),
        P(None, ("col", "dp"), "row"),
        P(None, ("col", "dp"), "row"),
        P(("row", "dp"), "col"),
        P(("row", "dp"), "col"),
        P(),
        P(),
        P(),
        P(),
    )
    return jax.shard_map(
        body,
        mesh=mesh,
        in_specs=placed,
        out_specs=(
            P(None, None, ("dp", "row"), "col"),
            P(None, None, ("dp", "row"), "col"),
            P(),
            P(None, ("col", "dp"), "row"),
            P(None, ("col", "dp"), "row"),
            P(("row", "dp"), "col"),
            P(("row", "dp"), "col"),
            P(),
            P(None, ("col", "dp"), "row"),
            P(None, ("col", "dp"), "row"),
            P(("row", "dp"), "col"),
            P(("row", "dp"), "col"),
            P(),
            P(None, ("col", "dp"), "row"),
            P(None, ("col", "dp"), "row"),
            P(("row", "dp"), "col"),
            P(("row", "dp"), "col"),
            P(),
            P(None, ("col", "dp"), "row"),
            P(None, ("col", "dp"), "row"),
            P(("row", "dp"), "col"),
            P(("row", "dp"), "col"),
            P(),
        ),
        check_vma=False,
    )
```

```python
import functools
import math

import jax
import jax.numpy as jnp
from jax import lax
from jax.experimental import pallas as pl
from jax.experimental.pallas import tpu as pltpu
from jax.sharding import PartitionSpec as P

D = 2048
HEAD = 128
STREAMS = 4
MICRO = 2


norm_eps = 1e-05
beta_first = 0.9
beta_second = 0.95
adam_eps = 1e-08
learning_rate = 0.05
weight_decay = 0.1

LOW = jnp.bfloat16
FULL = jnp.float32
DMA = pltpu.SemaphoreType.DMA
ANY = pl.BlockSpec(memory_space=pl.ANY)
VMEM = pl.BlockSpec(memory_space=pltpu.VMEM)
SMEM = pl.BlockSpec(memory_space=pltpu.SMEM)
ROOM = 63 * 2**20


def rotary_parts(segment):
    starts = jnp.sum((segment[None, :] < segment[:, None]).astype(jnp.int32), axis=1)
    halves = jnp.tile(jnp.arange(HEAD // 2, dtype=jnp.float32), 2)
    return starts[:, None], jnp.exp(halves * (-2.0 * math.log(10000.0) / HEAD))[None, :]


def norm_forward(hidden):
    means = jnp.sum(hidden, axis=-1, keepdims=True) / D
    squares = jnp.sum(hidden * hidden, axis=-1, keepdims=True) / D
    inverse = lax.rsqrt(squares - means * means + norm_eps)
    return ((hidden - means) * inverse, inverse)


def norm_backward(upstream, hidden):
    normed, inverse = norm_forward(hidden)
    mean_one = jnp.sum(upstream, axis=-1, keepdims=True) / D
    mean_two = jnp.sum(upstream * normed, axis=-1, keepdims=True) / D
    return inverse * (upstream - mean_one - normed * mean_two)


def hyper_parts(hyper):
    width = STREAMS + 2
    parts = []
    for layer in range(2):
        at = [[hyper[(layer * STREAMS + i) * width + k] for k in range(width)] for i in range(STREAMS)]
        parts.append(
            ([row[0] for row in at], [row[1 : STREAMS + 1] for row in at], [row[-1] for row in at])
        )
    return parts


def dot_of(left, right):
    total = left[0] * right[0]
    for a, b in zip(left[1:], right[1:]):
        total = total + a * b
    return total


def column(matrix, index):
    return [row[index] for row in matrix]


def branch_weight(hyper):
    (_, _, c0), (a1, _, _) = hyper_parts(hyper)
    return dot_of(a1, c0)


def combine(weights, stream_set):
    return dot_of(weights, stream_set)


def fold(product):
    rows, width = product.shape
    return jnp.sum(product.reshape(rows // 8, 8, width), axis=0)


def place_rows(match, values_in):
    match = match.astype(LOW)
    if values_in.dtype == LOW:
        return jnp.dot(match, values_in, preferred_element_type=FULL)
    high = values_in.astype(LOW)
    rest = values_in - high.astype(FULL)
    middle = rest.astype(LOW)
    last = (rest - middle.astype(FULL)).astype(LOW)
    high, middle, last = (jnp.dot(match, piece, preferred_element_type=FULL) for piece in (high, middle, last))
    return high + (middle + last)


def prepare_kernel(hyper, streams, cotangent, sent, h_out, mix_out, back_out, gy_out, gram_out):
    rows, width = streams.shape[2:]
    parts, slot = h_out.shape[0], h_out.shape[2]
    (a0, m0, c0), (a1, m1, c1) = hyper_parts(hyper)
    first = [streams[0, i] for i in range(STREAMS)]
    second = [cotangent[0, j] for j in range(STREAMS)]
    match = lax.broadcasted_iota(jnp.int32, (rows, rows), 0) == sent[0]

    def put(out, values_in):
        moved = place_rows(match, values_in)
        for part in range(parts):
            out[part, 0] = moved[part * slot : (part + 1) * slot].astype(out.dtype)

    put(h_out, combine(a0, first))
    put(mix_out, combine([dot_of(row, a1) for row in m0], first))
    put(gy_out, combine(c1, second).astype(LOW))
    put(back_out, combine([dot_of(c0, column(m1, k)) for k in range(STREAMS)], second))

    @pl.when((pl.program_id(0) == 0) & (pl.program_id(1) == 0))
    def _():
        gram_out[...] = jnp.zeros_like(gram_out)

    for i in range(STREAMS):
        for j in range(STREAMS):
            gram_out[i * STREAMS + j] += fold(first[i] * second[j])


def prepare(hyper, streams, cotangent, sent, n_dp, travel):
    micro, _, rows, width = streams.shape
    slot, wide = rows // n_dp, 512
    block = pl.BlockSpec((1, STREAMS, rows, wide), lambda m, f: (m, 0, 0, f))
    home = pl.BlockSpec((n_dp, 1, slot, wide), lambda m, f: (0, m, 0, f))
    shape = (n_dp, micro, slot, width)
    return pl.pallas_call(
        prepare_kernel,
        grid=(micro, width // wide),
        in_specs=[SMEM, block, block, pl.BlockSpec((1, 1, rows), lambda m, f: (m, 0, 0))],
        out_specs=[home] * 4 + [pl.BlockSpec((STREAMS * STREAMS, 8, wide), lambda m, f: (0, 0, 0))],
        out_shape=[jax.ShapeDtypeStruct(shape, FULL)] * 3
        + [
            jax.ShapeDtypeStruct(shape, travel),
            jax.ShapeDtypeStruct((STREAMS * STREAMS, 8, wide), FULL),
        ],
        compiler_params=pltpu.CompilerParams(vmem_limit_bytes=ROOM),
    )(hyper, streams, cotangent, sent[:, None, :])


def finish_kernel(
    hyper, streams, cotangent, sent, y_att, y_ffn, gh_ffn, gh_att, streams_out, grad_out, dots_out
):
    rows, width = streams.shape[2:]
    (a0, m0, c0), (a1, m1, c1) = hyper_parts(hyper)
    first = [streams[0, i] for i in range(STREAMS)]
    second = [cotangent[0, j] for j in range(STREAMS)]
    match = lax.broadcasted_iota(jnp.int32, (rows, rows), 1) == sent[0]
    home_att, home_ffn, back_ffn, back_att = (
        place_rows(match, value[:, 0].reshape(rows, width)) for value in (y_att, y_ffn, gh_ffn, gh_att)
    )
    for j in range(STREAMS):
        mixed = combine([dot_of(m0[k], column(m1, j)) for k in range(STREAMS)], first)
        streams_out[0, j] = mixed + dot_of(c0, column(m1, j)) * home_att + c1[j] * home_ffn
    for i in range(STREAMS):
        mixed = combine([dot_of(m0[i], column(m1, k)) for k in range(STREAMS)], second)
        grad_out[0, i] = mixed + dot_of(m0[i], a1) * back_ffn + a0[i] * back_att

    @pl.when((pl.program_id(0) == 0) & (pl.program_id(1) == 0))
    def _():
        dots_out[...] = jnp.zeros_like(dots_out)

    pairs = (
        [(value, home_att) for value in second]
        + [(value, home_ffn) for value in second]
        + [(value, back_ffn) for value in first]
        + [(value, back_att) for value in first]
        + [(home_att, back_ffn)]
    )
    for index, (left, right) in enumerate(pairs):
        dots_out[index] += fold(left * right)


def finish(hyper, streams, cotangent, sent, homes):
    micro, _, rows, width = streams.shape
    n_dp, _, slot, _ = homes[0].shape
    wide = 512
    block = pl.BlockSpec((1, STREAMS, rows, wide), lambda m, f: (m, 0, 0, f))
    home = pl.BlockSpec((n_dp, 1, slot, wide), lambda m, f: (0, m, 0, f))
    count = 4 * STREAMS + 1
    return pl.pallas_call(
        finish_kernel,
        grid=(micro, width // wide),
        in_specs=[SMEM, block, block, pl.BlockSpec((1, rows, 1), lambda m, f: (m, 0, 0))] + [home] * 4,
        out_specs=[block, block, pl.BlockSpec((count, 8, wide), lambda m, f: (0, 0, 0))],
        out_shape=[
            jax.ShapeDtypeStruct(streams.shape, FULL),
            jax.ShapeDtypeStruct(streams.shape, FULL),
            jax.ShapeDtypeStruct((count, 8, wide), FULL),
        ],
        compiler_params=pltpu.CompilerParams(vmem_limit_bytes=ROOM),
    )(hyper, streams, cotangent, sent[:, :, None], *homes)


def turn(values_in, cosine, sine):
    half = HEAD // 2
    swapped = jnp.concatenate([values_in[:, half:], values_in[:, :half]], axis=1)
    return values_in * cosine + swapped * sine


def dot_last(left, right):
    return lax.dot_general(left, right, (((1,), (1,)), ((), ())), preferred_element_type=jnp.float32)


def dot_first(left, right):
    return lax.dot_general(left, right, (((0,), (0,)), ((), ())), preferred_element_type=jnp.float32)


def allowed_pairs(start_ref, base, block, keys):
    column = lax.broadcasted_iota(jnp.int32, (block, keys), 1)
    row = lax.broadcasted_iota(jnp.int32, (block, keys), 0) + base
    return (column >= start_ref[pl.ds(base, block)]) & (column <= row)


def attend_head(head, q, k, v, start, out, log_out):
    length = q.shape[0]
    block = min(256, length)
    at = pl.ds(head * HEAD, HEAD)
    for base in range(0, length, block):
        keys = base + block
        rows, span = pl.ds(base, block), pl.ds(0, keys)
        scores = dot_last(q[rows, at], k[span, at]) * HEAD ** (-0.5)
        scores = jnp.where(allowed_pairs(start, base, block, keys), scores, -1e30)
        largest = jnp.max(scores, axis=1, keepdims=True)
        weights = jnp.exp(scores - largest)
        totals = jnp.sum(weights, axis=1, keepdims=True)
        probs = (weights * (1.0 / totals)).astype(LOW)
        out[rows, at] = jnp.dot(probs, v[span, at], preferred_element_type=FULL).astype(LOW)
        log_out[rows, pl.ds(head, 1)] = largest + jnp.log(totals)


def attend_head_back(head, grad, q, k, v, log_in, cosine, sine, start, units, k_sum, v_sum):
    length, width = q.shape
    block = min(256, length)
    at = pl.ds(head * HEAD, HEAD)
    k_sum[...] = jnp.zeros_like(k_sum)
    v_sum[...] = jnp.zeros_like(v_sum)
    for base in range(0, length, block):
        keys = base + block
        rows, span = pl.ds(base, block), pl.ds(0, keys)
        scores = dot_last(q[rows, at], k[span, at]) * HEAD ** (-0.5)
        probs = jnp.where(
            allowed_pairs(start, base, block, keys), jnp.exp(scores - log_in[rows, pl.ds(head, 1)]), 0.0
        )
        grad_probs = dot_last(grad[rows, at], v[span, at])
        inner = jnp.sum(probs * grad_probs, axis=1, keepdims=True)
        grad_scores = (probs * (grad_probs - inner) * HEAD ** (-0.5)).astype(LOW)
        grad_query = jnp.dot(grad_scores, k[span, at], preferred_element_type=FULL)
        units[rows, at] = turn(grad_query, cosine[rows], -sine[rows]).astype(LOW)
        k_sum[span] += dot_first(grad_scores, q[rows, at])
        v_sum[span] += dot_first(probs.astype(LOW), grad[rows, at])
    units[:, pl.ds(width + head * HEAD, HEAD)] = turn(k_sum[...], cosine[...], -sine[...]).astype(LOW)
    units[:, pl.ds(2 * width + head * HEAD, HEAD)] = v_sum[...].astype(LOW)


def remote(source, target, send_sem, recv_sem, device):
    return pltpu.make_async_remote_copy(
        src_ref=source,
        dst_ref=target,
        send_sem=send_sem,
        recv_sem=recv_sem,
        device_id=device,
        device_id_type=pl.DeviceIdType.MESH,
    )


def line_place():
    me = lax.axis_index("row")
    return me, me // 2, me % 2


def greet(pairs, plane=None):
    me, place, side = line_place()
    barrier = pltpu.get_barrier_semaphore()

    def signal(device):
        pl.semaphore_signal(barrier, inc=1, device_id=device, device_id_type=pl.DeviceIdType.MESH)

    signal({"row": me + 1 - 2 * side})

    @pl.when(place < pairs - 1)
    def _():
        signal({"row": me + 2})

    @pl.when(place > 0)
    def _():
        signal({"row": me - 2})

    count = 1
    if plane is not None:
        for offset in offsets(plane):
            signal(peer(plane, offset))
            count += 1
    last = pairs - 1
    neighbours = (place + last) // pairs + (2 * last - place) // pairs
    pl.semaphore_wait(barrier, count + neighbours)


def offsets(plane):
    n_dp, n_col = plane
    return [(d, c) for d in range(n_dp) for c in range(n_col) if (d, c) != (0, 0)]


def peer(plane, offset):
    n_dp, n_col = plane
    return {
        "dp": (lax.axis_index("dp") + offset[0]) % n_dp,
        "col": (lax.axis_index("col") + offset[1]) % n_col,
    }


class Exchange:
    def __init__(self, plane, source_of, target, sends, receives, keep):
        self.plane, self.source_of, self.target = plane, source_of, target
        self.sends, self.receives, self.keep = sends, receives, keep

    def move(self, offset):
        device = peer(self.plane, offset)
        return remote(
            self.source_of(device["dp"], device["col"]),
            self.target,
            self.sends.at[offset[0], offset[1]],
            self.receives.at[offset[0], offset[1]],
            device,
        )

    def stay(self):
        return pltpu.make_async_copy(
            self.source_of(lax.axis_index("dp"), lax.axis_index("col")), self.target, self.keep
        )

    def start(self):
        for offset in offsets(self.plane):
            self.move(offset).start()
        self.stay().start()

    def arrive(self):
        for offset in offsets(self.plane):
            self.move(offset).wait_recv()
        self.stay().wait()

    def leave(self):
        for offset in offsets(self.plane):
            self.move(offset).wait_send()


def exchange_sems(plane, count):
    return [DMA((count,) + plane), DMA((count,) + plane), DMA((count,))]


def work_block(work, slot, width, part, side):
    return work.at[
        pl.ds(pl.multiple_of(part * slot, slot), slot), pl.ds(pl.multiple_of(side * width, width), width)
    ]


def to_work(plane, home, work, sems, index):
    slot, width = home.shape[2:]
    return Exchange(
        plane,
        lambda b, c: home.at[b, c],
        work_block(work, slot, width, lax.axis_index("dp"), lax.axis_index("col")),
        sems[0].at[index],
        sems[1].at[index],
        sems[2].at[index],
    )


def to_home(plane, work, home, sems, index):
    slot, width = home.shape[2:]
    return Exchange(
        plane,
        lambda b, c: work_block(work, slot, width, b, c),
        home.at[lax.axis_index("dp"), lax.axis_index("col")],
        sems[0].at[index],
        sems[1].at[index],
        sems[2].at[index],
    )


class Gather:
    def __init__(self, pairs, cuts, own, out, sems):
        self.pairs, self.cuts, self.own, self.out = pairs, cuts, own, out
        self.right, self.left, self.twin_send, self.line, self.twin_recv, self.keep = sems
        self.height = own.shape[0] // cuts

    def piece(self, ref, cut):
        return ref.at[pl.ds(cut * self.height, self.height)]

    def move(self, row, sends, receives, origin, cut, first):
        _, _, side = line_place()
        block = self.piece(self.out.at[origin * 2 + side], cut)
        return remote(
            self.piece(self.own, cut) if first else block,
            block,
            sends.at[origin, cut],
            receives.at[origin, cut],
            {"row": row},
        )

    def to_twin(self, origin, cut, first=False):
        me, _, side = line_place()
        return self.move(me + 1 - 2 * side, self.twin_send, self.twin_recv, origin, cut, first)

    def to_right(self, origin, cut, first=False):
        return self.move(line_place()[0] + 2, self.right, self.line, origin, cut, first)

    def to_left(self, origin, cut, first=False):
        return self.move(line_place()[0] - 2, self.left, self.line, origin, cut, first)

    def stay(self):
        return pltpu.make_async_copy(self.own, self.out.at[line_place()[0]], self.keep)

    def start(self):
        _, place, _ = line_place()
        for cut in range(self.cuts):
            @pl.when(place < self.pairs - 1)
            def _():
                self.to_right(place, cut, True).start()

            @pl.when(place > 0)
            def _():
                self.to_left(place, cut, True).start()

        for cut in range(self.cuts):
            self.to_twin(place, cut, True).start()
        self.stay().start()

    def step(self, step, cut):
        _, place, _ = line_place()

        @pl.when(place >= step)
        def _():
            origin = place - step
            self.to_right(origin, cut).wait_recv()

            @pl.when(place < self.pairs - 1)
            def _():
                self.to_right(origin, cut).start()

            self.to_twin(origin, cut).start()

        @pl.when(place + step <= self.pairs - 1)
        def _():
            origin = place + step
            self.to_left(origin, cut).wait_recv()

            @pl.when(place > 0)
            def _():
                self.to_left(origin, cut).start()

            self.to_twin(origin, cut).start()

    def twin_arrive(self, origin):
        me, _, side = line_place()
        for cut in range(self.cuts):
            other = self.piece(self.out.at[origin * 2 + 1 - side], cut)
            remote(
                other,
                other,
                self.twin_send.at[origin, cut],
                self.twin_recv.at[origin, cut],
                {"row": me + 1 - 2 * side},
            ).wait_recv()

    def finish(self):
        self.stay().wait()
        for origin in range(self.pairs):
            self.twin_arrive(origin)
        self.leave()

    def leave(self):
        _, place, _ = line_place()
        for origin in range(self.pairs):
            for cut in range(self.cuts):
                self.to_twin(origin, cut).wait_send()

                @pl.when((place < self.pairs - 1) & (origin <= place))
                def _():
                    self.to_right(origin, cut).wait_send()

                @pl.when((place > 0) & (origin >= place))
                def _():
                    self.to_left(origin, cut).wait_send()


def gather_sems(pairs, cuts):
    return [DMA((pairs, cuts))] * 5 + [DMA]


def inner_order(pairs, cuts, inner):
    near = [(True, dest, cut) for dest in range(pairs - 1, inner, -1) for cut in range(cuts)]
    far = [(False, dest, cut) for dest in range(inner) for cut in range(cuts)]
    hops = pairs - 1 - 2 * inner
    timed = [(index, 0) + one for index, one in enumerate(near)]
    timed += [(index + hops, 1) + one for index, one in enumerate(far)]
    return [one[2:] for one in sorted(timed, key=lambda one: one[:2])]


class Scatter:
    def __init__(self, pairs, cuts, part, buffers, sems):
        self.pairs, self.cuts, self.part = pairs, cuts, part
        self.twin, self.from_left, self.from_right = buffers[:3]
        self.own = buffers[3] if len(buffers) > 3 else None
        (
            self.right_send,
            self.left_send,
            self.twin_send,
            self.right_recv,
            self.left_recv,
            self.twin_recv,
            self.loaded,
        ) = sems
        self.height = part.shape[1] // cuts

    def span(self, cut):
        return pl.ds(cut * self.height, self.height)

    def mine(self, dest, cut):
        _, _, side = line_place()
        if self.own is None:
            return self.part.at[dest * 2 + side, self.span(cut)]
        return self.own.at[dest, self.span(cut)]

    def load(self, dest, cut):
        _, _, side = line_place()
        return pltpu.make_async_copy(
            self.part.at[dest * 2 + side, self.span(cut)], self.mine(dest, cut), self.loaded.at[dest, cut]
        )

    def to_twin(self, dest, cut):
        me, _, side = line_place()
        return remote(
            self.part.at[dest * 2 + 1 - side, self.span(cut)],
            self.twin.at[dest, self.span(cut)],
            self.twin_send.at[dest, cut],
            self.twin_recv.at[dest, cut],
            {"row": me + 1 - 2 * side},
        )

    def to_right(self, dest, cut):
        return remote(
            self.mine(dest, cut),
            self.from_left.at[dest, self.span(cut)],
            self.right_send.at[dest, cut],
            self.right_recv.at[dest, cut],
            {"row": line_place()[0] + 2},
        )

    def to_left(self, dest, cut):
        return remote(
            self.mine(dest, cut),
            self.from_right.at[dest, self.span(cut)],
            self.left_send.at[dest, cut],
            self.left_recv.at[dest, cut],
            {"row": line_place()[0] - 2},
        )

    def order(self):
        order = []
        for step in range(self.pairs):
            for dest in (self.pairs - 1 - step, step):
                if dest not in order:
                    order.append(dest)
        return order

    def offer(self, dest):
        for cut in range(self.cuts):
            self.to_twin(dest, cut).start()
            if self.own is not None:
                self.load(dest, cut).start()

    def start(self):
        for dest in self.order():
            self.offer(dest)

    def here(self, dest, cut):
        return self.mine(dest, cut)[...].astype(FULL) + self.twin[dest, self.span(cut)].astype(FULL)

    def flows(self, step, place):
        last = self.pairs - 1
        return (
            (last - step, place < last - step, place == 0, self.from_left, self.to_right),
            (step, place > step, place == last, self.from_right, self.to_left),
        )

    def begin(self):
        _, place, _ = line_place()
        ready = []
        for step in range(self.pairs - 1):
            for dest, sending, first, _, copy in self.flows(step, place):
                for cut in range(self.cuts):
                    if (dest, cut) not in ready:
                        ready.append((dest, cut))
                        self.to_twin(dest, cut).wait_recv()
                        if self.own is not None:
                            self.load(dest, cut).wait()

                    @pl.when(sending & first)
                    def _():
                        self.mine(dest, cut)[...] = self.here(dest, cut).astype(LOW)
                        copy(dest, cut).start()

    def pass_on(self, dest, cut, rightward):
        copy, arrived = (self.to_right, self.from_left) if rightward else (self.to_left, self.from_right)
        copy(dest, cut).wait_recv()
        self.mine(dest, cut)[...] = (
            self.here(dest, cut) + arrived[dest, self.span(cut)].astype(FULL)
        ).astype(LOW)
        copy(dest, cut).start()

    def poll(self, index):
        _, place, _ = line_place()
        last = self.pairs - 1
        for inner in range(1, self.pairs // 2):
            order = inner_order(self.pairs, self.cuts, inner)
            if index < len(order):
                near, dest, cut = order[index]

                @pl.when(place == inner)
                def _():
                    self.pass_on(dest, cut, near)

                @pl.when(place == last - inner)
                def _():
                    self.pass_on(last - dest, cut, not near)

    def polls(self):
        return max(
            len(inner_order(self.pairs, self.cuts, inner)) for inner in range(1, self.pairs // 2)
        )

    def finish(self, total):
        _, place, _ = line_place()
        last = self.pairs - 1
        for cut in range(self.cuts):
            span = self.span(cut)
            total[span] = self.here(place, cut)

            @pl.when(place > 0)
            def _():
                self.to_right(place, cut).wait_recv()
                total[span] += self.from_left[place, span].astype(FULL)

            @pl.when(place < last)
            def _():
                self.to_left(place, cut).wait_recv()
                total[span] += self.from_right[place, span].astype(FULL)

        for dest in range(self.pairs):
            for cut in range(self.cuts):
                self.to_twin(dest, cut).wait_send()

                @pl.when(place < dest)
                def _():
                    self.to_right(dest, cut).wait_send()

                @pl.when(place > dest)
                def _():
                    self.to_left(dest, cut).wait_send()


def scatter_buffers(pairs, rows, width, loaded=True):
    return [pltpu.VMEM((pairs, rows, width), LOW)] * (4 if loaded else 3)


def scatter_sems(pairs, cuts):
    return [DMA((pairs, cuts))] * 7


class PlaneScatter:
    def __init__(self, block_of, out, square, buffers, sems):
        self.block_of, self.out, self.square = block_of, out, square
        self.arrived, self.mine, self.onward, self.final = buffers
        self.send, self.recv, self.loaded, self.send_on, self.recv_on = sems
        self.height = out.shape[-2] // 2

    def places(self, half, index):
        d, c = lax.axis_index("dp"), lax.axis_index("col")
        if half == 0:
            there = 1 - c if index == 0 else c
            return {"dp": 1 - d}, self.block_of(there, 1 - d, 0), self.block_of(there, d, 0)
        there = 1 - d if index == 0 else d
        return {"col": 1 - c}, self.block_of(1 - c, there, 1), self.block_of(c, there, 1)

    def move(self, half, index):
        device, block, _ = self.places(half, index)
        return remote(
            block, self.arrived.at[half, index], self.send.at[half, index], self.recv.at[half, index], device
        )

    def load(self, half, index):
        _, _, block = self.places(half, index)
        return pltpu.make_async_copy(block, self.mine.at[half, index], self.loaded.at[half, index])

    def move_on(self, half):
        device = (
            {"col": 1 - lax.axis_index("col")} if half == 0 else {"dp": 1 - lax.axis_index("dp")}
        )
        return remote(
            self.onward.at[half], self.final.at[half], self.send_on.at[half], self.recv_on.at[half], device
        )

    def start(self):
        for index in range(2):
            for half in range(2):
                self.move(half, index).start()
                if self.mine is not None:
                    self.load(half, index).start()

    def sum_of(self, half, index):
        self.move(half, index).wait_recv()
        if self.mine is None:
            _, _, block = self.places(half, index)
            mine = block[...]
        else:
            self.load(half, index).wait()
            mine = self.mine[half, index]
        return mine.astype(FULL) + self.arrived[half, index].astype(FULL)

    def forward(self):
        for half in range(2):
            self.onward[half] = self.sum_of(half, 0).astype(LOW)
            self.move_on(half).start()

    def finish(self):
        for half in range(2):
            total = self.sum_of(half, 1)
            self.move_on(half).wait_recv()
            total = total + self.final[half].astype(FULL)
            width = self.out.shape[-1]
            for index in range(self.out.shape[0]):
                self.out[index, pl.ds(half * self.height, self.height)] = total[
                    :, index * width : (index + 1) * width
                ]
            squares = fold(total * total)
            self.square[half] = sum(
                squares[:, at : at + 128] for at in range(0, squares.shape[1], 128)
            )
        for half in range(2):
            for index in range(2):
                self.move(half, index).wait_send()
            self.move_on(half).wait_send()


class PlaneGather:
    def __init__(self, own, block_of, sems):
        self.own, self.block_of = own, block_of
        self.send, self.recv, self.send_on, self.recv_on, self.keep = sems
        self.height = own.shape[0] // 2

    def direct(self, axis, half):
        d, c = lax.axis_index("dp"), lax.axis_index("col")
        return remote(
            self.own.at[pl.ds(half * self.height, self.height)],
            self.block_of(c, d, half),
            self.send.at[axis, half],
            self.recv.at[axis, half],
            {"dp": 1 - d} if axis == 0 else {"col": 1 - c},
        )

    def onward(self, half):
        d, c = lax.axis_index("dp"), lax.axis_index("col")
        block = self.block_of(c, 1 - d, 0) if half == 0 else self.block_of(1 - c, d, 1)
        return remote(
            block,
            block,
            self.send_on.at[half],
            self.recv_on.at[half],
            {"col": 1 - c} if half == 0 else {"dp": 1 - d},
        )

    def stay(self, half):
        d, c = lax.axis_index("dp"), lax.axis_index("col")
        return pltpu.make_async_copy(
            self.own.at[pl.ds(half * self.height, self.height)], self.block_of(c, d, half), self.keep.at[half]
        )

    def start(self):
        for half in range(2):
            self.direct(half, half).start()
        for half in range(2):
            self.stay(half).start()

    def forward(self):
        for half in range(2):
            self.direct(half, half).wait_recv()
            self.onward(half).start()
            self.direct(1 - half, half).start()

    def finish(self):
        for half in range(2):
            self.direct(1 - half, half).wait_recv()
            self.onward(half).wait_recv()
            self.stay(half).wait()
        for half in range(2):
            for axis in range(2):
                self.direct(axis, half).wait_send()
            self.onward(half).wait_send()


def plane_gather_sems():
    return [DMA((2, 2)), DMA((2, 2)), DMA((2,)), DMA((2,)), DMA((2,))]


def by_rows(part, height):
    half_height = height // 2
    return lambda c, d, half: part.at[pl.ds((c * 2 + d) * height + half * half_height, half_height)]


def by_owner(part, height):
    half_height = height // 2
    return lambda c, d, half: part.at[c, d, pl.ds(half * half_height, half_height)]


def by_tiles(part, height, width):
    half_height = height // 2
    return lambda c, d, half: part.at[
        pl.ds(d * height + half * half_height, half_height), pl.ds(pl.multiple_of(c * width, width), width)
    ]


CUTS = 2
SUM_CUTS = 4


def call_remote(kernel, collective, **options):
    return pl.pallas_call(
        kernel,
        compiler_params=pltpu.CompilerParams(
            collective_id=collective, has_side_effects=True, vmem_limit_bytes=ROOM
        ),
        **options,
    )


def block_view(whole, rows, width):
    return by_rows(whole, rows) if whole.shape[1] == width else by_tiles(whole, rows, width)


def plane_gathers(weights, wholes, sems):
    return [
        PlaneGather(weight, block_view(whole, *weight.shape), sems[5 * index : 5 * index + 5])
        for index, (weight, whole) in enumerate(zip(weights, wholes))
    ]


def whole_shapes(weights):
    return [
        jax.ShapeDtypeStruct((4 * rows, width) if width != D // 2 else (2 * rows, 2 * width), LOW)
        for rows, width in (weight.shape for weight in weights)
    ]


def enter_kernel(plane, pairs, count, h_home, gy_home, start, inverse, w_in, *rest):
    weights, rest = rest[:count], rest[count:]
    (rows_out, h, gy, cosine, sine, w_low), rest = rest[:6], rest[6:]
    wholes, rest = rest[:count], rest[count:]
    (own, w_full, load_sem), plane_sems, line_sems, rest = rest[:3], rest[3:6], rest[6:12], rest[12:]
    load = pltpu.make_async_copy(w_in, w_full, load_sem)
    load.start()
    gathers = plane_gathers(weights, wholes, rest)
    greet(pairs, plane)
    first = to_work(plane, h_home, h, plane_sems, 0)
    second = to_work(plane, gy_home, gy, plane_sems, 1)
    first.start()
    first.arrive()
    for one in gathers:
        one.start()
    own[...] = norm_forward(h[...])[0].astype(LOW)
    gather = Gather(pairs, CUTS, own, rows_out, line_sems)
    gather.start()

    def cast():
        load.wait()
        width = w_in.shape[2]
        for index in range(w_in.shape[0]):
            w_low[:, index * width : (index + 1) * width] = w_full[index].astype(LOW)

    def angles():
        places = lax.broadcasted_iota(jnp.int32, cosine.shape, 0)
        return (places - start[...]).astype(FULL) * inverse[...]

    def put_cosine():
        cosine[...] = jnp.cos(angles())

    def put_sine():
        sign = 2 * (lax.broadcasted_iota(jnp.int32, sine.shape, 1) // (HEAD // 2)) - 1
        sine[...] = jnp.sin(angles()) * sign.astype(FULL)

    fillers = [cast, put_cosine, put_sine]
    for step in range(1, pairs):
        for cut in range(CUTS):
            if fillers:
                fillers.pop(0)()
            gather.step(step, cut)
        if step == 1:
            second.start()
        if step == 2:
            for one in gathers:
                one.forward()
    gather.finish()
    for one in gathers:
        one.finish()
    second.arrive()
    second.leave()
    first.leave()


def enter(plane, pairs, h_home, gy_home, start, inverse, w_in, weights, collective):
    n_dp, n_col, slot, width = h_home.shape
    rows = n_dp * slot
    work = jax.ShapeDtypeStruct((rows, n_col * width), FULL)
    table = jax.ShapeDtypeStruct((start.shape[0], HEAD), FULL)
    outs = call_remote(
        functools.partial(enter_kernel, plane, pairs, len(weights)),
        collective,
        in_specs=[ANY, ANY, VMEM, VMEM] + [ANY] * (1 + len(weights)),
        out_specs=[ANY, VMEM, ANY, VMEM, VMEM, VMEM] + [ANY] * len(weights),
        out_shape=[
            jax.ShapeDtypeStruct((2 * pairs, rows, n_col * width), LOW),
            work,
            jax.ShapeDtypeStruct(work.shape, gy_home.dtype),
            table,
            table,
            jax.ShapeDtypeStruct((w_in.shape[1], w_in.shape[0] * w_in.shape[2]), LOW),
        ]
        + whole_shapes(weights),
        scratch_shapes=[pltpu.VMEM(work.shape, LOW), pltpu.VMEM(w_in.shape, FULL), DMA]
        + exchange_sems(plane, 2)
        + gather_sems(pairs, CUTS)
        + plane_gather_sems() * len(weights),
    )(h_home, gy_home, start, inverse, w_in, *weights)
    return [outs[0].reshape(2 * pairs * rows, n_col * width)] + list(outs[1:6]), outs[6:]


def attend_kernel(
    plane, pairs, count, x_in, w_in, w_out, cosine, sine, start, gathered, mix_home,
    *rest,
):
    weights, rest = rest[:count], rest[count:]
    (rows_out, mix, heads_out, log_out, q, k, v, low_out, total), rest = rest[:9], rest[9:]
    wholes, rest = rest[:count], rest[count:]
    (x, part, load_sem), plane_sems, scratch, line_sems = rest[:3], rest[3:6], rest[6:16], rest[16:22]
    scatter = Scatter(pairs, SUM_CUTS, part, scratch[:3], scratch[3:])
    gather = Gather(pairs, CUTS, gathered, rows_out, line_sems)
    gathers = plane_gathers(weights, wholes, rest[22:])
    load = pltpu.make_async_copy(x_in, x, load_sem)
    load.start()
    greet(pairs, plane)
    gather.start()
    exchange = to_work(plane, mix_home, mix, plane_sems, 0)
    for one in gathers:
        one.start()
    load.wait()
    width = q.shape[1]
    heads = width // HEAD
    for index, out in enumerate((q, k, v)):
        value = jnp.dot(x[...], w_in[:, index * width : (index + 1) * width], preferred_element_type=FULL)
        for head in range(heads):
            at = slice(head * HEAD, (head + 1) * HEAD)
            one = value[:, at]
            out[:, at] = (one if index == 2 else turn(one, cosine[...], sine[...])).astype(LOW)
    for head in range(heads):
        attend_head(head, q, k, v, start, heads_out, log_out)
        if head == 0:
            for cut in range(CUTS):
                gather.step(1, cut)
    for one in gathers:
        one.forward()
    exchange.start()
    rows = total.shape[0]
    for dest in scatter.order():
        for owner in (2 * dest, 2 * dest + 1):
            part[owner] = jnp.dot(
                heads_out[pl.ds(owner * rows, rows)], w_out[...], preferred_element_type=FULL
            ).astype(LOW)
        scatter.offer(dest)
    scatter.begin()
    polls = list(range(scatter.polls()))
    for step in range(2, pairs):
        for cut in range(CUTS):
            gather.step(step, cut)
            for index in polls[:2]:
                scatter.poll(index)
            polls = polls[2:]
    for index in polls:
        scatter.poll(index)
    scatter.finish(total)
    low_out[...] = total[...].astype(LOW)
    gather.finish()
    for one in gathers:
        one.finish()
    exchange.arrive()
    exchange.leave()


def attend(plane, pairs, x, w_in, w_out, cosine, sine, start, gathered, mix_home, weights, collective):
    tokens, width = x.shape
    rows = tokens // (2 * pairs)
    local = w_out.shape[0]
    low = jax.ShapeDtypeStruct((tokens, local), LOW)
    full = jax.ShapeDtypeStruct((rows, width), FULL)
    outs = call_remote(
        functools.partial(attend_kernel, plane, pairs, len(weights)),
        collective,
        in_specs=[ANY, VMEM, VMEM, VMEM, VMEM, VMEM, ANY, ANY] + [ANY] * len(weights),
        out_specs=[ANY, ANY] + [VMEM] * 7 + [ANY] * len(weights),
        out_shape=[
            jax.ShapeDtypeStruct((2 * pairs, rows, width), LOW),
            full,
            low,
            jax.ShapeDtypeStruct((tokens, local // HEAD), FULL),
            low,
            low,
            low,
            jax.ShapeDtypeStruct((rows, width), LOW),
            full,
        ]
        + whole_shapes(weights),
        scratch_shapes=[pltpu.VMEM(x.shape, LOW), pltpu.VMEM((2 * pairs, rows, width), LOW), DMA]
        + exchange_sems(plane, 1)
        + scatter_buffers(pairs, rows, width, False)
        + scatter_sems(pairs, SUM_CUTS)
        + gather_sems(pairs, CUTS)
        + plane_gather_sems() * len(weights),
    )(x, w_in, w_out, cosine, sine, start, gathered, mix_home, *weights)
    return [outs[0].reshape(tokens, width)] + list(outs[1:9]), outs[9:]


def back_kernel(
    pairs, plane, gathered, part, x_in, units_in, hid_in, gy_in,
    rows_out, low_out, out_grad, in_sum, square,
    total, left, right, grad, arrived, onward, final, load_sem,
    send, recv, loaded, send_on, recv_on, *rest,
):
    d, c = lax.axis_index("dp"), lax.axis_index("col")
    scatter = Scatter(pairs, SUM_CUTS, part, rest[:4], rest[4:11])
    gather = Gather(pairs, CUTS, gathered, rows_out, rest[11:])
    height = in_sum.shape[1]
    one = PlaneScatter(
        by_rows(grad, height),
        in_sum,
        square,
        (arrived, None, onward, final),
        (send, recv, loaded, send_on, recv_on),
    )
    narrow = hid_in.shape[1]
    loads = [
        pltpu.make_async_copy(x_in, left, load_sem.at[0]),
        pltpu.make_async_copy(units_in, right, load_sem.at[1]),
        pltpu.make_async_copy(hid_in, left.at[:, pl.ds(0, narrow)], load_sem.at[2]),
        pltpu.make_async_copy(gy_in, right, load_sem.at[3]),
    ]
    loads[0].start()
    loads[1].start()
    greet(pairs, plane)
    gather.start()
    scatter.start()

    def in_block(there, across):
        @pl.loop(0, height // UNIT)
        def _(index):
            at = pl.multiple_of((there * 2 + across) * height + index * UNIT, UNIT)
            grad[pl.ds(at, UNIT)] = dot_first(left[:, pl.ds(at, UNIT)], right[...]).astype(LOW)

    owned, width = out_grad.shape[2:]

    def out_block(part):
        @pl.loop(0, owned // UNIT)
        def _(index):
            at = pl.multiple_of(part * owned + index * UNIT, UNIT)
            tile = dot_first(left[:, pl.ds(at, UNIT)], right[...]).astype(LOW)
            for side in range(2):
                out_grad[side, part, pl.ds(pl.multiple_of(index * UNIT, UNIT), UNIT)] = tile[
                    :, side * width : (side + 1) * width
                ]

    each = -(-scatter.polls() // (CUTS * (pairs - 1)))

    def both(step):
        for cut in range(CUTS):
            gather.step(step + 1, cut)
            for index in range(each):
                scatter.poll((step * CUTS + cut) * each + index)

    scatter.begin()
    loads[0].wait()
    loads[1].wait()
    in_block(1 - c, 1 - d)
    one.move(0, 0).start()
    one.move(1, 0).start()
    in_block(c, 1 - d)
    one.move(0, 1).start()
    in_block(1 - c, d)
    one.move(1, 1).start()
    both(0)
    in_block(c, d)
    loads[2].start()
    loads[3].start()
    both(1)
    loads[2].wait()
    loads[3].wait()
    out_block(0)
    one.forward()
    out_block(1)
    for step in range(2, pairs - 1):
        both(step)
    scatter.finish(total)
    low_out[...] = total[...].astype(LOW)
    gather.finish()
    one.finish()


def back_gather(pairs, plane, gathered, partial, x, units, hid, gy, collective):
    rows, width = gathered.shape
    wide, narrow = units.shape[1], hid.shape[1]
    height = width // 4
    half = (height // 2, wide)
    whole = jax.ShapeDtypeStruct((2 * pairs, rows, width), LOW)
    outs = call_remote(
        functools.partial(back_kernel, pairs, plane),
        collective,
        in_specs=[ANY] * 6,
        out_specs=[ANY, VMEM, VMEM, VMEM, VMEM],
        out_shape=[
            whole,
            jax.ShapeDtypeStruct((rows, width), LOW),
            jax.ShapeDtypeStruct((2, 2, narrow // 2, width // 2), LOW),
            jax.ShapeDtypeStruct((2, height, wide // 2), FULL),
            jax.ShapeDtypeStruct((2, 8, 128), FULL),
        ],
        scratch_shapes=[
            pltpu.VMEM((rows, width), FULL),
            pltpu.VMEM(x.shape, LOW),
            pltpu.VMEM(units.shape, LOW),
            pltpu.VMEM((width, wide), LOW),
            pltpu.VMEM((2, 2) + half, LOW),
            pltpu.VMEM((2,) + half, LOW),
            pltpu.VMEM((2,) + half, LOW),
            DMA((4,)),
            DMA((2, 2)),
            DMA((2, 2)),
            DMA((2, 2)),
            DMA((2,)),
            DMA((2,)),
        ]
        + scatter_buffers(pairs, rows, width)
        + scatter_sems(pairs, SUM_CUTS)
        + gather_sems(pairs, CUTS),
    )(gathered, partial.reshape(whole.shape), x, units, hid, gy)
    return [outs[0].reshape(2 * pairs * rows, width)] + list(outs[1:])


def row_gather_kernel(pairs, gathered, rows_out, *line_sems):
    gather = Gather(pairs, CUTS, gathered, rows_out, line_sems)
    greet(pairs)
    gather.start()
    for step in range(1, pairs):
        for cut in range(CUTS):
            gather.step(step, cut)
    gather.finish()


def row_gather(pairs, gathered, collective):
    rows, width = gathered.shape
    out = call_remote(
        functools.partial(row_gather_kernel, pairs),
        collective,
        in_specs=[ANY],
        out_specs=ANY,
        out_shape=jax.ShapeDtypeStruct((2 * pairs, rows, width), LOW),
        scratch_shapes=gather_sems(pairs, CUTS),
    )(gathered)
    return out.reshape(2 * pairs * rows, width)


def arrival(place, pairs, step):
    chosen = jnp.int32(0)
    for here in range(pairs):
        order = sorted(range(pairs), key=lambda there: abs(there - here))
        chosen = jnp.where(place == here, order[step], chosen)
    return chosen


UNIT = 256


def ffn_kernel(
    plane, pairs, hyper, mix, branch, back_home, w_in, w_out, gy_rows,
    rows_out, hid_out, units_out, y_out, h, gh_out, gy_out,
    own, x, wd, gy, hid, units, y, part, twin, from_left, from_right, total, upstream,
    load_sem, gy_sem, hid_sem, units_sem, y_sem, x_sem,
    twin_send, twin_recv, right_send, right_recv, left_send, left_recv, *rest,
):
    plane_sems, line_sems = rest[:3], rest[3:]
    me, place, side = line_place()
    last = pairs - 1
    rows = own.shape[0]
    height = rows // SUM_CUTS
    half = units.shape[2] // 2
    n_col, n_dp, owned, width = w_out.shape
    tiles = [
        pltpu.make_async_copy(
            w_out.at[c, d],
            wd.at[pl.ds(d * owned, owned), pl.ds(c * width, width)],
            load_sem.at[2 + c * n_dp + d],
        )
        for c in range(n_col)
        for d in range(n_dp)
    ]
    for tile in tiles:
        tile.start()
    greet(pairs, plane)
    loads = [
        pltpu.make_async_copy(mix, h, load_sem.at[0]),
        pltpu.make_async_copy(branch, total, load_sem.at[1]),
    ]
    for load in loads:
        load.start()
    exchange = to_work(plane, back_home, upstream, plane_sems, 0)
    order = [arrival(place, pairs, step) for step in range(pairs)]

    def load_gy(step):
        return pltpu.make_async_copy(gy_rows.at[order[step]], gy.at[step % 2], gy_sem.at[step % 2])

    load_gy(0).start()
    loads[0].wait()
    loads[1].wait()
    h[...] = h[...] + branch_weight(hyper) * total[...]
    own[...] = norm_forward(h[...])[0].astype(LOW)
    gather = Gather(pairs, CUTS, own, x, line_sems)
    gather.start()
    for tile in tiles:
        tile.wait()

    def saves(step):
        slot = step % 2
        return [
            pltpu.make_async_copy(hid.at[slot], hid_out.at[order[step]], hid_sem.at[slot]),
            pltpu.make_async_copy(units.at[slot], units_out.at[order[step]], units_sem.at[slot]),
            pltpu.make_async_copy(y.at[slot], y_out.at[order[step]], y_sem.at[slot]),
        ]

    def save_x(step):
        return pltpu.make_async_copy(
            x.at[pl.ds(order[step] * 2, 2)], rows_out.at[pl.ds(order[step] * 2, 2)], x_sem.at[step]
        )

    def work(step):
        slot = step % 2
        x_block = x.at[pl.ds(order[step] * 2, 2)]

        @pl.loop(0, half // UNIT)
        def _(unit):
            at = pl.multiple_of(unit * UNIT, UNIT)
            rows_in = x_block[...].reshape(2 * rows, -1)
            gate = jnp.dot(rows_in, w_in[:, pl.ds(at, UNIT)], preferred_element_type=FULL)
            up = jnp.dot(rows_in, w_in[:, pl.ds(half + at, UNIT)], preferred_element_type=FULL)
            grad = dot_last(gy[slot], wd[pl.ds(at, UNIT)])
            sigma = 1.0 / (1.0 + jnp.exp(-gate))
            silu = gate * sigma
            hid[slot, :, pl.ds(at, UNIT)] = (silu * up).astype(LOW)
            units[slot, :, pl.ds(at, UNIT)] = (
                grad * up * sigma * (1.0 + gate * (1.0 - sigma))
            ).astype(LOW)
            units[slot, :, pl.ds(half + at, UNIT)] = (grad * silu).astype(LOW)

        @pl.loop(0, D // UNIT)
        def _(unit):
            at = pl.multiple_of(unit * UNIT, UNIT)
            tile = dot_last(units[slot], w_in[pl.ds(at, UNIT)]).astype(LOW)
            part[pl.ds(order[step] * 2, 2), :, pl.ds(at, UNIT)] = tile.reshape(2, rows, UNIT)

    def work_out(step):
        slot = step % 2

        @pl.loop(0, D // UNIT)
        def _(unit):
            at = pl.multiple_of(unit * UNIT, UNIT)
            tile = jnp.dot(hid[slot], wd[:, pl.ds(at, UNIT)], preferred_element_type=FULL)
            y[slot, :, pl.ds(at, UNIT)] = tile.astype(LOW)

    def to_twin(dest):
        return remote(
            part.at[dest * 2 + 1 - side],
            twin.at[dest],
            twin_send.at[dest],
            twin_recv.at[dest],
            {"row": me + 1 - 2 * side},
        )

    def line(dest, cut, rightward):
        span = pl.ds(cut * height, height)
        return remote(
            part.at[dest * 2 + side, span],
            (from_left if rightward else from_right).at[dest, span],
            (right_send if rightward else left_send).at[dest, cut],
            (right_recv if rightward else left_recv).at[dest, cut],
            {"row": me + 2 if rightward else me - 2},
        )

    def here(dest, span):
        return part[dest * 2 + side, span].astype(FULL) + twin[dest, span].astype(FULL)

    def send_first(step):
        dest = order[step]
        to_twin(dest).wait_recv()
        for at_end, rightward in ((place == 0, True), (place == last, False)):
            @pl.when(at_end & (dest != place))
            def _():
                for cut in range(SUM_CUTS):
                    span = pl.ds(cut * height, height)
                    part[dest * 2 + side, span] = here(dest, span).astype(LOW)
                    line(dest, cut, rightward).start()

    for step in range(pairs):
        if step > 0:
            for cut in range(CUTS):
                gather.step(step, cut)
        else:
            gather.stay().wait()
        if step + 1 < pairs:
            load_gy(step + 1).start()
        gather.twin_arrive(order[step])
        save_x(step).start()
        load_gy(step).wait()
        if step >= 2:
            for save in saves(step - 2):
                save.wait()
        work(step)
        if step == 1:
            exchange.start()
        to_twin(order[step]).start()
        if step > 0:
            send_first(step - 1)
        if step == pairs - 1:
            send_first(step)
        work_out(step)
        for save in saves(step):
            save.start()

    def pass_on(dest, cut, rightward):
        arrived = from_left if rightward else from_right
        span = pl.ds(cut * height, height)
        line(dest, cut, rightward).wait_recv()
        part[dest * 2 + side, span] = (here(dest, span) + arrived[dest, span].astype(FULL)).astype(LOW)
        line(dest, cut, rightward).start()

    for inner in range(1, pairs // 2):
        order_here = [(reach, cut, 0, True, reach) for reach in range(inner + 1, pairs) for cut in range(SUM_CUTS)]
        order_here += [
            (last - dest, cut + last - 2 * inner, 1, False, dest) for dest in range(inner) for cut in range(SUM_CUTS)
        ]
        for reach, at, late, near, dest in sorted(order_here):
            cut = at - (last - 2 * inner) * late

            @pl.when(place == inner)
            def _():
                pass_on(dest, cut, near)

            @pl.when(place == last - inner)
            def _():
                pass_on(last - dest, cut, not near)

    for cut in range(SUM_CUTS):
        span = pl.ds(cut * height, height)
        total[span] = here(place, span)

        @pl.when(place > 0)
        def _():
            line(place, cut, True).wait_recv()
            total[span] += from_left[place, span].astype(FULL)

        @pl.when(place < last)
        def _():
            line(place, cut, False).wait_recv()
            total[span] += from_right[place, span].astype(FULL)

    exchange.arrive()
    grad = norm_backward(total[...], h[...])
    gh_out[...] = grad.astype(LOW)
    gy_out[...] = (upstream[...] + branch_weight(hyper) * grad).astype(LOW)

    exchange.leave()
    gather.leave()
    for step in range(pairs):
        save_x(step).wait()
    for step in range(pairs - 2, pairs):
        for save in saves(step):
            save.wait()
    for dest in range(pairs):
        to_twin(dest).wait_send()
        for cut in range(SUM_CUTS):
            @pl.when(place < dest)
            def _():
                line(dest, cut, True).wait_send()

            @pl.when(place > dest)
            def _():
                line(dest, cut, False).wait_send()


def feed_forward(plane, pairs, hyper, mix, branch, back_home, w_in, w_out, gy_rows, collective):
    rows, width = mix.shape
    units = w_in.shape[1]
    half = units // 2
    low = jax.ShapeDtypeStruct((rows, width), LOW)

    def by_pair(last_width):
        return jax.ShapeDtypeStruct((pairs, 2 * rows, last_width), LOW)

    blocks = pltpu.VMEM((pairs, rows, width), LOW)
    full = pltpu.VMEM((rows, width), FULL)
    outs = call_remote(
        functools.partial(ffn_kernel, plane, pairs),
        collective,
        in_specs=[SMEM, ANY, ANY, ANY, VMEM, ANY, ANY],
        out_specs=[ANY, ANY, ANY, ANY, VMEM, VMEM, VMEM],
        out_shape=[
            jax.ShapeDtypeStruct((2 * pairs, rows, width), LOW),
            by_pair(half),
            by_pair(units),
            by_pair(width),
            jax.ShapeDtypeStruct((rows, width), FULL),
            low,
            low,
        ],
        scratch_shapes=[
            pltpu.VMEM((rows, width), LOW),
            pltpu.VMEM((2 * pairs, rows, width), LOW),
            pltpu.VMEM((half, width), LOW),
            pltpu.VMEM((2, 2 * rows, width), LOW),
            pltpu.VMEM((2, 2 * rows, half), LOW),
            pltpu.VMEM((2, 2 * rows, units), LOW),
            pltpu.VMEM((2, 2 * rows, width), LOW),
            pltpu.VMEM((2 * pairs, rows, width), LOW),
            blocks,
            blocks,
            blocks,
            full,
            full,
            DMA((2 + plane[0] * plane[1],)),
            DMA((2,)),
            DMA((2,)),
            DMA((2,)),
            DMA((2,)),
            DMA((pairs,)),
            DMA((pairs,)),
            DMA((pairs,)),
        ]
        + [DMA((pairs, SUM_CUTS))] * 4
        + exchange_sems(plane, 1)
        + gather_sems(pairs, CUTS),
    )(hyper, mix, branch, back_home, w_in, w_out, gy_rows.reshape(pairs, 2 * rows, width))
    tokens = 2 * pairs * rows
    return [value.reshape(tokens, -1) for value in outs[:4]] + list(outs[5:])


def leave_kernel(
    plane, pairs, in_kernel, gy_in, x_in, heads_in, log_in, q, k, v, cosine, sine, start, w_in, w_out, h,
    y_att, y_ffn, gh_ffn, *rest,
):
    if in_kernel:
        ffn_grad, rest = rest[0], rest[1:]
    homes, rest = rest[:4], rest[4:]
    if in_kernel:
        sums, rest = rest[:6], rest[6:]
    (grad_in, grad_out, rows_in, units, back, k_sum, v_sum, part, total, last, load_sem), rest = (
        rest[:11],
        rest[11:],
    )
    plane_sems, scratch, rest = rest[:3], rest[3:13], rest[13:]
    scatter = Scatter(pairs, SUM_CUTS, part, scratch[:3], scratch[3:])
    load_gy = pltpu.make_async_copy(gy_in, rows_in, load_sem.at[0])
    load_x = pltpu.make_async_copy(x_in, rows_in, load_sem.at[1])
    load_gy.start()
    planes = []
    if in_kernel:
        own_ffn, rest = rest[0], rest[1:]
        for index, block_of in enumerate(
            (
                by_owner(ffn_grad, sums[0].shape[1]),
                by_tiles(grad_out, *sums[2].shape[1:]),
                by_rows(grad_in, sums[4].shape[1]),
            )
        ):
            one = rest[8 * index : 8 * index + 8]
            planes.append(
                PlaneScatter(
                    block_of,
                    sums[2 * index],
                    sums[2 * index + 1],
                    (one[0], None if index else own_ffn, one[1], one[2]),
                    one[3:],
                )
            )
    greet(pairs, plane)
    ways = [
        to_home(plane, work, home, plane_sems, index)
        for index, (work, home) in enumerate(zip((y_att, y_ffn, gh_ffn, last), homes))
    ]
    for one in planes[:1]:
        one.start()
    for way in ways[:3]:
        way.start()
    load_gy.wait()
    back[...] = dot_last(rows_in[...], w_out[...]).astype(LOW)
    width = q.shape[1]
    for head in range(width // HEAD):
        attend_head_back(
            head, back, q, k, v, log_in, cosine, sine, start, units, k_sum, v_sum
        )
    rows = total.shape[0]
    for dest in scatter.order():
        for owner in (2 * dest, 2 * dest + 1):
            part[owner] = dot_last(units[pl.ds(owner * rows, rows)], w_in[...]).astype(LOW)
        scatter.offer(dest)
    scatter.begin()
    grad_out[...] = dot_first(heads_in[...], rows_in[...]).astype(LOW)
    load_x.start()
    for one in planes[1:2]:
        one.start()
    load_x.wait()
    quarter = D // SUM_CUTS
    polls = list(range(scatter.polls()))
    for cut in range(SUM_CUTS):
        for index in polls[:2]:
            scatter.poll(index)
        polls = polls[2:]

        @pl.loop(0, quarter // UNIT)
        def _(index):
            at = pl.multiple_of(cut * quarter + index * UNIT, UNIT)
            grad_in[pl.ds(at, UNIT)] = dot_first(rows_in[:, pl.ds(at, UNIT)], units[...]).astype(LOW)

    for one in planes[2:]:
        one.start()
    for one in planes[:1]:
        one.forward()
    for index in polls:
        scatter.poll(index)
    for one in planes[1:]:
        one.forward()
    scatter.finish(total)
    last[...] = norm_backward(total[...], h[...]).astype(last.dtype)
    ways[3].start()
    for one in planes:
        one.finish()
    for way in ways:
        way.arrive()
        way.leave()


def leave(
    plane, pairs, ffn_grad, gy, x, heads, log_totals, q, k, v, tables, w_in, w_out, h, works, collective
):
    in_kernel = len(ffn_grad) > 0
    rows, width = h.shape
    n_dp, n_col = plane
    tokens, local = q.shape
    home = jax.ShapeDtypeStruct((n_dp, n_col, rows // n_dp, width // n_col), works[0].dtype)
    grads = [(width, 3 * local), (local, width)]
    extra, planes = [], []
    if in_kernel:
        owned = [(1,) + ffn_grad[0].shape[2:], (1, local // 2, width // 2), (3, width // 4, local)]
        planes.append(pltpu.VMEM((2, 2, owned[0][1] // 2, owned[0][2]), LOW))
        for shape in owned:
            extra += [shape, (2, 8, 128)]
            half = (shape[1] // 2, shape[0] * shape[2])
            planes += [
                pltpu.VMEM((2, 2) + half, LOW),
                pltpu.VMEM((2,) + half, LOW),
                pltpu.VMEM((2,) + half, LOW),
                DMA((2, 2)),
                DMA((2, 2)),
                DMA((2, 2)),
                DMA((2,)),
                DMA((2,)),
            ]
    grad_refs = [pltpu.VMEM(shape, LOW) for shape in grads]
    grad_outs = [] if in_kernel else [jax.ShapeDtypeStruct(shape, LOW) for shape in grads]
    outs = call_remote(
        functools.partial(leave_kernel, plane, pairs, in_kernel),
        collective,
        in_specs=[ANY, ANY] + [VMEM] * 11 + [ANY] * (3 + len(ffn_grad)),
        out_specs=[ANY] * 4 + [VMEM] * (len(extra) + len(grad_outs)),
        out_shape=[home] * 4 + [jax.ShapeDtypeStruct(shape, FULL) for shape in extra] + grad_outs,
        scratch_shapes=(grad_refs if in_kernel else [])
        + [
            pltpu.VMEM(x.shape, LOW),
            pltpu.VMEM((tokens, 3 * local), LOW),
            pltpu.VMEM((tokens, local), LOW),
            pltpu.VMEM((tokens, HEAD), FULL),
            pltpu.VMEM((tokens, HEAD), FULL),
            pltpu.VMEM((2 * pairs, rows, width), LOW),
            pltpu.VMEM((rows, width), FULL),
            pltpu.VMEM((rows, width), works[0].dtype),
            DMA((2,)),
        ]
        + exchange_sems(plane, 4)
        + scatter_buffers(pairs, rows, width, False)
        + scatter_sems(pairs, SUM_CUTS)
        + planes,
    )(gy, x, heads, log_totals, q, k, v, *tables, w_in, w_out, h, *works, *ffn_grad)
    return outs[:4], outs[4:]


def total_kernel(plane, count, groups, *refs):
    parts, refs = refs[: len(groups)], refs[len(groups) :]
    out, line, flat, line_send, line_recv, flat_send, flat_recv = refs
    n_dp, n_col = plane
    me = lax.axis_index("row")
    here = lax.axis_index("dp") * n_col + lax.axis_index("col")
    barrier = pltpu.get_barrier_semaphore()
    rows = [(me + step) % count for step in range(1, count)]
    for row in rows:
        pl.semaphore_signal(barrier, inc=1, device_id={"row": row}, device_id_type=pl.DeviceIdType.MESH)
    for offset in offsets(plane):
        pl.semaphore_signal(
            barrier, inc=1, device_id=peer(plane, offset), device_id_type=pl.DeviceIdType.MESH
        )
    pl.semaphore_wait(barrier, count - 1 + n_dp * n_col - 1)
    lane = lax.broadcasted_iota(jnp.int32, out.shape, 1)
    own = jnp.zeros(out.shape, FULL)
    first = 0
    for part, group in zip(parts, groups):
        for index in range(part.shape[0]):
            value = jnp.sum(jnp.sum(part[index], axis=0, keepdims=True), axis=1, keepdims=True)
            own = own + jnp.where(lane == first + index * group, value, 0.0)
        first = first + part.shape[0] * group
    line[me] = own
    copies = [
        remote(line.at[me], line.at[me], line_send.at[step], line_recv.at[step], {"row": row})
        for step, row in enumerate(rows)
    ]
    for copy in copies:
        copy.start()
    for copy in copies:
        copy.wait()
    sums = line[0]
    for row in range(1, count):
        sums = sums + line[row]
    flat[here] = sums
    copies = [
        remote(
            flat.at[here],
            flat.at[here],
            flat_send.at[offset[0], offset[1]],
            flat_recv.at[offset[0], offset[1]],
            peer(plane, offset),
        )
        for offset in offsets(plane)
    ]
    for copy in copies:
        copy.start()
    for copy in copies:
        copy.wait()
    sums = flat[0]
    for index in range(1, n_dp * n_col):
        sums = sums + flat[index]
    out[...] = sums


def sum_everywhere(plane, parts, squares, collective):
    count = lax.axis_size("row")
    shape = (1, 128)
    groups = [1] * len(parts) + [0] * len(squares)
    return call_remote(
        functools.partial(total_kernel, plane, count, groups),
        collective,
        in_specs=[VMEM] * len(groups),
        out_specs=VMEM,
        out_shape=jax.ShapeDtypeStruct(shape, FULL),
        scratch_shapes=[
            pltpu.VMEM((count,) + shape, FULL),
            pltpu.VMEM((plane[0] * plane[1],) + shape, FULL),
            DMA((count - 1,)),
            DMA((count - 1,)),
            DMA(plane),
            DMA(plane),
        ],
    )(*parts, *squares)


def mat(left, right):
    return jnp.sum(left[:, :, None] * right[None, :, :], axis=1)


def gather_blocks(weight_low):
    return lax.all_gather(weight_low, ("col", "dp"), axis=0, tiled=True)


def scatter_blocks(grad_low):
    return lax.psum_scatter(grad_low, ("col", "dp"), scatter_dimension=0, tiled=True).astype(FULL)


def side_by_side(weight):
    return jnp.concatenate([weight[index] for index in range(weight.shape[0])], axis=1)


def apart(weight, count):
    width = weight.shape[1] // count
    return jnp.stack([weight[:, index * width : (index + 1) * width] for index in range(count)])


def whole_out(weight_low, n_dp, n_col):
    rows, width = weight_low.shape
    blocks = gather_blocks(weight_low).reshape(n_col, n_dp, rows, width)
    return blocks.transpose(1, 2, 0, 3).reshape(n_dp * rows, n_col * width)


def own_out(grad, n_dp, n_col):
    rows, width = grad.shape[0] // n_dp, grad.shape[1] // n_col
    blocks = grad.astype(LOW).reshape(n_dp, rows, n_col, width).transpose(2, 0, 1, 3)
    return scatter_blocks(blocks.reshape(n_col * n_dp * rows, width))


def adam_update(weight, grad_sum, moment_one, moment_two, clip_factor, step_value):
    clipped = grad_sum * clip_factor
    new_one = beta_first * moment_one + (1.0 - beta_first) * clipped
    new_two = beta_second * moment_two + (1.0 - beta_second) * clipped * clipped
    fix_one = 1.0 - jnp.power(beta_first, step_value)
    fix_two = 1.0 - jnp.power(beta_second, step_value)
    new_weight = weight - learning_rate * (
        new_one / fix_one / (jnp.sqrt(new_two / fix_two) + adam_eps) + weight_decay * weight
    )
    return (new_weight, new_one, new_two)


def body(
    streams,
    cotangent,
    destination,
    segments,
    attention_in,
    feedforward_in,
    attention_out,
    feedforward_out,
    attention_in_moment,
    feedforward_in_moment,
    attention_out_moment,
    feedforward_out_moment,
    attention_in_second,
    feedforward_in_second,
    attention_out_second,
    feedforward_out_second,
    hyper_weights,
    hyper_moment,
    hyper_second,
    step_count,
):
    n_dp, n_col, count = lax.axis_size("dp"), lax.axis_size("col"), lax.axis_size("row")
    plane, pairs = (n_dp, n_col), count // 2
    rows = destination.shape[1]
    group_tokens = segments.shape[2]
    slot = rows // n_dp
    travel = LOW if slot % 16 == 0 else FULL
    in_kernel = plane == (2, 2)
    attention_low = [side_by_side(attention_in).astype(LOW), attention_out.astype(LOW)]
    feedforward_out_own = feedforward_out.astype(LOW)

    group = destination // group_tokens
    sent = (
        group * slot
        + (destination - group * group_tokens)
        - lax.axis_index("row") * rows
        - lax.axis_index("dp") * slot
    )
    hyper = hyper_weights.reshape(-1)
    h_home, mix_home, back_home, gy_home, gram = prepare(
        hyper, streams, cotangent, sent, n_dp, travel
    )
    segment = lax.dynamic_index_in_dim(segments[:, 0], lax.axis_index("col"), 0, keepdims=False)
    start, inverse = rotary_parts(segment)

    feedforward_out_low = gather_blocks(feedforward_out_own).reshape(n_col, n_dp, *feedforward_out.shape)
    early = attention_low if in_kernel else []
    (rows_att, hidden_att, gy_work, cosine, sine, feedforward_in_own), wholes = enter(
        plane, pairs, h_home, gy_home, start, inverse, feedforward_in, early, 1
    )
    if not in_kernel:
        wholes = [gather_blocks(attention_low[0]), whole_out(attention_low[1], n_dp, n_col)]
    attention_in_low, attention_out_low = wholes
    (
        grad_rows_ffn,
        mix_work,
        heads_low,
        log_totals,
        query_low,
        key_low,
        value_low,
        branch_low,
        branch_att,
    ), wholes = attend(
        plane,
        pairs,
        rows_att,
        attention_in_low,
        attention_out_low,
        cosine,
        sine,
        start,
        gy_work.astype(LOW),
        mix_home,
        [feedforward_in_own] if in_kernel else [],
        2,
    )
    feedforward_in_low = wholes[0] if in_kernel else gather_blocks(feedforward_in_own)
    rows_ffn, hidden_low, grad_units, partial_ffn, grad_hidden_ffn, grad_branch = feed_forward(
        plane,
        pairs,
        hyper,
        mix_work,
        branch_att,
        back_home,
        feedforward_in_low,
        feedforward_out_low,
        grad_rows_ffn,
        3,
    )
    if in_kernel:
        grad_rows_att, branch_ffn, grad_out, sum_in, square = back_gather(
            pairs, plane, grad_branch, partial_ffn, rows_ffn, grad_units, hidden_low, grad_rows_ffn, 5
        )
        ffn_grad, squares = [grad_out], [square]
    else:
        grad_rows_att = row_gather(pairs, grad_branch, 5)
        branch_ffn = lax.psum_scatter(partial_ffn, "row", scatter_dimension=0, tiled=True)
        sums_ffn = [
            apart(
                scatter_blocks(
                    jnp.einsum("td,tu->du", rows_ffn, grad_units, preferred_element_type=FULL).astype(LOW)
                ),
                2,
            ),
            own_out(
                jnp.einsum("tu,td->ud", hidden_low, grad_rows_ffn, preferred_element_type=FULL), n_dp, n_col
            ),
        ]
        ffn_grad, squares = [], [value * value for value in sums_ffn]

    homes, sums_att = leave(
        plane,
        pairs,
        ffn_grad,
        grad_rows_att,
        rows_att,
        heads_low,
        log_totals,
        query_low,
        key_low,
        value_low,
        (cosine, sine, start),
        attention_in_low,
        attention_out_low,
        hidden_att,
        [value.astype(travel) for value in (branch_low, branch_ffn, grad_hidden_ffn)],
        6,
    )
    if in_kernel:
        squares += sums_att[1::2]
        shard_feedforward_out, shard_attention_out, shard_attention_in = sums_att[::2]
        shard_feedforward_out, shard_attention_out = shard_feedforward_out[0], shard_attention_out[0]
        shard_feedforward_in = sum_in
    else:
        shard_attention_in = apart(scatter_blocks(sums_att[0]), 3)
        shard_attention_out = own_out(sums_att[1], n_dp, n_col)
        squares += [value * value for value in (shard_attention_in, shard_attention_out)]
        shard_feedforward_in, shard_feedforward_out = sums_ffn
    if not in_kernel:
        square = sum(jnp.sum(value) for value in squares)
        squares = [jnp.zeros((1, 8, 128), FULL).at[0, 0, 0].set(square)]
    streams_out, stream_grad, dots = finish(hyper, streams, cotangent, sent, homes)
    totals = sum_everywhere(plane, [gram, dots], squares, 7)[0]
    a0, m0, c0 = hyper_weights[0, :, 0], hyper_weights[0, :, 1:5], hyper_weights[0, :, 5]
    a1, m1, c1 = hyper_weights[1, :, 0], hyper_weights[1, :, 1:5], hyper_weights[1, :, 5]
    gram = totals[:16].reshape(STREAMS, STREAMS)
    att_cot, ffn_cot = totals[16:20], totals[20:24]
    streams_ffn, streams_att = totals[24:28], totals[28:32]
    att_ffn, square_total = totals[32], totals[33]
    grad_m1 = mat(m0.T, gram) + c0[:, None] * att_cot[None, :]
    grad_a1 = jnp.sum(m0 * streams_ffn[:, None], axis=0) + c0 * att_ffn
    grad_m0 = mat(gram, m1.T) + streams_ffn[:, None] * a1[None, :]
    grad_c0 = jnp.sum(m1 * att_cot[None, :], axis=1) + a1 * att_ffn
    hyper_grad = jnp.stack(
        [
            jnp.concatenate([streams_att[:, None], grad_m0, grad_c0[:, None]], axis=1),
            jnp.concatenate([grad_a1[:, None], grad_m1, ffn_cot[:, None]], axis=1),
        ]
    )
    grad_norm = jnp.sqrt(square_total + jnp.sum(hyper_grad * hyper_grad))
    clip_factor = 1.0 / jnp.maximum(grad_norm, 1.0)
    step_value = step_count[0].astype(jnp.float32)
    attention_in_new = adam_update(
        attention_in,
        shard_attention_in,
        attention_in_moment,
        attention_in_second,
        clip_factor,
        step_value,
    )
    feedforward_in_new = adam_update(
        feedforward_in,
        shard_feedforward_in,
        feedforward_in_moment,
        feedforward_in_second,
        clip_factor,
        step_value,
    )
    attention_out_new = adam_update(
        attention_out,
        shard_attention_out,
        attention_out_moment,
        attention_out_second,
        clip_factor,
        step_value,
    )
    feedforward_out_new = adam_update(
        feedforward_out,
        shard_feedforward_out,
        feedforward_out_moment,
        feedforward_out_second,
        clip_factor,
        step_value,
    )
    hyper_new = adam_update(
        hyper_weights, hyper_grad, hyper_moment, hyper_second, clip_factor, step_value
    )
    return (
        streams_out,
        stream_grad,
        grad_norm.reshape(1),
        shard_attention_in,
        shard_feedforward_in,
        shard_attention_out,
        shard_feedforward_out,
        hyper_grad,
        attention_in_new[0],
        feedforward_in_new[0],
        attention_out_new[0],
        feedforward_out_new[0],
        hyper_new[0],
        attention_in_new[1],
        feedforward_in_new[1],
        attention_out_new[1],
        feedforward_out_new[1],
        hyper_new[1],
        attention_in_new[2],
        feedforward_in_new[2],
        attention_out_new[2],
        feedforward_out_new[2],
        hyper_new[2],
    )


def solution(mesh):
    placed = (
        P(None, None, ("dp", "row"), "col"),
        P(None, None, ("dp", "row"), "col"),
        P(None, ("dp", "row")),
        P(None, "dp", None),
        P(None, ("col", "dp"), "row"),
        P(None, ("col", "dp"), "row"),
        P(("row", "dp"), "col"),
        P(("row", "dp"), "col"),
        P(None, ("col", "dp"), "row"),
        P(None, ("col", "dp"), "row"),
        P(("row", "dp"), "col"),
        P(("row", "dp"), "col"),
        P(None, ("col", "dp"), "row"),
        P(None, ("col", "dp"), "row"),
        P(("row", "dp"), "col"),
        P(("row", "dp"), "col"),
        P(),
        P(),
        P(),
        P(),
    )
    return jax.shard_map(
        body,
        mesh=mesh,
        in_specs=placed,
        out_specs=(
            P(None, None, ("dp", "row"), "col"),
            P(None, None, ("dp", "row"), "col"),
            P(),
            P(None, ("col", "dp"), "row"),
            P(None, ("col", "dp"), "row"),
            P(("row", "dp"), "col"),
            P(("row", "dp"), "col"),
            P(),
            P(None, ("col", "dp"), "row"),
            P(None, ("col", "dp"), "row"),
            P(("row", "dp"), "col"),
            P(("row", "dp"), "col"),
            P(),
            P(None, ("col", "dp"), "row"),
            P(None, ("col", "dp"), "row"),
            P(("row", "dp"), "col"),
            P(("row", "dp"), "col"),
            P(),
            P(None, ("col", "dp"), "row"),
            P(None, ("col", "dp"), "row"),
            P(("row", "dp"), "col"),
            P(("row", "dp"), "col"),
            P(),
        ),
        check_vma=False,
    )
```
